256 devices in a mesh: dom: 128 (over z, x, y_lo, core), band: 2 (over y_hi).
Axes of the slice: x: 4, y: 4 (y_hi: 2, y_lo: 2; y = y_hi * 2 + y_lo), z: 8, core: 2. Of those that a mesh axis runs over, the one named last changes fastest.
Arguments:
- orbitals: float32 [16, 1024, 32, 128], P('band', 'dom'), may hold values from -10 to 10
- potential: float32 [1024, 32, 128], P('dom'), may hold values from -1 to 1
- coefficients: float32 [16, 16], replicated, may hold values from -1.5 to 1.5
Outputs:
- intersection: float32 [16, 16], replicated
- rotated: float32 [16, 4096, 1024], P('band', 'dom')
The draws below stay inside these ranges and needn't reach their ends.
All inputs are finite; a program needn't handle non-finite values.
Results may differ from the reference program's by a relative error of at most 0.000071.
Values sent between devices are 32-bit elements; how exact they have to be, the bound alone decides.
No kernel may reach another device: no remote copies, remote signals or barrier semaphores. Data moves between devices by JAX's collectives and lax.ppermute only.
A program may use at most 64 MiB of HBM per device.

```python
import jax
import jax.numpy as jnp
from jax import lax

NORB = 16
NY = 32
NZ = 128
NX = 1024


def draw_orbitals(key, part):
    key = jax.random.fold_in(key, 5)
    own_key, common_key = jax.random.split(key)
    position = jnp.arange(NX, dtype=jnp.float32) / NX
    scale = jnp.sqrt(1.0 + 2.0 * position)[None, :, None, None]
    shape = (NORB, NX, NY, NZ)
    own = jnp.clip(jax.random.normal(own_key, shape, jnp.float32), -4.0, 4.0)
    common = jnp.clip(jax.random.normal(common_key, (1,) + shape[1:], jnp.float32), -4.0, 4.0)
    values = (0.9 * own + 0.45 * common) * scale
    return values.astype(jnp.float32)


def block_levels(stream_key, dims, shards, low, largest):
    def one(dim, blocks):
        draws = jax.random.uniform(jax.random.fold_in(jax.random.fold_in(stream_key, 6), dim), (blocks,), jnp.float32, low / len(shards), largest / len(shards))
        return jnp.repeat(jnp.exp(draws), dims[dim] // blocks).reshape((-1,) + (1,) * (len(dims) - dim - 1))

    level = one(*shards[0])
    for cut in shards[1:]:
        level = level * one(*cut)
    return level


def centred(stream_key, dims, deviation, most, kind=jnp.bfloat16):
    array = jax.random.normal(stream_key, dims, jnp.float32) * deviation
    return jnp.minimum(jnp.maximum(array, -most), most).astype(kind)


def setup_inputs(seed: int = 0) -> dict:
    keys = jax.random.split(jax.random.key(seed), 4)
    return {
        "orbitals": draw_orbitals(jax.random.fold_in(keys[3], 71), 0),
        "potential": jnp.clip(jax.random.uniform(keys[1], (NX, NY, NZ), jnp.float32, -1.0, 1.0) * block_levels(keys[1], (NX, NY, NZ), ((0, 128),), -0.4, 0.0), -1.0, 1.0),
        "coefficients": centred(keys[2], (NORB, NORB), NORB ** -0.5, 1.5, jnp.float32),
    }


STENCIL = (-5369.0 / 1800.0, 12.0 / 7.0, -15.0 / 56.0, 10.0 / 189.0, -1.0 / 112.0, 2.0 / 1925.0, -1.0 / 16632.0)
filter_center = 8.5
filter_half = 6.5


def laplace(field):
    padded = jnp.pad(field, 6)
    size_x, size_y, size_z = field.shape
    total = (3.0 * STENCIL[0]) * field
    for offset in range(1, 7):
        beside = padded[6 + offset:6 + offset + size_x, 6:-6, 6:-6] + padded[6 - offset:6 - offset + size_x, 6:-6, 6:-6]
        beside = beside + padded[6:-6, 6 + offset:6 + offset + size_y, 6:-6] + padded[6:-6, 6 - offset:6 - offset + size_y, 6:-6]
        beside = beside + padded[6:-6, 6:-6, 6 + offset:6 + offset + size_z] + padded[6:-6, 6:-6, 6 - offset:6 - offset + size_z]
        total = total + STENCIL[offset] * beside
    return total


def hamiltonian(field, potential):
    return -0.5 * laplace(field) + potential * field


def filter_field(field, potential):
    first = (hamiltonian(field, potential) - filter_center * field) / filter_half
    second = 2.0 * (hamiltonian(first, potential) - filter_center * first) / filter_half - field
    third = 2.0 * (hamiltonian(second, potential) - filter_center * second) / filter_half - first
    return third


def reference(orbitals, potential, coefficients):
    filtered = lax.map(lambda field: filter_field(field, potential), orbitals)
    count = NX * NY * NZ
    flat = filtered.reshape(NORB, count)
    intersection = jnp.dot(flat, flat.T, precision=lax.Precision.HIGHEST) / count
    turned = jnp.dot(coefficients.T, flat, precision=lax.Precision.HIGHEST)
    rotated = jnp.transpose(turned.reshape(NORB, NX, NY, NZ), (0, 3, 2, 1)).reshape(NORB, NZ * NY, NX)
    return intersection, rotated
```

```python
import functools

import jax
import jax.numpy as jnp
import ml_dtypes
import numpy as np
from jax import lax
from jax.experimental import pallas as pl
from jax.experimental.pallas import tpu as pltpu
from jax.sharding import Mesh
from jax.sharding import PartitionSpec as P

STENCIL = (
    -5369.0 / 1800.0,
    12.0 / 7.0,
    -15.0 / 56.0,
    10.0 / 189.0,
    -1.0 / 112.0,
    2.0 / 1925.0,
    -1.0 / 16632.0,
)
CENTER = 8.5
HALF = 6.5
WIDTH = 6
NORB, NX, NY, NZ = 16, 1024, 32, 128
CHUNK = 32
OWN = 2
YPAD = 8
F32 = jnp.float32
BF16 = jnp.bfloat16


def banded(scale):
    band = np.zeros((NZ, NZ), np.float64)
    for k in range(1, 7):
        band += np.eye(NZ, k=k) * STENCIL[k] + np.eye(NZ, k=-k) * STENCIL[k]
    band = (-0.5 * scale * band).astype(np.float32)
    high = band.astype(ml_dtypes.bfloat16)
    low = (band - high.astype(np.float32)).astype(ml_dtypes.bfloat16)
    zero = np.zeros_like(high)
    return np.block([[high, low], [high, zero]]).astype(ml_dtypes.bfloat16)


def split(x):
    high = x.astype(BF16)
    low = (x - high.astype(F32)).astype(BF16)
    return high, low


def dot3(a, b, dims):
    ah, al = split(a)
    bh, bl = split(b)
    dot = functools.partial(lax.dot_general, dimension_numbers=(dims, ((), ())), preferred_element_type=F32)
    return dot(ah, bh) + (dot(ah, bl) + dot(al, bh))


def stencil(scale, field, before, after, potential, band, pad, zpart, put):
    run = 4
    span = CHUNK + 2 * WIDTH
    zeros = jnp.zeros((YPAD, NZ), F32)

    def clear(p, _):
        pad[p, 0:YPAD, :] = zeros
        pad[p, YPAD + NY :, :] = zeros
        return 0

    lax.fori_loop(0, OWN * span, clear, 0)
    for o in range(OWN):
        pad[o * span : o * span + WIDTH, YPAD : YPAD + NY, :] = before[o]
        pad[o * span + WIDTH + CHUNK : (o + 1) * span, YPAD : YPAD + NY, :] = after[o]
        for s in range(CHUNK // 8):
            block = field(o, s)
            start = o * span + WIDTH + s * 8
            pad[start : start + 8, YPAD : YPAD + NY, :] = block
            high, low = split(block.reshape(8 * NY, NZ))
            both = jnp.dot(jnp.concatenate([high, low], axis=1), band[...], preferred_element_type=F32)
            zpart[o * CHUNK + s * 8 : o * CHUNK + (s + 1) * 8] = (both[:, :NZ] + both[:, NZ:]).reshape(8, NY, NZ)

    def step(i, _):
        o = i // (CHUNK // run)
        x = (i % (CHUNK // run)) * run
        base = o * span + WIDTH + x
        here = pad[pl.ds(base, run), YPAD : YPAD + NY, :]
        total = zpart[pl.ds(o * CHUNK + x, run)]
        total = total + (scale * (-1.5 * STENCIL[0] - CENTER) + scale * potential[pl.ds(x, run)]) * here
        for k in range(1, 7):
            beside = pad[pl.ds(base + k, run), YPAD : YPAD + NY, :] + pad[pl.ds(base - k, run), YPAD : YPAD + NY, :]
            beside = beside + pad[pl.ds(base, run), YPAD + k : YPAD + NY + k, :]
            beside = beside + pad[pl.ds(base, run), YPAD - k : YPAD + NY - k, :]
            total = total + (-0.5 * scale * STENCIL[k]) * beside
        put(o, x, run, total)
        return 0

    lax.fori_loop(0, OWN * CHUNK // run, step, 0)


def ends(out, first, last):
    for o in range(OWN):
        first[o] = out[o, 0:WIDTH]
        last[o] = out[o, CHUNK - WIDTH :]


def first_kernel(slabs, before, after, potential, band, out, first, last, pad, zpart):
    def put(o, x, run, total):
        out[o, pl.ds(x, run)] = total

    stencil(1.0 / HALF, lambda o, s: slabs[s, o], before, after, potential, band, pad, zpart, put)
    ends(out, first, last)


def second_kernel(field, before, after, potential, slabs, band, out, first, last, pad, zpart):
    def put(o, x, run, total):
        out[o, pl.ds(x, run)] = total - slabs[x // 8, o, pl.ds(x % 8, run)]

    stencil(2.0 / HALF, lambda o, s: field[o, s * 8 : s * 8 + 8], before, after, potential, band, pad, zpart, put)
    ends(out, first, last)


def third_kernel(field, before, after, potential, previous, band, out, pad, zpart, result, turned):
    def put(o, x, run, total):
        result[o, pl.ds(x, run)] = total - previous[o, pl.ds(x, run)]

    stencil(2.0 / HALF, lambda o, s: field[o, s * 8 : s * 8 + 8], before, after, potential, band, pad, zpart, put)

    def turn(x, _):
        for b in range(2):
            rows = [result[o, t * 8 + x, b * 16 : b * 16 + 16, :] for t in range(4) for o in range(OWN)]
            turned[pl.ds((b * 8 + x) * NZ, NZ), :] = jnp.concatenate(rows, axis=0).T
        return 0

    lax.fori_loop(0, 8, turn, 0)

    def pick(q, _):
        for c in range(4):
            for b in range(2):
                out[c, b, q] = turned[pl.ds(b * 8 * NZ + 4 * q + c, 8, stride=NZ), :]
        return 0

    lax.fori_loop(0, NZ // 4, pick, 0)


def rotate_kernel(ring, weights, out, gram):
    lane = lax.broadcasted_iota(jnp.int32, (256, 128), 1) // 32
    sums = jnp.zeros((256, 256), F32)
    for t in range(4):
        halves = []
        for b in range(2):
            value = None
            for c in range(4):
                piece = ring[c * 2 + b]
                if c != t:
                    piece = pltpu.roll(piece, ((c - t) % 4) * 32, 1)
                value = piece if value is None else jnp.where(lane == c, piece, value)
            halves.append(value)
        all_orbitals = jnp.concatenate(halves, axis=1)
        turned = dot3(all_orbitals, weights[...], ((1,), (0,)))
        for b in range(2):
            out[:, b, t] = turned[:, b * 128 : (b + 1) * 128].reshape(32, 8, 128)
        sums = sums + dot3(all_orbitals, all_orbitals, ((0,), (0,)))
    row = lax.broadcasted_iota(jnp.int32, (256, 256), 0) % 16
    column = lax.broadcasted_iota(jnp.int32, (256, 256), 1) % 16
    diagonal = jnp.where(row == column, sums, 0.0).reshape(16, 16, 256).sum(axis=1)
    place = lax.broadcasted_iota(jnp.int32, (256, 16), 0) // 16
    ones = (place == lax.broadcasted_iota(jnp.int32, (256, 16), 1)).astype(F32)
    gram[...] = jnp.dot(diagonal, ones, precision=lax.Precision.HIGHEST, preferred_element_type=F32)


def lines_kernel(received, out):
    for b in range(2):
        for s in range(8):
            block = received[s * 4 : s * 4 + 4, b].reshape(128, 128).T.reshape(8, 16, 128)
            out[:, b * 16 : b * 16 + 16, s * 128 : (s + 1) * 128] = block


def call(kernel, outs, scratch=()):
    many = isinstance(outs, list)
    vmem = pl.BlockSpec(memory_space=pltpu.VMEM)
    return lambda *args: pl.pallas_call(
        kernel,
        out_shape=[jax.ShapeDtypeStruct(s, F32) for s in outs] if many else jax.ShapeDtypeStruct(outs, F32),
        in_specs=[vmem] * len(args),
        out_specs=[vmem] * len(outs) if many else vmem,
        scratch_shapes=[pltpu.VMEM(s, F32) for s in scratch],
        compiler_params=pltpu.CompilerParams(vmem_limit_bytes=48 * 1024 * 1024),
    )(*args)


def local(orbitals, potential, coefficients):
    chunks = ("z", "x")
    count = lax.axis_size(chunks)
    up = [(i, i + 1) for i in range(count - 1)]
    down = [(j, i) for i, j in up]

    def beside(first, last):
        return lax.ppermute(last, chunks, up), lax.ppermute(first, chunks, down)

    slabs = lax.all_to_all(orbitals.reshape(4, OWN, 8, NY, NZ), ("u", "c"), 0, 0, tiled=True)
    potential = lax.all_gather(potential, ("u", "c"), axis=0, tiled=True)
    weights = (coefficients[:, None, :, None] * jnp.eye(16, dtype=F32)[None, :, None, :]).reshape(256, 256)

    own = (OWN, CHUNK, NY, NZ)
    end = (OWN, WIDTH, NY, NZ)
    scratch = [(OWN * (CHUNK + 2 * WIDTH), NY + 2 * YPAD, NZ), (OWN * CHUNK, NY, NZ)]
    one = jnp.asarray(banded(1.0 / HALF))
    two = jnp.asarray(banded(2.0 / HALF))
    before, after = beside(slabs[0, :, :WIDTH], slabs[3, :, 8 - WIDTH :])
    first, low, high = call(first_kernel, [own, end, end], scratch)(slabs, before, after, potential, one)
    before, after = beside(low, high)
    second, low, high = call(second_kernel, [own, end, end], scratch)(first, before, after, potential, slabs, two)
    before, after = beside(low, high)
    message = call(third_kernel, (4, 2, 32, 8, 128), scratch + [own, (2 * 8 * NZ, 128)])(
        second, before, after, potential, first, two
    )
    ring = lax.all_to_all(message.reshape(8, 256, 128), ("u", "c", "b"), 0, 0, tiled=True)
    rotated, gram = call(rotate_kernel, [(32, 2, 4, 8, 128), (16, 16)])(ring, weights)
    received = lax.all_to_all(rotated.reshape(64, 32, 128), ("z", "x", "b"), 0, 0, tiled=True)
    parts = lax.all_gather(gram.reshape(2, 128), ("z", "x", "u", "c", "b"))
    intersection = (parts.sum(axis=0) / (NX * NY * NZ)).reshape(NORB, NORB)
    lines = call(lines_kernel, (8, NY, NX))(received.reshape(32, 2, 32, 128))
    return intersection, lines


def solution(mesh):
    grid = Mesh(mesh.devices.reshape(8, 4, 2, 2, 2), ("z", "x", "u", "c", "b"))
    dom = ("z", "x", "u", "c")
    return jax.shard_map(
        local,
        mesh=grid,
        in_specs=(P("b", dom, None, None), P(dom, None, None), P()),
        out_specs=(P(), P("b", dom, None)),
        check_vma=False,
    )
```

```python
import functools

import jax
import jax.numpy as jnp
import ml_dtypes
import numpy as np
from jax import lax
from jax.experimental import pallas as pl
from jax.experimental.pallas import tpu as pltpu
from jax.sharding import Mesh
from jax.sharding import PartitionSpec as P

STENCIL = (
    -5369.0 / 1800.0,
    12.0 / 7.0,
    -15.0 / 56.0,
    10.0 / 189.0,
    -1.0 / 112.0,
    2.0 / 1925.0,
    -1.0 / 16632.0,
)
CENTER = 8.5
HALF = 6.5
WIDTH = 6
NORB, NX, NY, NZ = 16, 1024, 32, 128
CHUNK = 32
OWN = 2
YPAD = 8
F32 = jnp.float32
BF16 = jnp.bfloat16


def banded(scale):
    band = np.zeros((NZ, NZ), np.float64)
    for k in range(1, 7):
        band += np.eye(NZ, k=k) * STENCIL[k] + np.eye(NZ, k=-k) * STENCIL[k]
    band = (-0.5 * scale * band).astype(np.float32)
    high = band.astype(ml_dtypes.bfloat16)
    low = (band - high.astype(np.float32)).astype(ml_dtypes.bfloat16)
    zero = np.zeros_like(high)
    return np.block([[high, low], [high, zero]]).astype(ml_dtypes.bfloat16)


def split(x):
    high = x.astype(BF16)
    low = (x - high.astype(F32)).astype(BF16)
    return high, low


def dot3(a, b, dims):
    ah, al = split(a)
    bh, bl = split(b)
    dot = functools.partial(lax.dot_general, dimension_numbers=(dims, ((), ())), preferred_element_type=F32)
    return dot(ah, bh) + (dot(ah, bl) + dot(al, bh))


def filter_kernel(chunk, slabs, before, after, potential, bands, out, field, other, local, zpart, result, turned):
    far, near = 3 * WIDTH, 2 * WIDTH + 2
    rows = slice(YPAD, YPAD + NY)
    zeros = jnp.zeros((YPAD, NZ), F32)

    def clear(p, _):
        for o in range(OWN):
            for pad in (field, other):
                pad[o, jnp.minimum(p, pad.shape[1] - 1), 0:YPAD, :] = zeros
                pad[o, jnp.minimum(p, pad.shape[1] - 1), YPAD + NY :, :] = zeros
        return 0

    lax.fori_loop(0, field.shape[1], clear, 0)
    for o in range(OWN):
        field[o, 0:far, rows, :] = before[o]
        field[o, far + CHUNK :, rows, :] = after[o]
        for s in range(4):
            field[o, far + 8 * s : far + 8 * s + 8, rows, :] = slabs[s, o]
    order = [(0, 1), (1, 1), (0, 0), (1, 0), (2, 0), (3, 0), (2, 1), (3, 1)]
    for j, (s, h) in enumerate(order):
        local[8 * j : 8 * j + 8] = (potential[s, h] + (-1.5 * STENCIL[0] - CENTER)) * (1.0 / HALF)

    def along_z(source, o, index, band):
        high, low = split(source[o, pl.ds(index, 8), rows, :].reshape(8 * NY, NZ))
        both = jnp.dot(jnp.concatenate([high, low], axis=1), band, preferred_element_type=F32)
        return (both[:, :NZ] + both[:, NZ:]).reshape(8, NY, NZ)

    def step(source, shift, first, blocks, scale, band, put):
        def body(i, _):
            o = i // blocks
            j = i % blocks
            start = first + 8 * j
            base = start + shift
            for y in range(0, NY, 8):
                beside = source[o, pl.ds(base - WIDTH, 8 + 2 * WIDTH), YPAD + y : YPAD + y + 8, :]
                here = beside[WIDTH : WIDTH + 8]
                total = local[pl.ds(start + 16, 8), y : y + 8, :] * here
                if scale != 1.0:
                    total = total * scale
                total = total + zpart[i, :, y : y + 8, :]
                for k in range(1, 7):
                    around = beside[WIDTH + k : WIDTH + 8 + k] + beside[WIDTH - k : WIDTH + 8 - k]
                    around = around + (
                        source[o, pl.ds(base, 8), YPAD + y + k : YPAD + y + 8 + k, :]
                        + source[o, pl.ds(base, 8), YPAD + y - k : YPAD + y + 8 - k, :]
                    )
                    total = total + (-0.5 * scale / HALF * STENCIL[k]) * around
                put(o, start, y, total)
            later = jnp.minimum(i + 1, OWN * blocks - 1)
            zpart[i + 1] = along_z(source, later // blocks, first + 8 * (later % blocks) + shift, band)
            return 0

        zpart[0] = along_z(source, 0, first + shift, band)
        lax.fori_loop(0, OWN * blocks, body, 0)

    def put_first(o, start, y, total):
        other[o, pl.ds(start + near, 8), YPAD + y : YPAD + y + 8, :] = total

    def put_second(o, start, y, total):
        place = (o, pl.ds(start + far, 8), slice(YPAD + y, YPAD + y + 8), slice(None))
        field[place] = total - field[place]

    def put_third(o, start, y, total):
        place = (o, pl.ds(start + near, 8), slice(YPAD + y, YPAD + y + 8), slice(None))
        result[o, pl.ds(start, 8), y : y + 8, :] = total - other[place]

    def outside(target, shift, count):
        blank = jnp.zeros((count, NY, NZ), F32)

        @pl.when(chunk[0] == 0)
        def _():
            for o in range(OWN):
                target[o, shift - count : shift, rows, :] = blank

        @pl.when(chunk[0] == NX // CHUNK - 1)
        def _():
            for o in range(OWN):
                target[o, shift + CHUNK : shift + CHUNK + count, rows, :] = blank

    step(field, far, -12, 7, 1.0, bands[0], put_first)
    outside(other, near, 12)
    step(other, near, -8, 6, 2.0, bands[1], put_second)
    outside(field, far, 8)
    step(field, far, 0, 4, 2.0, bands[1], put_third)

    def turn(x, _):
        for b in range(2):
            pieces = [result[o, t * 8 + x, b * 16 : b * 16 + 16, :] for t in range(4) for o in range(OWN)]
            turned[pl.ds((b * 8 + x) * NZ, NZ), :] = jnp.concatenate(pieces, axis=0).T
        return 0

    lax.fori_loop(0, 8, turn, 0)

    def pick(q, _):
        for c in range(4):
            for b in range(2):
                out[c, b, q] = turned[pl.ds(b * 8 * NZ + 4 * q + c, 8, stride=NZ), :]
        return 0

    lax.fori_loop(0, NZ // 4, pick, 0)


def rotate_kernel(ring, weights, out):
    lane = lax.broadcasted_iota(jnp.int32, (256, 128), 1) // 32
    sums = jnp.zeros((256, 256), F32)
    for t in range(4):
        halves = []
        for b in range(2):
            value = None
            for c in range(4):
                piece = ring[c * 2 + b]
                if c != t:
                    piece = pltpu.roll(piece, ((c - t) % 4) * 32, 1)
                value = piece if value is None else jnp.where(lane == c, piece, value)
            halves.append(value)
        all_orbitals = jnp.concatenate(halves, axis=1)
        turned = dot3(all_orbitals, weights[...], ((1,), (0,)))
        for b in range(2):
            out[:, b, t] = turned[:, b * 128 : (b + 1) * 128].reshape(32, 8, 128)
        sums = sums + dot3(all_orbitals, all_orbitals, ((0,), (0,)))
    row = lax.broadcasted_iota(jnp.int32, (256, 256), 0) % 16
    column = lax.broadcasted_iota(jnp.int32, (256, 256), 1) % 16
    diagonal = jnp.where(row == column, sums, 0.0).reshape(16, 16, 256).sum(axis=1)
    place = lax.broadcasted_iota(jnp.int32, (256, 128), 0) // 16
    ones = (place == lax.broadcasted_iota(jnp.int32, (256, 128), 1)).astype(F32)
    gram = jnp.dot(diagonal, ones, precision=lax.Precision.HIGHEST, preferred_element_type=F32)
    tile = gram[0:8] + pltpu.roll(gram[8:16], 16, 1)
    out[:, :, 4] = jnp.broadcast_to(tile, (32, 2, 8, 128))


def lines_kernel(received, out):
    for b in range(2):
        for s in range(8):
            block = received[s * 4 : s * 4 + 4, b, 0:4].reshape(128, 128).T.reshape(8, 16, 128)
            out[:, b * 16 : b * 16 + 16, s * 128 : (s + 1) * 128] = block


def call(kernel, out, scratch=()):
    vmem = pl.BlockSpec(memory_space=pltpu.VMEM)
    smem = pl.BlockSpec(memory_space=pltpu.SMEM)
    return lambda *args: pl.pallas_call(
        kernel,
        out_shape=jax.ShapeDtypeStruct(out, F32),
        in_specs=[smem if a.dtype == jnp.int32 else vmem for a in args],
        out_specs=vmem,
        scratch_shapes=[pltpu.VMEM(s, F32) for s in scratch],
        compiler_params=pltpu.CompilerParams(vmem_limit_bytes=48 * 1024 * 1024),
    )(*args)


def local(orbitals, potential, coefficients):
    chunks = ("z", "x")
    dom = ("z", "x", "u", "c")
    count = lax.axis_size(chunks)
    up = [(i, i + 1) for i in range(count - 1)]
    down = [(j, i) for i, j in up]

    shift = [(d, d + 2 if d % 4 >= 2 else d - 2) for d in range(4 * count)]
    beyond = lax.ppermute(potential, dom, [(i, j) for i, j in shift if 0 <= j < 4 * count])
    slabs = lax.all_to_all(orbitals.reshape(4, OWN, 8, NY, NZ), ("u", "c"), 0, 0, tiled=True)
    far = 3 * WIDTH
    part = far - 16
    before = lax.ppermute(jnp.concatenate([slabs[1, :, 8 - part :], slabs[2], slabs[3]], axis=1), chunks, up)
    after = lax.ppermute(jnp.concatenate([slabs[0], slabs[1], slabs[2, :, :part]], axis=1), chunks, down)
    window = lax.all_gather(jnp.stack([potential, beyond]), ("u", "c"))

    weights = (coefficients[:, None, :, None] * jnp.eye(16, dtype=F32)[None, :, None, :]).reshape(256, 256)
    bands = jnp.asarray(np.stack([banded(1.0 / HALF), banded(2.0 / HALF)]))
    scratch = [
        (OWN, CHUNK + 2 * far, NY + 2 * YPAD, NZ),
        (OWN, CHUNK + 2 * (2 * WIDTH + 2), NY + 2 * YPAD, NZ),
        (64, NY, NZ),
        (OWN * 7 + 1, 8, NY, NZ),
        (OWN, CHUNK, NY, NZ),
        (2 * 8 * NZ, NZ),
    ]
    chunk = lax.axis_index(chunks).reshape(1)
    message = call(filter_kernel, (4, 2, 32, 8, 128), scratch)(chunk, slabs, before, after, window, bands)
    ring = lax.all_to_all(message.reshape(8, 256, 128), ("u", "c", "b"), 0, 0, tiled=True)
    rotated = call(rotate_kernel, (32, 2, 5, 8, 128))(ring, weights)
    received = lax.all_to_all(rotated.reshape(64, 40, 128), ("z", "x", "b"), 0, 0, tiled=True)
    received = received.reshape(32, 2, 5, 8, 128)
    gram = lax.all_gather(received[:, :, 4].sum(axis=(0, 1)), ("u", "c")).sum(axis=0) / (NX * NY * NZ)
    intersection = jnp.concatenate([gram[:, :NORB], gram[:, NORB : 2 * NORB]], axis=0)
    return intersection, call(lines_kernel, (8, NY, NX))(received)


def solution(mesh):
    grid = Mesh(mesh.devices.reshape(8, 4, 2, 2, 2), ("z", "x", "u", "c", "b"))
    dom = ("z", "x", "u", "c")
    return jax.shard_map(
        local,
        mesh=grid,
        in_specs=(P("b", dom, None, None), P(dom, None, None), P()),
        out_specs=(P(), P("b", dom, None)),
        check_vma=False,
    )
```

```python
import functools

import jax
import jax.numpy as jnp
import ml_dtypes
import numpy as np
from jax import lax
from jax.experimental import pallas as pl
from jax.experimental.pallas import tpu as pltpu
from jax.sharding import Mesh
from jax.sharding import PartitionSpec as P

STENCIL = (
    -5369.0 / 1800.0,
    12.0 / 7.0,
    -15.0 / 56.0,
    10.0 / 189.0,
    -1.0 / 112.0,
    2.0 / 1925.0,
    -1.0 / 16632.0,
)
CENTER = 8.5
HALF = 6.5
WIDTH = 6
NORB, NX, NY, NZ = 16, 1024, 32, 128
CHUNK = 32
OWN = 2
F32 = jnp.float32
BF16 = jnp.bfloat16


def banded(size):
    band = np.zeros((size, size), np.float64)
    for k in range(1, 7):
        band += np.eye(size, k=k) * STENCIL[k] + np.eye(size, k=-k) * STENCIL[k]
    band = (-0.5 / HALF * band).astype(np.float32)
    high = band.astype(ml_dtypes.bfloat16)
    return high, (band - high.astype(np.float32)).astype(ml_dtypes.bfloat16)


def bands():
    high, low = banded(NZ)
    along_z = np.block([[high, low], [high, np.zeros_like(high)]])
    high, low = (np.kron(np.eye(8), part) for part in banded(NY))
    along_y = np.concatenate([high, high, low], axis=1)
    return jnp.asarray(along_z.astype(ml_dtypes.bfloat16)), jnp.asarray(along_y.astype(ml_dtypes.bfloat16))


def split(x):
    high = x.astype(BF16)
    low = (x - high.astype(F32)).astype(BF16)
    return high, low


def dot3(a, b, dims):
    ah, al = split(a)
    bh, bl = split(b)
    dot = functools.partial(lax.dot_general, dimension_numbers=(dims, ((), ())), preferred_element_type=F32)
    return dot(ah, bh) + (dot(ah, bl) + dot(al, bh))


def filter_kernel(
    chunk, slabs, before, after, own, beyond, band_z, band_y, out, field, other, local, zy, result, turned
):
    far, near = 3 * WIDTH, 2 * WIDTH + 2
    for o in range(OWN):
        field[o, 0:far] = before[o]
        field[o, far + CHUNK :] = after[o]
        for s in range(4):
            field[o, far + 8 * s : far + 8 * s + 8] = slabs[s, o]
    order = [beyond[0], beyond[1], own[0], own[1], own[2], own[3], beyond[2], beyond[3]]
    for j, slab in enumerate(order):
        local[8 * j : 8 * j + 8] = (slab + (-1.5 * STENCIL[0] - CENTER)) * (1.0 / HALF)

    def along_zy(source, o, index):
        high, low = split(source[o, pl.ds(index, 8)].reshape(8 * NY, NZ))
        z = jnp.dot(jnp.concatenate([high, low], axis=1), band_z[...], preferred_element_type=F32)
        y = jnp.dot(band_y[...], jnp.concatenate([high, low, high], axis=0), preferred_element_type=F32)
        return ((z[:, :NZ] + z[:, NZ:]) + y).reshape(8, NY, NZ)

    def step(source, shift, first, blocks, double, put):
        def body(i, _):
            o = i // blocks
            start = first + 8 * (i % blocks)
            for y in range(0, NY, 8):
                beside = source[o, pl.ds(start + shift - WIDTH, 8 + 2 * WIDTH), y : y + 8, :]
                total = local[pl.ds(start + 16, 8), y : y + 8, :] * beside[WIDTH : WIDTH + 8]
                total = total + zy[i, :, y : y + 8, :]
                for k in range(1, 7):
                    around = beside[WIDTH + k : WIDTH + 8 + k] + beside[WIDTH - k : WIDTH + 8 - k]
                    total = total + (-0.5 / HALF * STENCIL[k]) * around
                put(o, start, y, total + total if double else total)
            later = jnp.minimum(i + 1, OWN * blocks - 1)
            zy[i + 1] = along_zy(source, later // blocks, first + 8 * (later % blocks) + shift)
            return 0

        zy[0] = along_zy(source, 0, first + shift)
        lax.fori_loop(0, OWN * blocks, body, 0)

    def put_first(o, start, y, total):
        other[o, pl.ds(start + near, 8), y : y + 8, :] = total

    def put_second(o, start, y, total):
        place = (o, pl.ds(start + far, 8), slice(y, y + 8), slice(None))
        field[place] = total - field[place]

    def put_third(o, start, y, total):
        result[o, pl.ds(start, 8), y : y + 8, :] = total - other[o, pl.ds(start + near, 8), y : y + 8, :]

    def outside(target, shift, count):
        blank = jnp.zeros((count, NY, NZ), F32)

        @pl.when(chunk[0] == 0)
        def _():
            for o in range(OWN):
                target[o, shift - count : shift] = blank

        @pl.when(chunk[0] == NX // CHUNK - 1)
        def _():
            for o in range(OWN):
                target[o, shift + CHUNK : shift + CHUNK + count] = blank

    step(field, far, -12, 7, False, put_first)
    outside(other, near, 12)
    step(other, near, -8, 6, True, put_second)
    outside(field, far, 8)
    step(field, far, 0, 4, True, put_third)

    def turn(x, _):
        for b in range(2):
            pieces = [result[o, t * 8 + x, b * 16 : b * 16 + 16, :] for t in range(4) for o in range(OWN)]
            turned[pl.ds((b * 8 + x) * NZ, NZ), :] = jnp.concatenate(pieces, axis=0).T
        return 0

    lax.fori_loop(0, 8, turn, 0)

    def pick(z, _):
        for x in range(4):
            for c in range(4):
                for b in range(2):
                    out[x, c, b, z] = turned[pl.ds(b * 8 * NZ + 16 * z + 4 * x + c, 8, stride=NZ), :]
        return 0

    lax.fori_loop(0, 8, pick, 0)


def rotate_kernel(ring, weights, out, gram):
    lane = lax.broadcasted_iota(jnp.int32, (256, 128), 1) // 32
    sums = jnp.zeros((256, 256), F32)
    for t in range(4):
        halves = []
        for b in range(2):
            value = None
            for c in range(4):
                piece = ring[:, c * 2 + b].reshape(256, 128)
                if c != t:
                    piece = pltpu.roll(piece, ((c - t) % 4) * 32, 1)
                value = piece if value is None else jnp.where(lane == c, piece, value)
            halves.append(value)
        all_orbitals = jnp.concatenate(halves, axis=1)
        turned = dot3(all_orbitals, weights[...], ((1,), (0,)))
        for b in range(2):
            for x in range(4):
                out[:, b, x, t] = turned[x * 64 : (x + 1) * 64, b * 128 : (b + 1) * 128].reshape(8, 8, 128)
        sums = sums + dot3(all_orbitals, all_orbitals, ((0,), (0,)))
    row = lax.broadcasted_iota(jnp.int32, (256, 256), 0) % 16
    column = lax.broadcasted_iota(jnp.int32, (256, 256), 1) % 16
    diagonal = jnp.where(row == column, sums, 0.0).reshape(16, 16, 256).sum(axis=1)
    place = lax.broadcasted_iota(jnp.int32, (256, 128), 0) // 16
    ones = (place == lax.broadcasted_iota(jnp.int32, (256, 128), 1)).astype(F32)
    both = jnp.dot(diagonal, ones, precision=lax.Precision.HIGHEST, preferred_element_type=F32)
    gram[...] = both[0:8] + pltpu.roll(both[8:16], 16, 1)


def lines_kernel(received, out):
    for z in range(8):
        for b in range(2):
            out[:, b * 16 : b * 16 + 16, z * 128 : (z + 1) * 128] = received[z * 2 + b].T.reshape(8, 16, 128)


def call(kernel, out, scratch=()):
    vmem = pl.BlockSpec(memory_space=pltpu.VMEM)
    smem = pl.BlockSpec(memory_space=pltpu.SMEM)
    return lambda *args: pl.pallas_call(
        kernel,
        out_shape=[jax.ShapeDtypeStruct(s, F32) for s in out],
        in_specs=[smem if a.dtype == jnp.int32 else vmem for a in args],
        out_specs=[vmem] * len(out),
        scratch_shapes=[pltpu.VMEM(s, F32) for s in scratch],
        compiler_params=pltpu.CompilerParams(vmem_limit_bytes=48 * 1024 * 1024),
    )(*args)


def local(orbitals, potential, coefficients):
    chunks = ("z", "x")
    dom = ("z", "x", "u", "c")
    count = lax.axis_size(chunks)
    up = [(i, i + 1) for i in range(count - 1)]
    down = [(j, i) for i, j in up]

    shift = [(d, d + 2 if d % 4 >= 2 else d - 2) for d in range(4 * count)]
    beyond = lax.ppermute(potential, dom, [(i, j) for i, j in shift if 0 <= j < 4 * count])
    slabs = lax.all_to_all(orbitals.reshape(4, OWN, 8, NY, NZ), ("u", "c"), 0, 0, tiled=True)
    far = 3 * WIDTH
    part = far - 16
    before = lax.ppermute(jnp.concatenate([slabs[1, :, 8 - part :], slabs[2], slabs[3]], axis=1), chunks, up)
    after = lax.ppermute(jnp.concatenate([slabs[0], slabs[1], slabs[2, :, :part]], axis=1), chunks, down)
    own = lax.all_gather(potential, ("u", "c"))
    beyond = lax.all_gather(beyond, ("u", "c"))

    weights = (coefficients[:, None, :, None] * jnp.eye(16, dtype=F32)[None, :, None, :]).reshape(256, 256)
    scratch = [
        (OWN, CHUNK + 2 * far, NY, NZ),
        (OWN, CHUNK + 2 * (2 * WIDTH + 2), NY, NZ),
        (64, NY, NZ),
        (OWN * 7 + 1, 8, NY, NZ),
        (OWN, CHUNK, NY, NZ),
        (2 * 8 * NZ, NZ),
    ]
    chunk = lax.axis_index(chunks).reshape(1)
    (message,) = call(filter_kernel, [(4, 4, 2, 8, 8, 128)], scratch)(
        chunk, slabs, before, after, own, beyond, *bands()
    )
    ring = lax.all_to_all(message.reshape(32, 64, 128), ("x", "u", "c", "b"), 0, 0, tiled=True)
    rotated, gram = call(rotate_kernel, [(8, 2, 4, 4, 8, 128), (8, 128)])(ring.reshape(4, 8, 64, 128), weights)
    received = lax.all_to_all(rotated.reshape(16, 128, 128), ("z", "b"), 0, 0, tiled=True)
    for axes in (("u", "c"), ("x", "b"), ("z",)):
        gram = lax.all_gather(gram, axes).sum(axis=0)
    gram = gram / (NX * NY * NZ)
    intersection = jnp.concatenate([gram[:, :NORB], gram[:, NORB : 2 * NORB]], axis=0)
    (lines,) = call(lines_kernel, [(8, NY, NX)])(received)
    return intersection, lines


def solution(mesh):
    grid = Mesh(mesh.devices.reshape(8, 4, 2, 2, 2), ("z", "x", "u", "c", "b"))
    dom = ("z", "x", "u", "c")
    return jax.shard_map(
        local,
        mesh=grid,
        in_specs=(P("b", dom, None, None), P(dom, None, None), P()),
        out_specs=(P(), P("b", dom, None)),
        check_vma=False,
    )
```

```python
import functools

import jax
import jax.numpy as jnp
import ml_dtypes
import numpy as np
from jax import lax
from jax.experimental import pallas as pl
from jax.experimental.pallas import tpu as pltpu
from jax.sharding import Mesh
from jax.sharding import PartitionSpec as P

STENCIL = (
    -5369.0 / 1800.0,
    12.0 / 7.0,
    -15.0 / 56.0,
    10.0 / 189.0,
    -1.0 / 112.0,
    2.0 / 1925.0,
    -1.0 / 16632.0,
)
CENTER = 8.5
HALF = 6.5
WIDTH = 6
YPAD = 8
NORB, NX, NY, NZ = 16, 1024, 32, 128
CHUNK = 32
OWN = 2
F32 = jnp.float32
BF16 = jnp.bfloat16


def banded(scale):
    band = np.zeros((NZ, NZ), np.float64)
    for k in range(1, 7):
        band += np.eye(NZ, k=k) * STENCIL[k] + np.eye(NZ, k=-k) * STENCIL[k]
    band = (-0.5 * scale * band).astype(np.float32)
    high = band.astype(ml_dtypes.bfloat16)
    low = (band - high.astype(np.float32)).astype(ml_dtypes.bfloat16)
    zero = np.zeros_like(high)
    return np.block([[high, low], [high, zero]]).astype(ml_dtypes.bfloat16)


def split(x):
    high = x.astype(BF16)
    low = (x - high.astype(F32)).astype(BF16)
    return high, low


def dot3(a, b, dims):
    ah, al = split(a)
    bh, bl = split(b)
    dot = functools.partial(lax.dot_general, dimension_numbers=(dims, ((), ())), preferred_element_type=F32)
    return dot(ah, bh) + (dot(ah, bl) + dot(al, bh))


def filter_kernel(chunk, slabs, before, after, own, beyond, bands, out, field, other, local, zpart, result, turned):
    far, near = 3 * WIDTH, 2 * WIDTH + 2
    rows = slice(YPAD, YPAD + NY)
    zeros = jnp.zeros((YPAD, NZ), F32)

    def clear(p, _):
        for o in range(OWN):
            for pad in (field, other):
                pad[o, jnp.minimum(p, pad.shape[1] - 1), 0:YPAD, :] = zeros
                pad[o, jnp.minimum(p, pad.shape[1] - 1), YPAD + NY :, :] = zeros
        return 0

    lax.fori_loop(0, field.shape[1], clear, 0)
    for o in range(OWN):
        field[o, 0:far, rows, :] = before[o]
        field[o, far + CHUNK :, rows, :] = after[o]
        for s in range(4):
            field[o, far + 8 * s : far + 8 * s + 8, rows, :] = slabs[s, o]
    order = [beyond[0], beyond[1], own[0], own[1], own[2], own[3], beyond[2], beyond[3]]
    for j, slab in enumerate(order):
        local[8 * j : 8 * j + 8] = (slab + (-1.5 * STENCIL[0] - CENTER)) * (1.0 / HALF)

    def along_z(source, o, index, band):
        high, low = split(source[o, pl.ds(index, 8), rows, :].reshape(8 * NY, NZ))
        both = jnp.dot(jnp.concatenate([high, low], axis=1), band, preferred_element_type=F32)
        return (both[:, :NZ] + both[:, NZ:]).reshape(8, NY, NZ)

    def step(source, shift, first, blocks, scale, band, put):
        def body(i, _):
            o = i // blocks
            j = i % blocks
            start = first + 8 * j
            base = start + shift
            for y in range(0, NY, 8):
                beside = source[o, pl.ds(base - WIDTH, 8 + 2 * WIDTH), YPAD + y : YPAD + y + 8, :]
                here = beside[WIDTH : WIDTH + 8]
                total = local[pl.ds(start + 16, 8), y : y + 8, :] * here
                if scale != 1.0:
                    total = total * scale
                total = total + zpart[i, :, y : y + 8, :]
                for k in range(1, 7):
                    around = beside[WIDTH + k : WIDTH + 8 + k] + beside[WIDTH - k : WIDTH + 8 - k]
                    around = around + (
                        source[o, pl.ds(base, 8), YPAD + y + k : YPAD + y + 8 + k, :]
                        + source[o, pl.ds(base, 8), YPAD + y - k : YPAD + y + 8 - k, :]
                    )
                    total = total + (-0.5 * scale / HALF * STENCIL[k]) * around
                put(o, start, y, total)
            later = jnp.minimum(i + 1, OWN * blocks - 1)
            zpart[i + 1] = along_z(source, later // blocks, first + 8 * (later % blocks) + shift, band)
            return 0

        zpart[0] = along_z(source, 0, first + shift, band)
        lax.fori_loop(0, OWN * blocks, body, 0)

    def put_first(o, start, y, total):
        other[o, pl.ds(start + near, 8), YPAD + y : YPAD + y + 8, :] = total

    def put_second(o, start, y, total):
        place = (o, pl.ds(start + far, 8), slice(YPAD + y, YPAD + y + 8), slice(None))
        field[place] = total - field[place]

    def put_third(o, start, y, total):
        place = (o, pl.ds(start + near, 8), slice(YPAD + y, YPAD + y + 8), slice(None))
        result[o, pl.ds(start, 8), y : y + 8, :] = total - other[place]

    def outside(target, shift, count):
        blank = jnp.zeros((count, NY, NZ), F32)

        @pl.when(chunk[0] == 0)
        def _():
            for o in range(OWN):
                target[o, shift - count : shift, rows, :] = blank

        @pl.when(chunk[0] == NX // CHUNK - 1)
        def _():
            for o in range(OWN):
                target[o, shift + CHUNK : shift + CHUNK + count, rows, :] = blank

    step(field, far, -12, 7, 1.0, bands[0], put_first)
    outside(other, near, 12)
    step(other, near, -8, 6, 2.0, bands[1], put_second)
    outside(field, far, 8)
    step(field, far, 0, 4, 2.0, bands[1], put_third)

    def turn(x, _):
        for b in range(2):
            pieces = [result[o, t * 8 + x, b * 16 : b * 16 + 16, :] for t in range(4) for o in range(OWN)]
            turned[pl.ds((b * 8 + x) * NZ, NZ), :] = jnp.concatenate(pieces, axis=0).T
        return 0

    lax.fori_loop(0, 8, turn, 0)

    def pick(z, _):
        for x in range(4):
            for c in range(4):
                for b in range(2):
                    out[x, c, b, z] = turned[pl.ds(b * 8 * NZ + 16 * z + 4 * x + c, 8, stride=NZ), :]
        return 0

    lax.fori_loop(0, 8, pick, 0)


def rotate_kernel(ring, weights, out, gram):
    lane = lax.broadcasted_iota(jnp.int32, (256, 128), 1) // 32
    sums = jnp.zeros((256, 256), F32)
    for t in range(4):
        halves = []
        for b in range(2):
            value = None
            for c in range(4):
                piece = ring[:, c * 2 + b].reshape(256, 128)
                if c != t:
                    piece = pltpu.roll(piece, ((c - t) % 4) * 32, 1)
                value = piece if value is None else jnp.where(lane == c, piece, value)
            halves.append(value)
        all_orbitals = jnp.concatenate(halves, axis=1)
        turned = dot3(all_orbitals, weights[...], ((1,), (0,)))
        for b in range(2):
            for x in range(4):
                out[:, b, x, t] = turned[x * 64 : (x + 1) * 64, b * 128 : (b + 1) * 128].reshape(8, 8, 128)
        sums = sums + dot3(all_orbitals, all_orbitals, ((0,), (0,)))
    row = lax.broadcasted_iota(jnp.int32, (256, 256), 0) % 16
    column = lax.broadcasted_iota(jnp.int32, (256, 256), 1) % 16
    diagonal = jnp.where(row == column, sums, 0.0).reshape(16, 16, 256).sum(axis=1)
    place = lax.broadcasted_iota(jnp.int32, (256, 128), 0) // 16
    ones = (place == lax.broadcasted_iota(jnp.int32, (256, 128), 1)).astype(F32)
    both = jnp.dot(diagonal, ones, precision=lax.Precision.HIGHEST, preferred_element_type=F32)
    gram[...] = both[0:8] + pltpu.roll(both[8:16], 16, 1)


def lines_kernel(received, out):
    for z in range(8):
        for b in range(2):
            out[:, b * 16 : b * 16 + 16, z * 128 : (z + 1) * 128] = received[z * 2 + b].T.reshape(8, 16, 128)


def call(kernel, out, scratch=()):
    vmem = pl.BlockSpec(memory_space=pltpu.VMEM)
    smem = pl.BlockSpec(memory_space=pltpu.SMEM)
    return lambda *args: pl.pallas_call(
        kernel,
        out_shape=[jax.ShapeDtypeStruct(s, F32) for s in out],
        in_specs=[smem if a.dtype == jnp.int32 else vmem for a in args],
        out_specs=[vmem] * len(out),
        scratch_shapes=[pltpu.VMEM(s, F32) for s in scratch],
        compiler_params=pltpu.CompilerParams(vmem_limit_bytes=48 * 1024 * 1024),
    )(*args)


def local(orbitals, potential, coefficients):
    chunks = ("z", "x")
    dom = ("z", "x", "u", "c")
    count = lax.axis_size(chunks)
    up = [(i, i + 1) for i in range(count - 1)]
    down = [(j, i) for i, j in up]

    shift = [(d, d + 2 if d % 4 >= 2 else d - 2) for d in range(4 * count)]
    beyond = lax.ppermute(potential, dom, [(i, j) for i, j in shift if 0 <= j < 4 * count])
    slabs = lax.all_to_all(orbitals.reshape(4, OWN, 8, NY, NZ), ("u", "c"), 0, 0, tiled=True)
    own = lax.all_gather(potential, ("u", "c"))
    slabs, own, beyond = lax.optimization_barrier((slabs, own, beyond))
    far = 3 * WIDTH
    part = far - 16
    before = lax.ppermute(jnp.concatenate([slabs[1, :, 8 - part :], slabs[2], slabs[3]], axis=1), chunks, up)
    after = lax.ppermute(jnp.concatenate([slabs[0], slabs[1], slabs[2, :, :part]], axis=1), chunks, down)
    beyond = lax.all_gather(beyond, ("u", "c"))

    weights = (coefficients[:, None, :, None] * jnp.eye(16, dtype=F32)[None, :, None, :]).reshape(256, 256)
    scratch = [
        (OWN, CHUNK + 2 * far, NY + 2 * YPAD, NZ),
        (OWN, CHUNK + 2 * (2 * WIDTH + 2), NY + 2 * YPAD, NZ),
        (64, NY, NZ),
        (OWN * 7 + 1, 8, NY, NZ),
        (OWN, CHUNK, NY, NZ),
        (2 * 8 * NZ, NZ),
    ]
    bands = jnp.asarray(np.stack([banded(1.0 / HALF), banded(2.0 / HALF)]))
    chunk = lax.axis_index(chunks).reshape(1)
    (message,) = call(filter_kernel, [(4, 4, 2, 8, 8, 128)], scratch)(
        chunk, slabs, before, after, own, beyond, bands
    )
    ring = lax.all_to_all(message.reshape(32, 64, 128), ("x", "u", "c", "b"), 0, 0, tiled=True)
    rotated, gram = call(rotate_kernel, [(8, 2, 4, 4, 8, 128), (8, 128)])(ring.reshape(4, 8, 64, 128), weights)
    received = lax.all_to_all(rotated.reshape(16, 128, 128), ("z", "b"), 0, 0, tiled=True)
    for axes in (("u", "c"), ("x",)):
        gram = lax.all_gather(gram, axes).sum(axis=0)
    gram, received = lax.optimization_barrier((gram, received))
    copies = jnp.broadcast_to(gram[None], (16, 8, 128))
    gram = lax.all_to_all(copies, ("z", "b"), 0, 0, tiled=True).sum(axis=0)
    gram = gram / (NX * NY * NZ)
    intersection = jnp.concatenate([gram[:, :NORB], gram[:, NORB : 2 * NORB]], axis=0)
    (lines,) = call(lines_kernel, [(8, NY, NX)])(received)
    return intersection, lines


def solution(mesh):
    grid = Mesh(mesh.devices.reshape(8, 4, 2, 2, 2), ("z", "x", "u", "c", "b"))
    dom = ("z", "x", "u", "c")
    return jax.shard_map(
        local,
        mesh=grid,
        in_specs=(P("b", dom, None, None), P(dom, None, None), P()),
        out_specs=(P(), P("b", dom, None)),
        check_vma=False,
    )
```

```python
import functools

import jax
import jax.numpy as jnp
import ml_dtypes
import numpy as np
from jax import lax
from jax.experimental import pallas as pl
from jax.experimental.pallas import tpu as pltpu
from jax.sharding import Mesh
from jax.sharding import PartitionSpec as P

STENCIL = (
    -5369.0 / 1800.0,
    12.0 / 7.0,
    -15.0 / 56.0,
    10.0 / 189.0,
    -1.0 / 112.0,
    2.0 / 1925.0,
    -1.0 / 16632.0,
)
CENTER = 8.5
HALF = 6.5
WIDTH = 6
YPAD = 8
NORB, NX, NY, NZ = 16, 1024, 32, 128
CHUNK = 32
OWN = 2
F32 = jnp.float32
BF16 = jnp.bfloat16


def banded(scale):
    band = np.zeros((NZ, NZ), np.float64)
    for k in range(1, 7):
        band += np.eye(NZ, k=k) * STENCIL[k] + np.eye(NZ, k=-k) * STENCIL[k]
    band = (-0.5 * scale * band).astype(np.float32)
    high = band.astype(ml_dtypes.bfloat16)
    low = (band - high.astype(np.float32)).astype(ml_dtypes.bfloat16)
    zero = np.zeros_like(high)
    return np.block([[high, low], [high, zero]]).astype(ml_dtypes.bfloat16)


def split(x):
    high = x.astype(BF16)
    low = (x - high.astype(F32)).astype(BF16)
    return high, low


def dot3(a, b, dims):
    ah, al = split(a)
    bh, bl = split(b)
    dot = functools.partial(lax.dot_general, dimension_numbers=(dims, ((), ())), preferred_element_type=F32)
    return dot(ah, bh) + (dot(ah, bl) + dot(al, bh))


def filter_kernel(chunk, slabs, before, after, own, beyond, bands, out, field, other, local, zpart, result, turned):
    far, near = 3 * WIDTH, 2 * WIDTH + 2
    rows = slice(YPAD, YPAD + NY)
    zeros = jnp.zeros((YPAD, NZ), F32)

    def clear(p, _):
        for o in range(OWN):
            for pad in (field, other):
                pad[o, jnp.minimum(p, pad.shape[1] - 1), 0:YPAD, :] = zeros
                pad[o, jnp.minimum(p, pad.shape[1] - 1), YPAD + NY :, :] = zeros
        return 0

    lax.fori_loop(0, field.shape[1], clear, 0)
    for o in range(OWN):
        field[o, 0:far, rows, :] = before[o]
        field[o, far + CHUNK :, rows, :] = after[o]
        for s in range(4):
            field[o, far + 8 * s : far + 8 * s + 8, rows, :] = slabs[s, o]
    order = [beyond[0], beyond[1], own[0], own[1], own[2], own[3], beyond[2], beyond[3]]
    for j, slab in enumerate(order):
        local[8 * j : 8 * j + 8] = (slab + (-1.5 * STENCIL[0] - CENTER)) * (1.0 / HALF)

    def along_z(source, o, index, band):
        high, low = split(source[o, pl.ds(index, 8), rows, :].reshape(8 * NY, NZ))
        both = jnp.dot(jnp.concatenate([high, low], axis=1), band, preferred_element_type=F32)
        return (both[:, :NZ] + both[:, NZ:]).reshape(8, NY, NZ)

    def step(source, shift, first, blocks, scale, band, put):
        def body(i, _):
            o = i // blocks
            j = i % blocks
            start = first + 8 * j
            base = start + shift
            for y in range(0, NY, 8):
                beside = source[o, pl.ds(base - WIDTH, 8 + 2 * WIDTH), YPAD + y : YPAD + y + 8, :]
                here = beside[WIDTH : WIDTH + 8]
                total = local[pl.ds(start + 16, 8), y : y + 8, :] * here
                if scale != 1.0:
                    total = total * scale
                total = total + zpart[i, :, y : y + 8, :]
                for k in range(1, 7):
                    around = beside[WIDTH + k : WIDTH + 8 + k] + beside[WIDTH - k : WIDTH + 8 - k]
                    around = around + (
                        source[o, pl.ds(base, 8), YPAD + y + k : YPAD + y + 8 + k, :]
                        + source[o, pl.ds(base, 8), YPAD + y - k : YPAD + y + 8 - k, :]
                    )
                    total = total + (-0.5 * scale / HALF * STENCIL[k]) * around
                put(o, start, y, total)
            later = jnp.minimum(i + 1, OWN * blocks - 1)
            zpart[i + 1] = along_z(source, later // blocks, first + 8 * (later % blocks) + shift, band)
            return 0

        zpart[0] = along_z(source, 0, first + shift, band)
        lax.fori_loop(0, OWN * blocks, body, 0)

    def put_first(o, start, y, total):
        other[o, pl.ds(start + near, 8), YPAD + y : YPAD + y + 8, :] = total

    def put_second(o, start, y, total):
        place = (o, pl.ds(start + far, 8), slice(YPAD + y, YPAD + y + 8), slice(None))
        field[place] = total - field[place]

    def put_third(o, start, y, total):
        place = (o, pl.ds(start + near, 8), slice(YPAD + y, YPAD + y + 8), slice(None))
        result[o, pl.ds(start, 8), y : y + 8, :] = total - other[place]

    def outside(target, shift, count):
        blank = jnp.zeros((count, NY, NZ), F32)

        @pl.when(chunk[0] == 0)
        def _():
            for o in range(OWN):
                target[o, shift - count : shift, rows, :] = blank

        @pl.when(chunk[0] == NX // CHUNK - 1)
        def _():
            for o in range(OWN):
                target[o, shift + CHUNK : shift + CHUNK + count, rows, :] = blank

    step(field, far, -12, 7, 1.0, bands[0], put_first)
    outside(other, near, 12)
    step(other, near, -8, 6, 2.0, bands[1], put_second)
    outside(field, far, 8)
    step(field, far, 0, 4, 2.0, bands[1], put_third)

    def turn(x, _):
        for b in range(2):
            pieces = [result[o, t * 8 + x, b * 16 : b * 16 + 16, :] for t in range(4) for o in range(OWN)]
            turned[pl.ds((b * 8 + x) * NZ, NZ), :] = jnp.concatenate(pieces, axis=0).T
        return 0

    lax.fori_loop(0, 8, turn, 0)

    def pick(q, _):
        for c in range(4):
            for b in range(2):
                out[c, b, q] = turned[pl.ds(b * 8 * NZ + 4 * q + c, 8, stride=NZ), :]
        return 0

    lax.fori_loop(0, NZ // 4, pick, 0)


def rotate_kernel(ring, weights, out, gram):
    lane = lax.broadcasted_iota(jnp.int32, (256, 128), 1) // 32
    sums = jnp.zeros((256, 256), F32)
    for t in range(4):
        halves = []
        for b in range(2):
            value = None
            for c in range(4):
                piece = ring[c * 2 + b]
                if c != t:
                    piece = pltpu.roll(piece, ((c - t) % 4) * 32, 1)
                value = piece if value is None else jnp.where(lane == c, piece, value)
            halves.append(value)
        all_orbitals = jnp.concatenate(halves, axis=1)
        turned = dot3(all_orbitals, weights[...], ((1,), (0,)))
        for b in range(2):
            out[:, b, t] = turned[:, b * 128 : (b + 1) * 128].reshape(32, 8, 128)
        sums = sums + dot3(all_orbitals, all_orbitals, ((0,), (0,)))
    row = lax.broadcasted_iota(jnp.int32, (256, 256), 0) % 16
    column = lax.broadcasted_iota(jnp.int32, (256, 256), 1) % 16
    diagonal = jnp.where(row == column, sums, 0.0).reshape(16, 16, 256).sum(axis=1)
    place = lax.broadcasted_iota(jnp.int32, (256, 128), 0) // 16
    ones = (place == lax.broadcasted_iota(jnp.int32, (256, 128), 1)).astype(F32)
    both = jnp.dot(diagonal, ones, precision=lax.Precision.HIGHEST, preferred_element_type=F32)
    gram[...] = both[0:8] + pltpu.roll(both[8:16], 16, 1)


def lines_kernel(received, out):
    for b in range(2):
        for s in range(8):
            block = received[s * 4 : s * 4 + 4, b].reshape(128, 128).T.reshape(8, 16, 128)
            out[:, b * 16 : b * 16 + 16, s * 128 : (s + 1) * 128] = block


def call(kernel, out, scratch=()):
    vmem = pl.BlockSpec(memory_space=pltpu.VMEM)
    smem = pl.BlockSpec(memory_space=pltpu.SMEM)
    return lambda *args: pl.pallas_call(
        kernel,
        out_shape=[jax.ShapeDtypeStruct(s, F32) for s in out],
        in_specs=[smem if a.dtype == jnp.int32 else vmem for a in args],
        out_specs=[vmem] * len(out),
        scratch_shapes=[pltpu.VMEM(s, F32) for s in scratch],
        compiler_params=pltpu.CompilerParams(vmem_limit_bytes=48 * 1024 * 1024),
    )(*args)


def local(orbitals, potential, coefficients):
    chunks = ("z", "x")
    dom = ("z", "x", "u", "c")
    count = lax.axis_size(chunks)
    up = [(i, i + 1) for i in range(count - 1)]
    down = [(j, i) for i, j in up]

    shift = [(d, d + 2 if d % 4 >= 2 else d - 2) for d in range(4 * count)]
    beyond = lax.ppermute(potential, dom, [(i, j) for i, j in shift if 0 <= j < 4 * count])
    slabs = lax.all_to_all(orbitals.reshape(4, OWN, 8, NY, NZ), ("u", "c"), 0, 0, tiled=True)
    slabs, beyond = lax.optimization_barrier((slabs, beyond))
    far = 3 * WIDTH
    part = far - 16
    before = lax.ppermute(jnp.concatenate([slabs[1, :, 8 - part :], slabs[2], slabs[3]], axis=1), chunks, up)
    after = lax.ppermute(jnp.concatenate([slabs[0], slabs[1], slabs[2, :, :part]], axis=1), chunks, down)
    own = lax.all_gather(potential, ("u", "c"))
    beyond = lax.all_gather(beyond, ("u", "c"))

    weights = (coefficients[:, None, :, None] * jnp.eye(16, dtype=F32)[None, :, None, :]).reshape(256, 256)
    scratch = [
        (OWN, CHUNK + 2 * far, NY + 2 * YPAD, NZ),
        (OWN, CHUNK + 2 * (2 * WIDTH + 2), NY + 2 * YPAD, NZ),
        (64, NY, NZ),
        (OWN * 7 + 1, 8, NY, NZ),
        (OWN, CHUNK, NY, NZ),
        (2 * 8 * NZ, NZ),
    ]
    bands = jnp.asarray(np.stack([banded(1.0 / HALF), banded(2.0 / HALF)]))
    chunk = lax.axis_index(chunks).reshape(1)
    (message,) = call(filter_kernel, [(4, 2, 32, 8, 128)], scratch)(
        chunk, slabs, before, after, own, beyond, bands
    )
    ring = lax.all_to_all(message.reshape(8, 256, 128), ("u", "c", "b"), 0, 0, tiled=True)
    rotated, gram = call(rotate_kernel, [(32, 2, 4, 8, 128), (8, 128)])(ring, weights)
    received = lax.all_to_all(rotated.reshape(64, 32, 128), ("z", "x", "b"), 0, 0, tiled=True)
    gram = lax.all_gather(gram, ("u", "c")).sum(axis=0)
    for axis, bit in (("x", 1), ("x", 2), ("b", 1), ("z", 1), ("z", 2), ("z", 4)):
        gram = gram + lax.ppermute(gram, axis, [(i, i ^ bit) for i in range(lax.axis_size(axis))])
    gram = gram / (NX * NY * NZ)
    intersection = jnp.concatenate([gram[:, :NORB], gram[:, NORB : 2 * NORB]], axis=0)
    (lines,) = call(lines_kernel, [(8, NY, NX)])(received.reshape(32, 2, 32, 128))
    return intersection, lines


def solution(mesh):
    grid = Mesh(mesh.devices.reshape(8, 4, 2, 2, 2), ("z", "x", "u", "c", "b"))
    dom = ("z", "x", "u", "c")
    return jax.shard_map(
        local,
        mesh=grid,
        in_specs=(P("b", dom, None, None), P(dom, None, None), P()),
        out_specs=(P(), P("b", dom, None)),
        check_vma=False,
    )
```

```python
import functools

import jax
import jax.numpy as jnp
import ml_dtypes
import numpy as np
from jax import lax
from jax.experimental import pallas as pl
from jax.experimental.pallas import tpu as pltpu
from jax.sharding import Mesh
from jax.sharding import PartitionSpec as P

STENCIL = (
    -5369.0 / 1800.0,
    12.0 / 7.0,
    -15.0 / 56.0,
    10.0 / 189.0,
    -1.0 / 112.0,
    2.0 / 1925.0,
    -1.0 / 16632.0,
)
CENTER = 8.5
HALF = 6.5
WIDTH = 6
EXT = 6
NORB, NX, NY, NZ = 16, 1024, 32, 128
CHUNK = 32
OWN = 2
F32 = jnp.float32
BF16 = jnp.bfloat16


def banded(scale):
    band = np.zeros((NZ, NZ), np.float64)
    for k in range(1, 7):
        band += np.eye(NZ, k=k) * STENCIL[k] + np.eye(NZ, k=-k) * STENCIL[k]
    band = (-0.5 * scale * band).astype(np.float32)
    high = band.astype(ml_dtypes.bfloat16)
    low = (band - high.astype(np.float32)).astype(ml_dtypes.bfloat16)
    zero = np.zeros_like(high)
    return np.block([[high, low], [high, zero]]).astype(ml_dtypes.bfloat16)


def split(x):
    high = x.astype(BF16)
    low = (x - high.astype(F32)).astype(BF16)
    return high, low


def dot3(a, b, dims):
    ah, al = split(a)
    bh, bl = split(b)
    dot = functools.partial(lax.dot_general, dimension_numbers=(dims, ((), ())), preferred_element_type=F32)
    return dot(ah, bh) + (dot(ah, bl) + dot(al, bh))


def filter_kernel(
    chunk, slabs, before, after, own, beyond, bands, out, field, other, local, zy, result, turned
):
    far, near = 3 * WIDTH, 2 * WIDTH + 2
    row = lax.broadcasted_iota(jnp.int32, (8, 8, NZ), 1) % 4

    def store(target, plane, r, value):
        planes = pl.ds(plane, 8)
        target[planes, EXT + r] = value
        if r >= 8 - EXT:
            target[planes, r - (8 - EXT)] = jnp.where(row == 0, 0.0, pltpu.roll(value, 1, 1))
        if r < EXT:
            target[planes, EXT + 8 + r] = jnp.where(row == 3, 0.0, pltpu.roll(value, 7, 1))

    def tiles(pieces):
        return jnp.swapaxes(jnp.concatenate([piece.reshape(4, 8, NZ) for piece in pieces], axis=0), 0, 1)

    def enter(plane, pieces):
        value = tiles(pieces)
        field[plane, EXT : EXT + 8] = value
        field[plane, 0:EXT] = jnp.where(row[:EXT] == 0, 0.0, pltpu.roll(value[8 - EXT :], 1, 1))
        field[plane, EXT + 8 :] = jnp.where(row[:EXT] == 3, 0.0, pltpu.roll(value[:EXT], 7, 1))

    def enter_ends(p, _):
        enter(p, [before[o, p] for o in range(OWN)])
        enter(far + CHUNK + p, [after[o, p] for o in range(OWN)])
        return 0

    lax.fori_loop(0, far, enter_ends, 0)

    def enter_slabs(p, _):
        for s in range(4):
            enter(far + 8 * s + p, [slabs[s, o, p] for o in range(OWN)])
        return 0

    lax.fori_loop(0, 8, enter_slabs, 0)

    def enter_local(p, _):
        for j, (source, s) in enumerate(
            [(beyond, 0), (beyond, 1), (own, 0), (own, 1), (own, 2), (own, 3), (beyond, 2), (beyond, 3)]
        ):
            value = (source[s, p] + (-1.5 * STENCIL[0] - CENTER)) * (1.0 / HALF)
            local[8 * j + p] = tiles([value, value])
        return 0

    lax.fori_loop(0, 8, enter_local, 0)

    def around(window, total):
        for k in range(1, 7):
            beside = window[WIDTH + k : WIDTH + 8 + k] + window[WIDTH - k : WIDTH + 8 - k]
            term = (-0.5 / HALF * STENCIL[k]) * beside
            total = term if total is None else total + term
        return total

    def along_zy(slot, source, index):
        high, low = split(source[pl.ds(index, 8), EXT : EXT + 8].reshape(8 * 64, NZ))
        both = jnp.dot(jnp.concatenate([high, low], axis=1), bands[...], preferred_element_type=F32)
        z = (both[:, :NZ] + both[:, NZ:]).reshape(8, 8, 8, NZ)
        for x in range(8):
            zy[slot, x] = around(source[index + x], z[x])

    def step(source, shift, first, blocks, put):
        def body(i, _):
            start = first + 8 * i
            for r in range(8):
                window = source[pl.ds(start + shift - WIDTH, 8 + 2 * WIDTH), EXT + r]
                total = local[pl.ds(start + 16, 8), r] * window[WIDTH : WIDTH + 8]
                put(start, r, around(window, total + zy[i, :, r]))
            along_zy(i + 1, source, first + 8 * jnp.minimum(i + 1, blocks - 1) + shift)
            return 0

        along_zy(0, source, first + shift)
        lax.fori_loop(0, blocks, body, 0)

    def put_first(start, r, total):
        store(other, start + near, r, total)

    def put_second(start, r, total):
        store(field, start + far, r, (total + total) - field[pl.ds(start + far, 8), EXT + r])

    def put_third(start, r, total):
        result[pl.ds(start, 8), r] = (total + total) - other[pl.ds(start + near, 8), EXT + r]

    def outside(target, shift, count):
        blank = jnp.zeros((count, 8 + 2 * EXT, 8, NZ), F32)

        @pl.when(chunk[0] == 0)
        def _():
            target[shift - count : shift] = blank

        @pl.when(chunk[0] == NX // CHUNK - 1)
        def _():
            target[shift + CHUNK : shift + CHUNK + count] = blank

    step(field, far, -12, 7, put_first)
    outside(other, near, 12)
    step(other, near, -8, 6, put_second)
    outside(field, far, 8)
    step(field, far, 0, 4, put_third)

    def turn(x, _):
        for b in range(2):
            pieces = [result[t * 8 + x, b * 4 + r] for t in range(4) for r in range(4)]
            turned[pl.ds((b * 8 + x) * NZ, NZ), :] = jnp.concatenate(pieces, axis=0).T
        return 0

    lax.fori_loop(0, 8, turn, 0)

    def pick(q, _):
        for c in range(4):
            for b in range(2):
                out[c, b, q] = turned[pl.ds(b * 8 * NZ + 4 * q + c, 8, stride=NZ), :]
        return 0

    lax.fori_loop(0, NZ // 4, pick, 0)


def rotate_kernel(ring, coefficients, out, gram):
    exact = functools.partial(
        lax.dot_general, precision=lax.Precision.HIGHEST, preferred_element_type=F32
    )
    row = lax.broadcasted_iota(jnp.int32, (256, 256), 0)
    column = lax.broadcasted_iota(jnp.int32, (256, 256), 1)
    number = lax.broadcasted_iota(jnp.int32, (256, 16), 0)
    entry = lax.broadcasted_iota(jnp.int32, (256, 16), 1)
    before = (number // 32 * 2 + number // 4 % 2 == entry).astype(F32)
    after = (number // 16 == entry).astype(F32)
    spread = exact(before, exact(coefficients[...], after, (((1,), (1,)), ((), ()))), (((1,), (0,)), ((), ())))
    same = (row // 8 % 4 == column % 4) & (row % 4 == column // 4 % 4)
    weights = jnp.where(same, spread, 0.0)

    lane = lax.broadcasted_iota(jnp.int32, (256, 128), 1) // 32
    sums = jnp.zeros((256, 256), F32)
    for t in range(4):
        halves = []
        for b in range(2):
            value = None
            for c in range(4):
                piece = ring[c * 2 + b]
                if c != t:
                    piece = pltpu.roll(piece, ((c - t) % 4) * 32, 1)
                value = piece if value is None else jnp.where(lane == c, piece, value)
            halves.append(value)
        all_orbitals = jnp.concatenate(halves, axis=1)
        turned = dot3(all_orbitals, weights, ((1,), (0,)))
        for b in range(2):
            out[:, b, t] = turned[:, b * 128 : (b + 1) * 128].reshape(32, 8, 128)
        sums = sums + dot3(all_orbitals, all_orbitals, ((0,), (0,)))
    diagonal = jnp.where((row // 8 % 4 == column // 8 % 4) & (row % 4 == column % 4), sums, 0.0)
    both = exact(before, exact(diagonal, before, (((1,), (0,)), ((), ()))), (((0,), (0,)), ((), ())))
    gram[...] = jnp.concatenate([both[0:8], both[8:16], jnp.zeros((8, 96), F32)], axis=1)


def lines_kernel(received, out):
    low = lax.broadcasted_iota(jnp.int32, (16, 8, 128), 1) < 4
    for s in range(8):
        first, second = (received[s * 4 : s * 4 + 4, b].reshape(128, 128).T.reshape(16, 8, 128) for b in range(2))
        even = jnp.where(low, first, pltpu.roll(second, 4, 1)).reshape(8, 2, 8, 128)
        odd = jnp.where(low, pltpu.roll(first, 4, 1), second).reshape(8, 2, 8, 128)
        for q in range(2):
            out[:, q * 16 : q * 16 + 8, s * 128 : (s + 1) * 128] = even[:, q]
            out[:, q * 16 + 8 : q * 16 + 16, s * 128 : (s + 1) * 128] = odd[:, q]


def call(kernel, out, scratch=()):
    vmem = pl.BlockSpec(memory_space=pltpu.VMEM)
    smem = pl.BlockSpec(memory_space=pltpu.SMEM)
    return lambda *args: pl.pallas_call(
        kernel,
        out_shape=[jax.ShapeDtypeStruct(s, F32) for s in out],
        in_specs=[smem if a.dtype == jnp.int32 else vmem for a in args],
        out_specs=[vmem] * len(out),
        scratch_shapes=[pltpu.VMEM(s, F32) for s in scratch],
        compiler_params=pltpu.CompilerParams(vmem_limit_bytes=48 * 1024 * 1024),
    )(*args)


def four(x, one, one_bit, two, two_bit):
    def swap(axes, bits):
        sizes = [lax.axis_size(a) for a in axes]
        flat = [np.ravel_multi_index([i ^ b for i, b in zip(at, bits)], sizes) for at in np.ndindex(*sizes)]
        return lax.ppermute(x, axes, [(i, int(j)) for i, j in enumerate(flat)])

    if one == two:
        parts = [swap((one,), (bits,)) for bits in (one_bit, two_bit, one_bit ^ two_bit)]
    else:
        parts = [swap((one, two), bits) for bits in ((one_bit, 0), (0, two_bit), (one_bit, two_bit))]
    return (x + parts[0]) + (parts[1] + parts[2])


def local(orbitals, potential, coefficients):
    chunks = ("z", "x")
    dom = ("z", "x", "u", "c")
    count = lax.axis_size(chunks)
    up = [(i, i + 1) for i in range(count - 1)]
    down = [(j, i) for i, j in up]

    shift = [(d, d + 2 if d % 4 >= 2 else d - 2) for d in range(4 * count)]
    beyond = lax.ppermute(potential, dom, [(i, j) for i, j in shift if 0 <= j < 4 * count])
    slabs = lax.all_to_all(orbitals.reshape(4, OWN, 8, NY, NZ), ("u", "c"), 0, 0, tiled=True)
    slabs, beyond = lax.optimization_barrier((slabs, beyond))
    far = 3 * WIDTH
    part = far - 16
    before = lax.ppermute(jnp.concatenate([slabs[1, :, 8 - part :], slabs[2], slabs[3]], axis=1), chunks, up)
    after = lax.ppermute(jnp.concatenate([slabs[0], slabs[1], slabs[2, :, :part]], axis=1), chunks, down)
    own = lax.all_gather(potential, ("u", "c"))
    beyond = lax.all_gather(beyond, ("u", "c"))

    scratch = [
        (CHUNK + 2 * far, 8 + 2 * EXT, 8, NZ),
        (CHUNK + 2 * (2 * WIDTH + 2), 8 + 2 * EXT, 8, NZ),
        (64, 8, 8, NZ),
        (8, 8, 8, 8, NZ),
        (CHUNK, 8, 8, NZ),
        (2 * 8 * NZ, NZ),
    ]
    bands = jnp.asarray(banded(1.0 / HALF))
    chunk = lax.axis_index(chunks).reshape(1)
    (message,) = call(filter_kernel, [(4, 2, 32, 8, 128)], scratch)(
        chunk, slabs, before, after, own, beyond, bands
    )
    ring = lax.all_to_all(message.reshape(8, 256, 128), ("u", "c", "b"), 0, 0, tiled=True)
    rotated, gram = call(rotate_kernel, [(32, 2, 4, 8, 128), (8, 128)])(ring, coefficients)
    received = lax.all_to_all(rotated.reshape(64, 32, 128), ("z", "x", "b"), 0, 0, tiled=True)
    gram = lax.all_gather(gram, ("u", "c")).sum(axis=0)
    for axes in (("x", 1, "x", 2), ("z", 1, "z", 2), ("z", 4, "b", 1)):
        gram = four(gram, *axes)
    gram = gram / (NX * NY * NZ)
    intersection = jnp.concatenate([gram[:, :NORB], gram[:, NORB : 2 * NORB]], axis=0)
    (lines,) = call(lines_kernel, [(8, NY, NX)])(received.reshape(32, 2, 32, 128))
    return intersection, lines


def solution(mesh):
    grid = Mesh(mesh.devices.reshape(8, 4, 2, 2, 2), ("z", "x", "u", "c", "b"))
    dom = ("z", "x", "u", "c")
    return jax.shard_map(
        local,
        mesh=grid,
        in_specs=(P("b", dom, None, None), P(dom, None, None), P()),
        out_specs=(P(), P("b", dom, None)),
        check_vma=False,
    )
```

```python
import functools

import jax
import jax.numpy as jnp
import ml_dtypes
import numpy as np
from jax import lax
from jax.experimental import pallas as pl
from jax.experimental.pallas import tpu as pltpu
from jax.sharding import Mesh
from jax.sharding import PartitionSpec as P

STENCIL = (
    -5369.0 / 1800.0,
    12.0 / 7.0,
    -15.0 / 56.0,
    10.0 / 189.0,
    -1.0 / 112.0,
    2.0 / 1925.0,
    -1.0 / 16632.0,
)
CENTER = 8.5
HALF = 6.5
WIDTH = 6
EXT = 6
NORB, NX, NY, NZ = 16, 1024, 32, 128
CHUNK = 32
OWN = 2
F32 = jnp.float32
BF16 = jnp.bfloat16


def banded(scale):
    band = np.zeros((NZ, NZ), np.float64)
    for k in range(1, 7):
        band += np.eye(NZ, k=k) * STENCIL[k] + np.eye(NZ, k=-k) * STENCIL[k]
    band = (-0.5 * scale * band).astype(np.float32)
    high = band.astype(ml_dtypes.bfloat16)
    low = (band - high.astype(np.float32)).astype(ml_dtypes.bfloat16)
    zero = np.zeros_like(high)
    return np.block([[high, low], [high, zero]]).astype(ml_dtypes.bfloat16)


def split(x):
    high = x.astype(BF16)
    low = (x - high.astype(F32)).astype(BF16)
    return high, low


def dot3(a, b, dims):
    ah, al = split(a)
    bh, bl = split(b)
    dot = functools.partial(lax.dot_general, dimension_numbers=(dims, ((), ())), preferred_element_type=F32)
    return dot(ah, bh) + (dot(ah, bl) + dot(al, bh))


def filter_kernel(
    chunk, slabs, before, after, own, beyond, bands, out, field, other, local, zy, result, turned
):
    far, near = 3 * WIDTH, 2 * WIDTH + 2
    row = lax.broadcasted_iota(jnp.int32, (8, 8, NZ), 1) % 4

    def store(target, plane, r, value):
        planes = pl.ds(plane, 8)
        target[planes, EXT + r] = value
        if r >= 8 - EXT:
            target[planes, r - (8 - EXT)] = jnp.where(row == 0, 0.0, pltpu.roll(value, 1, 1))
        if r < EXT:
            target[planes, EXT + 8 + r] = jnp.where(row == 3, 0.0, pltpu.roll(value, 7, 1))

    def tiles(sources):
        rows = [jnp.concatenate([source[(*at, pl.ds(r, 4, stride=8), slice(None))] for source, at in sources], axis=0) for r in range(8)]
        return jnp.stack(rows)

    def enter(plane, sources):
        value = tiles(sources)
        field[plane, EXT : EXT + 8] = value
        field[plane, 0:EXT] = jnp.where(row[:EXT] == 0, 0.0, pltpu.roll(value[8 - EXT :], 1, 1))
        field[plane, EXT + 8 :] = jnp.where(row[:EXT] == 3, 0.0, pltpu.roll(value[:EXT], 7, 1))

    def enter_ends(p, _):
        enter(p, [(before, (o, p)) for o in range(OWN)])
        enter(far + CHUNK + p, [(after, (o, p)) for o in range(OWN)])
        return 0

    lax.fori_loop(0, far, enter_ends, 0)

    def enter_slabs(p, _):
        for s in range(4):
            enter(far + 8 * s + p, [(slabs, (s, o, p)) for o in range(OWN)])
        return 0

    lax.fori_loop(0, 8, enter_slabs, 0)

    def enter_local(p, _):
        for j, (source, s) in enumerate(
            [(beyond, 2), (beyond, 3), (own, 0), (own, 1), (own, 2), (own, 3), (beyond, 0), (beyond, 1)]
        ):
            value = tiles([(source, (s, p)), (source, (s, p))])
            local[8 * j + p] = (value + (-1.5 * STENCIL[0] - CENTER)) * (1.0 / HALF)
        return 0

    lax.fori_loop(0, 8, enter_local, 0)

    def around(window, total):
        for k in range(1, 7):
            beside = window[WIDTH + k : WIDTH + 8 + k] + window[WIDTH - k : WIDTH + 8 - k]
            term = (-0.5 / HALF * STENCIL[k]) * beside
            total = term if total is None else total + term
        return total

    def along_zy(slot, source, index):
        high, low = split(source[pl.ds(index, 8), EXT : EXT + 8].reshape(8 * 64, NZ))
        both = jnp.dot(jnp.concatenate([high, low], axis=1), bands[...], preferred_element_type=F32)
        z = (both[:, :NZ] + both[:, NZ:]).reshape(8, 8, 8, NZ)
        for x in range(8):
            zy[slot, x] = around(source[index + x], z[x])

    def step(source, shift, first, blocks, put):
        def body(i, _):
            start = first + 8 * i
            for r in range(8):
                window = source[pl.ds(start + shift - WIDTH, 8 + 2 * WIDTH), EXT + r]
                total = local[pl.ds(start + 16, 8), r] * window[WIDTH : WIDTH + 8]
                put(start, r, around(window, total + zy[i, :, r]))
            along_zy(i + 1, source, first + 8 * jnp.minimum(i + 1, blocks - 1) + shift)
            return 0

        along_zy(0, source, first + shift)
        lax.fori_loop(0, blocks, body, 0)

    def put_first(start, r, total):
        store(other, start + near, r, total)

    def put_second(start, r, total):
        store(field, start + far, r, (total + total) - field[pl.ds(start + far, 8), EXT + r])

    def put_third(start, r, total):
        result[pl.ds(start, 8), r] = (total + total) - other[pl.ds(start + near, 8), EXT + r]

    def outside(target, shift, count):
        blank = jnp.zeros((count, 8 + 2 * EXT, 8, NZ), F32)

        @pl.when(chunk[0] == 0)
        def _():
            target[shift - count : shift] = blank

        @pl.when(chunk[0] == NX // CHUNK - 1)
        def _():
            target[shift + CHUNK : shift + CHUNK + count] = blank

    step(field, far, -12, 7, put_first)
    outside(other, near, 12)
    step(other, near, -8, 6, put_second)
    outside(field, far, 8)
    step(field, far, 0, 4, put_third)

    def turn(x, _):
        for b in range(2):
            pieces = [result[t * 8 + x, b * 4 + r] for t in range(4) for r in range(4)]
            turned[pl.ds((b * 8 + x) * NZ, NZ), :] = jnp.concatenate(pieces, axis=0).T
        return 0

    lax.fori_loop(0, 8, turn, 0)

    def pick(q, _):
        for c in range(4):
            for b in range(2):
                out[c, b, q] = turned[pl.ds(b * 8 * NZ + 4 * q + c, 8, stride=NZ), :]
        return 0

    lax.fori_loop(0, NZ // 4, pick, 0)


def rotate_kernel(ring, coefficients, out, gram):
    exact = functools.partial(
        lax.dot_general, precision=lax.Precision.HIGHEST, preferred_element_type=F32
    )
    row = lax.broadcasted_iota(jnp.int32, (256, 256), 0)
    column = lax.broadcasted_iota(jnp.int32, (256, 256), 1)
    number = lax.broadcasted_iota(jnp.int32, (256, 16), 0)
    entry = lax.broadcasted_iota(jnp.int32, (256, 16), 1)
    before = (number // 32 * 2 + number // 4 % 2 == entry).astype(F32)
    after = (number // 16 == entry).astype(F32)
    spread = exact(before, exact(coefficients[...], after, (((1,), (1,)), ((), ()))), (((1,), (0,)), ((), ())))
    same = (row // 8 % 4 == column % 4) & (row % 4 == column // 4 % 4)
    weights = jnp.where(same, spread, 0.0)

    lane = lax.broadcasted_iota(jnp.int32, (256, 128), 1) // 32
    sums = jnp.zeros((256, 256), F32)
    for t in range(4):
        halves = []
        for b in range(2):
            value = None
            for c in range(4):
                piece = ring[c * 2 + b]
                if c != t:
                    piece = pltpu.roll(piece, ((c - t) % 4) * 32, 1)
                value = piece if value is None else jnp.where(lane == c, piece, value)
            halves.append(value)
        all_orbitals = jnp.concatenate(halves, axis=1)
        turned = dot3(all_orbitals, weights, ((1,), (0,)))
        for b in range(2):
            out[:, b, t] = turned[:, b * 128 : (b + 1) * 128].reshape(32, 8, 128)
        sums = sums + dot3(all_orbitals, all_orbitals, ((0,), (0,)))
    diagonal = jnp.where((row // 8 % 4 == column // 8 % 4) & (row % 4 == column % 4), sums, 0.0)
    both = exact(before, exact(diagonal, before, (((1,), (0,)), ((), ()))), (((0,), (0,)), ((), ())))
    gram[...] = jnp.concatenate([both[0:8], both[8:16], jnp.zeros((8, 96), F32)], axis=1)


def lines_kernel(received, out):
    low = lax.broadcasted_iota(jnp.int32, (16, 8, 128), 1) < 4
    for s in range(8):
        first, second = (received[s * 4 : s * 4 + 4, b].reshape(128, 128).T.reshape(16, 8, 128) for b in range(2))
        even = jnp.where(low, first, pltpu.roll(second, 4, 1)).reshape(8, 2, 8, 128)
        odd = jnp.where(low, pltpu.roll(first, 4, 1), second).reshape(8, 2, 8, 128)
        for q in range(2):
            out[:, q * 16 : q * 16 + 8, s * 128 : (s + 1) * 128] = even[:, q]
            out[:, q * 16 + 8 : q * 16 + 16, s * 128 : (s + 1) * 128] = odd[:, q]


def call(kernel, out, scratch=()):
    vmem = pl.BlockSpec(memory_space=pltpu.VMEM)
    smem = pl.BlockSpec(memory_space=pltpu.SMEM)
    return lambda *args: pl.pallas_call(
        kernel,
        out_shape=[jax.ShapeDtypeStruct(s, F32) for s in out],
        in_specs=[smem if a.dtype == jnp.int32 else vmem for a in args],
        out_specs=[vmem] * len(out),
        scratch_shapes=[pltpu.VMEM(s, F32) for s in scratch],
        compiler_params=pltpu.CompilerParams(vmem_limit_bytes=48 * 1024 * 1024),
    )(*args)


def four(x, one, one_bit, two, two_bit):
    def swap(axes, bits):
        sizes = [lax.axis_size(a) for a in axes]
        flat = [np.ravel_multi_index([i ^ b for i, b in zip(at, bits)], sizes) for at in np.ndindex(*sizes)]
        return lax.ppermute(x, axes, [(i, int(j)) for i, j in enumerate(flat)])

    if one == two:
        parts = [swap((one,), (bits,)) for bits in (one_bit, two_bit, one_bit ^ two_bit)]
    else:
        parts = [swap((one, two), bits) for bits in ((one_bit, 0), (0, two_bit), (one_bit, two_bit))]
    return (x + parts[0]) + (parts[1] + parts[2])


def local(orbitals, potential, coefficients):
    chunks = ("z", "x")
    dom = ("z", "x", "u", "c")
    count = lax.axis_size(chunks)
    up = [(i, i + 1) for i in range(count - 1)]
    down = [(j, i) for i, j in up]

    shift = [(d, d + 4 if d % 4 >= 2 else d - 4) for d in range(4 * count)]
    beyond = lax.ppermute(potential, dom, [(i, j) for i, j in shift if 0 <= j < 4 * count])
    slabs = lax.all_to_all(orbitals.reshape(4, OWN, 8, NY, NZ), ("u", "c"), 0, 0, tiled=True)
    slabs, beyond = lax.optimization_barrier((slabs, beyond))
    far = 3 * WIDTH
    part = far - 16
    before = lax.ppermute(jnp.concatenate([slabs[1, :, 8 - part :], slabs[2], slabs[3]], axis=1), chunks, up)
    after = lax.ppermute(jnp.concatenate([slabs[0], slabs[1], slabs[2, :, :part]], axis=1), chunks, down)
    own = lax.all_gather(potential, ("u", "c"))
    beyond = lax.all_gather(beyond, ("u", "c"))

    scratch = [
        (CHUNK + 2 * far, 8 + 2 * EXT, 8, NZ),
        (CHUNK + 2 * (2 * WIDTH + 2), 8 + 2 * EXT, 8, NZ),
        (64, 8, 8, NZ),
        (8, 8, 8, 8, NZ),
        (CHUNK, 8, 8, NZ),
        (2 * 8 * NZ, NZ),
    ]
    bands = jnp.asarray(banded(1.0 / HALF))
    chunk = lax.axis_index(chunks).reshape(1)
    (message,) = call(filter_kernel, [(4, 2, 32, 8, 128)], scratch)(
        chunk, slabs, before, after, own, beyond, bands
    )
    ring = lax.all_to_all(message.reshape(8, 256, 128), ("u", "c", "b"), 0, 0, tiled=True)
    rotated, gram = call(rotate_kernel, [(32, 2, 4, 8, 128), (8, 128)])(ring, coefficients)
    gram = four(gram, "z", 4, "b", 1)
    gram, rotated = lax.optimization_barrier((gram, rotated))
    received = lax.all_to_all(rotated.reshape(64, 32, 128), ("z", "x", "b"), 0, 0, tiled=True)
    gram = lax.all_gather(gram, ("u", "c")).sum(axis=0)
    gram = four(gram, "x", 1, "x", 2)
    gram = four(gram, "z", 1, "z", 2)
    gram = gram / (NX * NY * NZ)
    intersection = jnp.concatenate([gram[:, :NORB], gram[:, NORB : 2 * NORB]], axis=0)
    (lines,) = call(lines_kernel, [(8, NY, NX)])(received.reshape(32, 2, 32, 128))
    return intersection, lines


def solution(mesh):
    grid = Mesh(mesh.devices.reshape(8, 4, 2, 2, 2), ("z", "x", "u", "c", "b"))
    dom = ("z", "x", "u", "c")
    return jax.shard_map(
        local,
        mesh=grid,
        in_specs=(P("b", dom, None, None), P(dom, None, None), P()),
        out_specs=(P(), P("b", dom, None)),
        check_vma=False,
    )
```

```python
import functools

import jax
import jax.numpy as jnp
import ml_dtypes
import numpy as np
from jax import lax
from jax.experimental import pallas as pl
from jax.experimental.pallas import tpu as pltpu
from jax.sharding import Mesh
from jax.sharding import PartitionSpec as P

STENCIL = (
    -5369.0 / 1800.0,
    12.0 / 7.0,
    -15.0 / 56.0,
    10.0 / 189.0,
    -1.0 / 112.0,
    2.0 / 1925.0,
    -1.0 / 16632.0,
)
CENTER = 8.5
HALF = 6.5
WIDTH = 6
EXT = 6
NORB, NX, NY, NZ = 16, 1024, 32, 128
CHUNK = 32
OWN = 2
F32 = jnp.float32
BF16 = jnp.bfloat16


def banded(scale):
    band = np.zeros((NZ, NZ), np.float64)
    for k in range(1, 7):
        band += np.eye(NZ, k=k) * STENCIL[k] + np.eye(NZ, k=-k) * STENCIL[k]
    band = (-0.5 * scale * band).astype(np.float32)
    high = band.astype(ml_dtypes.bfloat16)
    low = (band - high.astype(np.float32)).astype(ml_dtypes.bfloat16)
    zero = np.zeros_like(high)
    return np.block([[high, low], [high, zero]]).astype(ml_dtypes.bfloat16)


def split(x):
    high = x.astype(BF16)
    low = (x - high.astype(F32)).astype(BF16)
    return high, low


def dot3(a, b, dims):
    ah, al = split(a)
    bh, bl = split(b)
    dot = functools.partial(lax.dot_general, dimension_numbers=(dims, ((), ())), preferred_element_type=F32)
    return dot(ah, bh) + (dot(ah, bl) + dot(al, bh))


def filter_kernel(
    chunk, slabs, before, after, own, beyond, bands, out, field, other, local, z, result, turned
):
    far, near = 3 * WIDTH, 2 * WIDTH + 2
    row = lax.broadcasted_iota(jnp.int32, (8, 8, NZ), 1) % 4

    def store(target, plane, r, value):
        planes = pl.ds(plane, 8)
        target[planes, EXT + r] = value
        if r >= 8 - EXT:
            target[planes, r - (8 - EXT)] = jnp.where(row == 0, 0.0, pltpu.roll(value, 1, 1))
        if r < EXT:
            target[planes, EXT + 8 + r] = jnp.where(row == 3, 0.0, pltpu.roll(value, 7, 1))

    def tiles(sources):
        rows = [jnp.concatenate([source[(*at, pl.ds(r, 4, stride=8), slice(None))] for source, at in sources], axis=0) for r in range(8)]
        return jnp.stack(rows)

    def enter(plane, sources):
        value = tiles(sources)
        field[plane, EXT : EXT + 8] = value
        field[plane, 0:EXT] = jnp.where(row[:EXT] == 0, 0.0, pltpu.roll(value[8 - EXT :], 1, 1))
        field[plane, EXT + 8 :] = jnp.where(row[:EXT] == 3, 0.0, pltpu.roll(value[:EXT], 7, 1))

    def enter_ends(p, _):
        enter(p, [(before, (o, p)) for o in range(OWN)])
        enter(far + CHUNK + p, [(after, (o, p)) for o in range(OWN)])
        return 0

    lax.fori_loop(0, far, enter_ends, 0)

    def enter_slabs(p, _):
        for s in range(4):
            enter(far + 8 * s + p, [(slabs, (s, o, p)) for o in range(OWN)])
        return 0

    lax.fori_loop(0, 8, enter_slabs, 0)

    def enter_local(p, _):
        for j, (source, s) in enumerate(
            [(beyond, 2), (beyond, 3), (own, 0), (own, 1), (own, 2), (own, 3), (beyond, 0), (beyond, 1)]
        ):
            value = tiles([(source, (s, p)), (source, (s, p))])
            local[8 * j + p] = (value + (-1.5 * STENCIL[0] - CENTER)) * (1.0 / HALF)
        return 0

    lax.fori_loop(0, 8, enter_local, 0)

    def along_z(source, index):
        high, low = split(source[pl.ds(index, 4), EXT : EXT + 8].reshape(4 * 64, NZ))
        both = jnp.dot(jnp.concatenate([high, low], axis=1), bands[...], preferred_element_type=F32)
        return (both[:, :NZ] + both[:, NZ:]).reshape(4, 8, 8, NZ)

    def step(source, shift, first, blocks, put):
        def body(i, _):
            start = first + 8 * i
            later = first + 8 * jnp.minimum(i + 1, blocks - 1) + shift
            for half in range(2):
                ahead = along_z(source, later + 4 * half)
                for r in range(4 * half, 4 * half + 4):
                    window = source[pl.ds(start + shift - WIDTH, 8 + 2 * WIDTH), EXT + r]
                    total = local[pl.ds(start + 16, 8), r] * window[WIDTH : WIDTH + 8] + z[i, :, r]
                    for k in range(1, 7):
                        beside = window[WIDTH + k : WIDTH + 8 + k] + window[WIDTH - k : WIDTH + 8 - k]
                        planes = pl.ds(start + shift, 8)
                        beside = beside + (source[planes, EXT + r + k] + source[planes, EXT + r - k])
                        total = total + (-0.5 / HALF * STENCIL[k]) * beside
                    put(start, r, total)
                z[i + 1, 4 * half : 4 * half + 4] = ahead
            return 0

        for half in range(2):
            z[0, 4 * half : 4 * half + 4] = along_z(source, first + shift + 4 * half)
        lax.fori_loop(0, blocks, body, 0)

    def put_first(start, r, total):
        store(other, start + near, r, total)

    def put_second(start, r, total):
        store(field, start + far, r, (total + total) - field[pl.ds(start + far, 8), EXT + r])

    def put_third(start, r, total):
        result[pl.ds(start, 8), r] = (total + total) - other[pl.ds(start + near, 8), EXT + r]

    def outside(target, shift, count):
        blank = jnp.zeros((count, 8 + 2 * EXT, 8, NZ), F32)

        @pl.when(chunk[0] == 0)
        def _():
            target[shift - count : shift] = blank

        @pl.when(chunk[0] == NX // CHUNK - 1)
        def _():
            target[shift + CHUNK : shift + CHUNK + count] = blank

    step(field, far, -12, 7, put_first)
    outside(other, near, 12)
    step(other, near, -8, 6, put_second)
    outside(field, far, 8)
    step(field, far, 0, 4, put_third)

    def turn(x, _):
        for b in range(2):
            pieces = [result[t * 8 + x, b * 4 + r] for t in range(4) for r in range(4)]
            turned[pl.ds((b * 8 + x) * NZ, NZ), :] = jnp.concatenate(pieces, axis=0).T
        return 0

    lax.fori_loop(0, 8, turn, 0)

    def pick(q, _):
        for c in range(4):
            for b in range(2):
                out[c, b, q] = turned[pl.ds(b * 8 * NZ + 4 * q + c, 8, stride=NZ), :]
        return 0

    lax.fori_loop(0, NZ // 4, pick, 0)


def rotate_kernel(ring, coefficients, out, gram):
    exact = functools.partial(
        lax.dot_general, precision=lax.Precision.HIGHEST, preferred_element_type=F32
    )
    row = lax.broadcasted_iota(jnp.int32, (256, 256), 0)
    column = lax.broadcasted_iota(jnp.int32, (256, 256), 1)
    number = lax.broadcasted_iota(jnp.int32, (256, 16), 0)
    entry = lax.broadcasted_iota(jnp.int32, (256, 16), 1)
    before = (number // 32 * 2 + number // 4 % 2 == entry).astype(F32)
    after = (number // 16 == entry).astype(F32)
    spread = exact(before, exact(coefficients[...], after, (((1,), (1,)), ((), ()))), (((1,), (0,)), ((), ())))
    same = (row // 8 % 4 == column % 4) & (row % 4 == column // 4 % 4)
    weights = jnp.where(same, spread, 0.0)

    lane = lax.broadcasted_iota(jnp.int32, (256, 128), 1) // 32
    sums = jnp.zeros((256, 256), F32)
    for t in range(4):
        halves = []
        for b in range(2):
            value = None
            for c in range(4):
                piece = ring[c * 2 + b]
                if c != t:
                    piece = pltpu.roll(piece, ((c - t) % 4) * 32, 1)
                value = piece if value is None else jnp.where(lane == c, piece, value)
            halves.append(value)
        all_orbitals = jnp.concatenate(halves, axis=1)
        turned = dot3(all_orbitals, weights, ((1,), (0,)))
        for b in range(2):
            out[:, b, t] = turned[:, b * 128 : (b + 1) * 128].reshape(32, 8, 128)
        sums = sums + dot3(all_orbitals, all_orbitals, ((0,), (0,)))
    diagonal = jnp.where((row // 8 % 4 == column // 8 % 4) & (row % 4 == column % 4), sums, 0.0)
    both = exact(before, exact(diagonal, before, (((1,), (0,)), ((), ()))), (((0,), (0,)), ((), ())))
    gram[...] = jnp.concatenate([both[0:8], both[8:16], jnp.zeros((8, 96), F32)], axis=1)


def lines_kernel(received, out):
    low = lax.broadcasted_iota(jnp.int32, (16, 8, 128), 1) < 4
    for s in range(8):
        first, second = (received[s * 4 : s * 4 + 4, b].reshape(128, 128).T.reshape(16, 8, 128) for b in range(2))
        even = jnp.where(low, first, pltpu.roll(second, 4, 1)).reshape(8, 2, 8, 128)
        odd = jnp.where(low, pltpu.roll(first, 4, 1), second).reshape(8, 2, 8, 128)
        for q in range(2):
            out[:, q * 16 : q * 16 + 8, s * 128 : (s + 1) * 128] = even[:, q]
            out[:, q * 16 + 8 : q * 16 + 16, s * 128 : (s + 1) * 128] = odd[:, q]


def call(kernel, out, scratch=()):
    vmem = pl.BlockSpec(memory_space=pltpu.VMEM)
    smem = pl.BlockSpec(memory_space=pltpu.SMEM)
    return lambda *args: pl.pallas_call(
        kernel,
        out_shape=[jax.ShapeDtypeStruct(s, F32) for s in out],
        in_specs=[smem if a.dtype == jnp.int32 else vmem for a in args],
        out_specs=[vmem] * len(out),
        scratch_shapes=[pltpu.VMEM(s, F32) for s in scratch],
        compiler_params=pltpu.CompilerParams(vmem_limit_bytes=48 * 1024 * 1024),
    )(*args)


def four(x, one, one_bit, two, two_bit):
    def swap(axes, bits):
        sizes = [lax.axis_size(a) for a in axes]
        flat = [np.ravel_multi_index([i ^ b for i, b in zip(at, bits)], sizes) for at in np.ndindex(*sizes)]
        return lax.ppermute(x, axes, [(i, int(j)) for i, j in enumerate(flat)])

    if one == two:
        parts = [swap((one,), (bits,)) for bits in (one_bit, two_bit, one_bit ^ two_bit)]
    else:
        parts = [swap((one, two), bits) for bits in ((one_bit, 0), (0, two_bit), (one_bit, two_bit))]
    return (x + parts[0]) + (parts[1] + parts[2])


def local(orbitals, potential, coefficients):
    chunks = ("z", "x")
    dom = ("z", "x", "u", "c")
    count = lax.axis_size(chunks)
    up = [(i, i + 1) for i in range(count - 1)]
    down = [(j, i) for i, j in up]

    shift = [(d, d + 4 if d % 4 >= 2 else d - 4) for d in range(4 * count)]
    beyond = lax.ppermute(potential, dom, [(i, j) for i, j in shift if 0 <= j < 4 * count])
    slabs = lax.all_to_all(orbitals.reshape(4, OWN, 8, NY, NZ), ("u", "c"), 0, 0, tiled=True)
    slabs, beyond = lax.optimization_barrier((slabs, beyond))
    far = 3 * WIDTH
    part = far - 16
    before = lax.ppermute(jnp.concatenate([slabs[1, :, 8 - part :], slabs[2], slabs[3]], axis=1), chunks, up)
    after = lax.ppermute(jnp.concatenate([slabs[0], slabs[1], slabs[2, :, :part]], axis=1), chunks, down)
    own = lax.all_gather(potential, ("u", "c"))
    beyond = lax.all_gather(beyond, ("u", "c"))

    scratch = [
        (CHUNK + 2 * far, 8 + 2 * EXT, 8, NZ),
        (CHUNK + 2 * (2 * WIDTH + 2), 8 + 2 * EXT, 8, NZ),
        (64, 8, 8, NZ),
        (8, 8, 8, 8, NZ),
        (CHUNK, 8, 8, NZ),
        (2 * 8 * NZ, NZ),
    ]
    bands = jnp.asarray(banded(1.0 / HALF))
    chunk = lax.axis_index(chunks).reshape(1)
    (message,) = call(filter_kernel, [(4, 2, 32, 8, 128)], scratch)(
        chunk, slabs, before, after, own, beyond, bands
    )
    ring = lax.all_to_all(message.reshape(8, 256, 128), ("u", "c", "b"), 0, 0, tiled=True)
    rotated, gram = call(rotate_kernel, [(32, 2, 4, 8, 128), (8, 128)])(ring, coefficients)
    gram = lax.all_gather(gram, ("u", "c")).sum(axis=0)
    gram, rotated = lax.optimization_barrier((gram, rotated))
    received = lax.all_to_all(rotated.reshape(64, 32, 128), ("z", "x", "b"), 0, 0, tiled=True)
    gram = four(gram, "x", 1, "x", 2)
    for axis, bit in (("z", 1), ("z", 2), ("b", 1), ("z", 4)):
        gram = gram + lax.ppermute(gram, axis, [(i, i ^ bit) for i in range(lax.axis_size(axis))])
    gram = gram / (NX * NY * NZ)
    intersection = jnp.concatenate([gram[:, :NORB], gram[:, NORB : 2 * NORB]], axis=0)
    (lines,) = call(lines_kernel, [(8, NY, NX)])(received.reshape(32, 2, 32, 128))
    return intersection, lines


def solution(mesh):
    grid = Mesh(mesh.devices.reshape(8, 4, 2, 2, 2), ("z", "x", "u", "c", "b"))
    dom = ("z", "x", "u", "c")
    return jax.shard_map(
        local,
        mesh=grid,
        in_specs=(P("b", dom, None, None), P(dom, None, None), P()),
        out_specs=(P(), P("b", dom, None)),
        check_vma=False,
    )
```

```python
import functools

import jax
import jax.numpy as jnp
import ml_dtypes
import numpy as np
from jax import lax
from jax.experimental import pallas as pl
from jax.experimental.pallas import tpu as pltpu
from jax.sharding import Mesh
from jax.sharding import PartitionSpec as P

STENCIL = (
    -5369.0 / 1800.0,
    12.0 / 7.0,
    -15.0 / 56.0,
    10.0 / 189.0,
    -1.0 / 112.0,
    2.0 / 1925.0,
    -1.0 / 16632.0,
)
CENTER = 8.5
HALF = 6.5
WIDTH = 6
EXT = 6
NORB, NX, NY, NZ = 16, 1024, 32, 128
CHUNK = 32
OWN = 2
F32 = jnp.float32
BF16 = jnp.bfloat16


def banded(scale):
    band = np.zeros((NZ, NZ), np.float64)
    for k in range(1, 7):
        band += np.eye(NZ, k=k) * STENCIL[k] + np.eye(NZ, k=-k) * STENCIL[k]
    band = (-0.5 * scale * band).astype(np.float32)
    high = band.astype(ml_dtypes.bfloat16)
    low = (band - high.astype(np.float32)).astype(ml_dtypes.bfloat16)
    zero = np.zeros_like(high)
    return np.block([[high, low], [high, zero]]).astype(ml_dtypes.bfloat16)


def split(x):
    high = x.astype(BF16)
    low = (x - high.astype(F32)).astype(BF16)
    return high, low


def dot3(a, b, dims):
    ah, al = split(a)
    bh, bl = split(b)
    dot = functools.partial(lax.dot_general, dimension_numbers=(dims, ((), ())), preferred_element_type=F32)
    return dot(ah, bh) + (dot(ah, bl) + dot(al, bh))


def filter_kernel(
    chunk, slabs, before, after, own, beyond, bands, out, field, other, local, z, result, turned
):
    far, near = 3 * WIDTH, 2 * WIDTH + 2
    row = lax.broadcasted_iota(jnp.int32, (8, 8, NZ), 1) % 4

    def store(target, plane, r, value):
        planes = pl.ds(plane, 8)
        target[planes, EXT + r] = value
        if r >= 8 - EXT:
            target[planes, r - (8 - EXT)] = jnp.where(row == 0, 0.0, pltpu.roll(value, 1, 1))
        if r < EXT:
            target[planes, EXT + 8 + r] = jnp.where(row == 3, 0.0, pltpu.roll(value, 7, 1))

    def tiles(sources):
        rows = [jnp.concatenate([source[(*at, pl.ds(r, 4, stride=8), slice(None))] for source, at in sources], axis=0) for r in range(8)]
        return jnp.stack(rows)

    def enter(plane, sources):
        value = tiles(sources)
        field[plane, EXT : EXT + 8] = value
        field[plane, 0:EXT] = jnp.where(row[:EXT] == 0, 0.0, pltpu.roll(value[8 - EXT :], 1, 1))
        field[plane, EXT + 8 :] = jnp.where(row[:EXT] == 3, 0.0, pltpu.roll(value[:EXT], 7, 1))

    def enter_ends(p, _):
        enter(p, [(before, (o, p)) for o in range(OWN)])
        enter(far + CHUNK + p, [(after, (o, p)) for o in range(OWN)])
        return 0

    lax.fori_loop(0, far, enter_ends, 0)

    def enter_slabs(p, _):
        for s in range(4):
            enter(far + 8 * s + p, [(slabs, (s, o, p)) for o in range(OWN)])
        return 0

    lax.fori_loop(0, 8, enter_slabs, 0)

    def enter_local(p, _):
        for j, (source, s) in enumerate(
            [(beyond, 2), (beyond, 3), (own, 0), (own, 1), (own, 2), (own, 3), (beyond, 0), (beyond, 1)]
        ):
            value = tiles([(source, (s, p)), (source, (s, p))])
            local[8 * j + p] = (value + (-1.5 * STENCIL[0] - CENTER)) * (1.0 / HALF)
        return 0

    lax.fori_loop(0, 8, enter_local, 0)

    def along_z(source, index):
        high, low = split(source[pl.ds(index, 4), EXT : EXT + 8].reshape(4 * 64, NZ))
        both = jnp.dot(jnp.concatenate([high, low], axis=1), bands[...], preferred_element_type=F32)
        return (both[:, :NZ] + both[:, NZ:]).reshape(4, 8, 8, NZ)

    def step(source, shift, first, blocks, put):
        def body(i, _):
            start = first + 8 * i
            later = first + 8 * jnp.minimum(i + 1, blocks - 1) + shift
            for half in range(2):
                ahead = along_z(source, later + 4 * half)
                for r in range(4 * half, 4 * half + 4):
                    window = source[pl.ds(start + shift - WIDTH, 8 + 2 * WIDTH), EXT + r]
                    total = local[pl.ds(start + 16, 8), r] * window[WIDTH : WIDTH + 8] + z[i, :, r]
                    for k in range(1, 7):
                        beside = window[WIDTH + k : WIDTH + 8 + k] + window[WIDTH - k : WIDTH + 8 - k]
                        planes = pl.ds(start + shift, 8)
                        beside = beside + (source[planes, EXT + r + k] + source[planes, EXT + r - k])
                        total = total + (-0.5 / HALF * STENCIL[k]) * beside
                    put(start, r, total)
                z[i + 1, 4 * half : 4 * half + 4] = ahead
            return 0

        for half in range(2):
            z[0, 4 * half : 4 * half + 4] = along_z(source, first + shift + 4 * half)
        lax.fori_loop(0, blocks, body, 0)

    def put_first(start, r, total):
        store(other, start + near, r, total)

    def put_second(start, r, total):
        store(field, start + far, r, (total + total) - field[pl.ds(start + far, 8), EXT + r])

    def put_third(start, r, total):
        result[pl.ds(start, 8), r] = (total + total) - other[pl.ds(start + near, 8), EXT + r]

    def outside(target, shift, count):
        blank = jnp.zeros((count, 8 + 2 * EXT, 8, NZ), F32)

        @pl.when(chunk[0] == 0)
        def _():
            target[shift - count : shift] = blank

        @pl.when(chunk[0] == NX // CHUNK - 1)
        def _():
            target[shift + CHUNK : shift + CHUNK + count] = blank

    step(field, far, -12, 7, put_first)
    outside(other, near, 12)
    step(other, near, -8, 6, put_second)
    outside(field, far, 8)
    step(field, far, 0, 4, put_third)

    def turn(x, _):
        for b in range(2):
            pieces = [result[t * 8 + x, b * 4 + r] for t in range(4) for r in range(4)]
            turned[pl.ds((b * 8 + x) * NZ, NZ), :] = jnp.concatenate(pieces, axis=0).T
        return 0

    lax.fori_loop(0, 8, turn, 0)

    def pick(q, _):
        for c in range(4):
            for b in range(2):
                out[c, b, q] = turned[pl.ds(b * 8 * NZ + 4 * q + c, 8, stride=NZ), :]
        return 0

    lax.fori_loop(0, NZ // 4, pick, 0)


def rotate_kernel(ring, coefficients, out):
    exact = functools.partial(
        lax.dot_general, precision=lax.Precision.HIGHEST, preferred_element_type=F32
    )
    row = lax.broadcasted_iota(jnp.int32, (256, 256), 0)
    column = lax.broadcasted_iota(jnp.int32, (256, 256), 1)
    number = lax.broadcasted_iota(jnp.int32, (256, 16), 0)
    entry = lax.broadcasted_iota(jnp.int32, (256, 16), 1)
    before = (number // 32 * 2 + number // 4 % 2 == entry).astype(F32)
    after = (number // 16 == entry).astype(F32)
    spread = exact(before, exact(coefficients[...], after, (((1,), (1,)), ((), ()))), (((1,), (0,)), ((), ())))
    same = (row // 8 % 4 == column % 4) & (row % 4 == column // 4 % 4)
    weights = jnp.where(same, spread, 0.0)

    lane = lax.broadcasted_iota(jnp.int32, (256, 128), 1) // 32
    sums = jnp.zeros((256, 256), F32)
    for t in range(4):
        halves = []
        for b in range(2):
            value = None
            for c in range(4):
                piece = ring[c * 2 + b]
                if c != t:
                    piece = pltpu.roll(piece, ((c - t) % 4) * 32, 1)
                value = piece if value is None else jnp.where(lane == c, piece, value)
            halves.append(value)
        all_orbitals = jnp.concatenate(halves, axis=1)
        turned = dot3(all_orbitals, weights, ((1,), (0,)))
        for b in range(2):
            rows = turned[:, b * 128 : (b + 1) * 128].reshape(32, 8, 128)
            out[:, b, 2 * t] = rows[:, 0:4]
            out[:, b, 2 * t + 1] = rows[:, 4:8]
        sums = sums + dot3(all_orbitals, all_orbitals, ((0,), (0,)))
    diagonal = jnp.where((row // 8 % 4 == column // 8 % 4) & (row % 4 == column % 4), sums, 0.0)
    both = exact(before, exact(diagonal, before, (((1,), (0,)), ((), ()))), (((0,), (0,)), ((), ())))
    tile = jnp.concatenate([both[4 * q : 4 * q + 4] for q in range(4)] + [jnp.zeros((4, 64), F32)], axis=1)
    out[:, :, 8] = jnp.broadcast_to(tile, (32, 2, 4, 128))


def lines_kernel(received, out):
    low = lax.broadcasted_iota(jnp.int32, (16, 8, 128), 1) < 4

    def lines(s, b):
        pieces = [
            jnp.concatenate([received[s * 4 + c, b, 2 * j], received[s * 4 + c, b, 2 * j + 1]], axis=0)
            for c in range(4)
            for j in range(4)
        ]
        return jnp.concatenate(pieces, axis=0).T.reshape(16, 8, 128)

    for s in range(8):
        first, second = lines(s, 0), lines(s, 1)
        even = jnp.where(low, first, pltpu.roll(second, 4, 1)).reshape(8, 2, 8, 128)
        odd = jnp.where(low, pltpu.roll(first, 4, 1), second).reshape(8, 2, 8, 128)
        for q in range(2):
            out[:, q * 16 : q * 16 + 8, s * 128 : (s + 1) * 128] = even[:, q]
            out[:, q * 16 + 8 : q * 16 + 16, s * 128 : (s + 1) * 128] = odd[:, q]


def call(kernel, out, scratch=()):
    vmem = pl.BlockSpec(memory_space=pltpu.VMEM)
    smem = pl.BlockSpec(memory_space=pltpu.SMEM)
    return lambda *args: pl.pallas_call(
        kernel,
        out_shape=[jax.ShapeDtypeStruct(s, F32) for s in out],
        in_specs=[smem if a.dtype == jnp.int32 else vmem for a in args],
        out_specs=[vmem] * len(out),
        scratch_shapes=[pltpu.VMEM(s, F32) for s in scratch],
        compiler_params=pltpu.CompilerParams(vmem_limit_bytes=48 * 1024 * 1024),
    )(*args)


def four(x, one, one_bit, two, two_bit):
    def swap(axes, bits):
        sizes = [lax.axis_size(a) for a in axes]
        flat = [np.ravel_multi_index([i ^ b for i, b in zip(at, bits)], sizes) for at in np.ndindex(*sizes)]
        return lax.ppermute(x, axes, [(i, int(j)) for i, j in enumerate(flat)])

    if one == two:
        parts = [swap((one,), (bits,)) for bits in (one_bit, two_bit, one_bit ^ two_bit)]
    else:
        parts = [swap((one, two), bits) for bits in ((one_bit, 0), (0, two_bit), (one_bit, two_bit))]
    return (x + parts[0]) + (parts[1] + parts[2])


def local(orbitals, potential, coefficients):
    chunks = ("z", "x")
    dom = ("z", "x", "u", "c")
    count = lax.axis_size(chunks)
    up = [(i, i + 1) for i in range(count - 1)]
    down = [(j, i) for i, j in up]

    shift = [(d, d + 4 if d % 4 >= 2 else d - 4) for d in range(4 * count)]
    beyond = lax.ppermute(potential, dom, [(i, j) for i, j in shift if 0 <= j < 4 * count])
    slabs = lax.all_to_all(orbitals.reshape(4, OWN, 8, NY, NZ), ("u", "c"), 0, 0, tiled=True)
    slabs, beyond = lax.optimization_barrier((slabs, beyond))
    far = 3 * WIDTH
    part = far - 16
    before = lax.ppermute(jnp.concatenate([slabs[1, :, 8 - part :], slabs[2], slabs[3]], axis=1), chunks, up)
    after = lax.ppermute(jnp.concatenate([slabs[0], slabs[1], slabs[2, :, :part]], axis=1), chunks, down)
    own = lax.all_gather(potential, ("u", "c"))
    beyond = lax.all_gather(beyond, ("u", "c"))

    scratch = [
        (CHUNK + 2 * far, 8 + 2 * EXT, 8, NZ),
        (CHUNK + 2 * (2 * WIDTH + 2), 8 + 2 * EXT, 8, NZ),
        (64, 8, 8, NZ),
        (8, 8, 8, 8, NZ),
        (CHUNK, 8, 8, NZ),
        (2 * 8 * NZ, NZ),
    ]
    bands = jnp.asarray(banded(1.0 / HALF))
    chunk = lax.axis_index(chunks).reshape(1)
    (message,) = call(filter_kernel, [(4, 2, 32, 8, 128)], scratch)(
        chunk, slabs, before, after, own, beyond, bands
    )
    ring = lax.all_to_all(message.reshape(8, 256, 128), ("u", "c", "b"), 0, 0, tiled=True)
    (rotated,) = call(rotate_kernel, [(32, 2, 9, 4, 128)])(ring, coefficients)
    received = lax.all_to_all(rotated.reshape(64, 9, 4, 128), ("z", "x", "b"), 0, 0, tiled=True)
    gram = four(received[:, 8].sum(axis=0), "u", 1, "c", 1) / (NX * NY * NZ)
    intersection = jnp.concatenate([gram[:, q * NORB : (q + 1) * NORB] for q in range(4)], axis=0)
    (lines,) = call(lines_kernel, [(8, NY, NX)])(received.reshape(32, 2, 9, 4, 128))
    return intersection, lines


def solution(mesh):
    grid = Mesh(mesh.devices.reshape(8, 4, 2, 2, 2), ("z", "x", "u", "c", "b"))
    dom = ("z", "x", "u", "c")
    return jax.shard_map(
        local,
        mesh=grid,
        in_specs=(P("b", dom, None, None), P(dom, None, None), P()),
        out_specs=(P(), P("b", dom, None)),
        check_vma=False,
    )
```

```python
import functools

import jax
import jax.numpy as jnp
import ml_dtypes
import numpy as np
from jax import lax
from jax.experimental import pallas as pl
from jax.experimental.pallas import tpu as pltpu
from jax.sharding import Mesh
from jax.sharding import PartitionSpec as P

STENCIL = (
    -5369.0 / 1800.0,
    12.0 / 7.0,
    -15.0 / 56.0,
    10.0 / 189.0,
    -1.0 / 112.0,
    2.0 / 1925.0,
    -1.0 / 16632.0,
)
CENTER = 8.5
HALF = 6.5
WIDTH = 6
EXT = 6
NORB, NX, NY, NZ = 16, 1024, 32, 128
CHUNK = 32
OWN = 2
F32 = jnp.float32
BF16 = jnp.bfloat16


def banded(scale):
    band = np.zeros((NZ, NZ), np.float64)
    for k in range(1, 7):
        band += np.eye(NZ, k=k) * STENCIL[k] + np.eye(NZ, k=-k) * STENCIL[k]
    band = (-0.5 * scale * band).astype(np.float32)
    high = band.astype(ml_dtypes.bfloat16)
    low = (band - high.astype(np.float32)).astype(ml_dtypes.bfloat16)
    zero = np.zeros_like(high)
    return np.block([[high, low], [high, zero]]).astype(ml_dtypes.bfloat16)


def split(x):
    high = x.astype(BF16)
    low = (x - high.astype(F32)).astype(BF16)
    return high, low


def filter_kernel(
    chunk, slabs, ahead, behind, own, beyond, bands, out, field, other, local, z, result, turned
):
    far, near = 3 * WIDTH, 2 * WIDTH + 2
    row = lax.broadcasted_iota(jnp.int32, (8, 8, NZ), 1) % 4

    def store(target, plane, r, value):
        planes = pl.ds(plane, 8)
        target[planes, EXT + r] = value
        if r >= 8 - EXT:
            target[planes, r - (8 - EXT)] = jnp.where(row == 0, 0.0, pltpu.roll(value, 1, 1))
        if r < EXT:
            target[planes, EXT + 8 + r] = jnp.where(row == 3, 0.0, pltpu.roll(value, 7, 1))

    def tiles(sources):
        rows = [jnp.concatenate([source[(*at, pl.ds(r, 4, stride=8), slice(None))] for source, at in sources], axis=0) for r in range(8)]
        return jnp.stack(rows)

    def enter(plane, sources):
        value = tiles(sources)
        field[plane, EXT : EXT + 8] = value
        field[plane, 0:EXT] = jnp.where(row[:EXT] == 0, 0.0, pltpu.roll(value[8 - EXT :], 1, 1))
        field[plane, EXT + 8 :] = jnp.where(row[:EXT] == 3, 0.0, pltpu.roll(value[:EXT], 7, 1))

    odd = chunk[0] % 2

    def enter_ends(p, _):
        enter(odd * (far + CHUNK) + p, [(ahead, (o, p)) for o in range(OWN)])
        enter((1 - odd) * (far + CHUNK) + p, [(behind, (o, p)) for o in range(OWN)])
        return 0

    lax.fori_loop(0, far, enter_ends, 0)

    def enter_slabs(p, _):
        for s in range(4):
            enter(far + 8 * s + p, [(slabs, (s, o, p)) for o in range(OWN)])
        return 0

    lax.fori_loop(0, 8, enter_slabs, 0)

    def enter_local(p, _):
        for j, (source, s) in enumerate(
            [(beyond, 2), (beyond, 3), (own, 0), (own, 1), (own, 2), (own, 3), (beyond, 0), (beyond, 1)]
        ):
            value = tiles([(source, (s, p)), (source, (s, p))])
            local[8 * j + p] = (value + (-1.5 * STENCIL[0] - CENTER)) * (1.0 / HALF)
        return 0

    lax.fori_loop(0, 8, enter_local, 0)

    def along_z(source, index):
        high, low = split(source[pl.ds(index, 4), EXT : EXT + 8].reshape(4 * 64, NZ))
        both = jnp.dot(jnp.concatenate([high, low], axis=1), bands[...], preferred_element_type=F32)
        return (both[:, :NZ] + both[:, NZ:]).reshape(4, 8, 8, NZ)

    def step(source, shift, first, blocks, put):
        def body(i, _):
            start = first + 8 * i
            later = first + 8 * jnp.minimum(i + 1, blocks - 1) + shift
            for half in range(2):
                ahead = along_z(source, later + 4 * half)
                for r in range(4 * half, 4 * half + 4):
                    window = source[pl.ds(start + shift - WIDTH, 8 + 2 * WIDTH), EXT + r]
                    total = local[pl.ds(start + 16, 8), r] * window[WIDTH : WIDTH + 8] + z[i, :, r]
                    for k in range(1, 7):
                        beside = window[WIDTH + k : WIDTH + 8 + k] + window[WIDTH - k : WIDTH + 8 - k]
                        planes = pl.ds(start + shift, 8)
                        beside = beside + (source[planes, EXT + r + k] + source[planes, EXT + r - k])
                        total = total + (-0.5 / HALF * STENCIL[k]) * beside
                    put(start, r, total)
                z[i + 1, 4 * half : 4 * half + 4] = ahead
            return 0

        for half in range(2):
            z[0, 4 * half : 4 * half + 4] = along_z(source, first + shift + 4 * half)
        lax.fori_loop(0, blocks, body, 0)

    def put_first(start, r, total):
        store(other, start + near, r, total)

    def put_second(start, r, total):
        store(field, start + far, r, (total + total) - field[pl.ds(start + far, 8), EXT + r])

    def put_third(start, r, total):
        result[pl.ds(start, 8), r] = (total + total) - other[pl.ds(start + near, 8), EXT + r]

    def outside(target, shift, count):
        blank = jnp.zeros((count, 8 + 2 * EXT, 8, NZ), F32)

        @pl.when(chunk[0] == 0)
        def _():
            target[shift - count : shift] = blank

        @pl.when(chunk[0] == NX // CHUNK - 1)
        def _():
            target[shift + CHUNK : shift + CHUNK + count] = blank

    step(field, far, -12, 7, put_first)
    outside(other, near, 12)
    step(other, near, -8, 6, put_second)
    outside(field, far, 8)
    step(field, far, 0, 4, put_third)

    def turn(x, _):
        for b in range(2):
            pieces = [result[t * 8 + x, b * 4 + r] for t in range(4) for r in range(4)]
            turned[pl.ds((b * 8 + x) * NZ, NZ), :] = jnp.concatenate(pieces, axis=0).T
        return 0

    lax.fori_loop(0, 8, turn, 0)

    def pick(q, _):
        for c in range(4):
            for b in range(2):
                out[c, b, q] = turned[pl.ds(b * 8 * NZ + 4 * q + c, 8, stride=NZ), :]
        return 0

    lax.fori_loop(0, NZ // 4, pick, 0)


exact = functools.partial(lax.dot_general, precision=lax.Precision.HIGHEST, preferred_element_type=F32)


def weights_kernel(coefficients, out):
    row = lax.broadcasted_iota(jnp.int32, (256, 256), 0)
    column = lax.broadcasted_iota(jnp.int32, (256, 256), 1)
    number = lax.broadcasted_iota(jnp.int32, (256, 16), 0)
    entry = lax.broadcasted_iota(jnp.int32, (256, 16), 1)
    before = (number // 32 * 2 + number // 4 % 2 == entry).astype(F32)
    after = (number // 16 == entry).astype(F32)
    spread = exact(before, exact(coefficients[...], after, (((1,), (1,)), ((), ()))), (((1,), (0,)), ((), ())))
    same = (row // 8 % 4 == column % 4) & (row % 4 == column // 4 % 4)
    out[...] = jnp.where(same, spread, 0.0)


def rotate_kernel(ring, weights, out):
    lane = lax.broadcasted_iota(jnp.int32, (256, 128), 1) // 32
    weights_high, weights_low = split(weights[...])
    dot = functools.partial(lax.dot_general, preferred_element_type=F32)
    right = (((1,), (0,)), ((), ()))
    rows_out = (((0,), (0,)), ((), ()))
    straight, cross = jnp.zeros((256, 256), F32), jnp.zeros((256, 256), F32)
    for t in range(4):
        halves = []
        for b in range(2):
            value = None
            for c in range(4):
                piece = ring[c * 2 + b]
                if c != t:
                    piece = pltpu.roll(piece, ((c - t) % 4) * 32, 1)
                value = piece if value is None else jnp.where(lane == c, piece, value)
            halves.append(value)
        all_orbitals = jnp.concatenate(halves, axis=1)
        high, low = split(all_orbitals)
        turned = dot(high, weights_high, right) + (dot(high, weights_low, right) + dot(low, weights_high, right))
        for b in range(2):
            rows = turned[:, b * 128 : (b + 1) * 128].reshape(32, 8, 128)
            out[:, b, 2 * t] = rows[:, 0:4]
            out[:, b, 2 * t + 1] = rows[:, 4:8]
        straight = straight + dot(high, high, rows_out)
        cross = cross + dot(high, low, rows_out)
    row = lax.broadcasted_iota(jnp.int32, (256, 256), 0)
    column = lax.broadcasted_iota(jnp.int32, (256, 256), 1)
    same = (row // 8 % 4 == column // 8 % 4) & (row % 4 == column % 4)
    diagonal = jnp.where(same, straight + (cross + cross.T), 0.0).reshape(8, 4, 8, 256).sum(axis=1).reshape(64, 256)
    number = lax.broadcasted_iota(jnp.int32, (256, 16), 0)
    entry = lax.broadcasted_iota(jnp.int32, (256, 16), 1)
    columns = (number // 32 * 2 + number // 4 % 2 == entry).astype(F32)
    number, entry = number[:64], entry[:64]
    rows = (number // 8 * 2 + number // 4 % 2 == entry).astype(F32)
    both = exact(rows, exact(diagonal, columns, (((1,), (0,)), ((), ()))), (((0,), (0,)), ((), ())))
    tile = jnp.concatenate([both[4 * q : 4 * q + 4] for q in range(4)] + [jnp.zeros((4, 64), F32)], axis=1)
    out[:, :, 8] = jnp.broadcast_to(tile, (32, 2, 4, 128))


def lines_kernel(received, out):
    low = lax.broadcasted_iota(jnp.int32, (16, 8, 128), 1) < 4

    def lines(s, b):
        pieces = [
            jnp.concatenate([received[s * 4 + c, b, 2 * j], received[s * 4 + c, b, 2 * j + 1]], axis=0)
            for c in range(4)
            for j in range(4)
        ]
        return jnp.concatenate(pieces, axis=0).T.reshape(16, 8, 128)

    for s in range(8):
        first, second = lines(s, 0), lines(s, 1)
        even = jnp.where(low, first, pltpu.roll(second, 4, 1)).reshape(8, 2, 8, 128)
        odd = jnp.where(low, pltpu.roll(first, 4, 1), second).reshape(8, 2, 8, 128)
        for q in range(2):
            out[:, q * 16 : q * 16 + 8, s * 128 : (s + 1) * 128] = even[:, q]
            out[:, q * 16 + 8 : q * 16 + 16, s * 128 : (s + 1) * 128] = odd[:, q]


def call(kernel, out, scratch=()):
    vmem = pl.BlockSpec(memory_space=pltpu.VMEM)
    smem = pl.BlockSpec(memory_space=pltpu.SMEM)
    return lambda *args: pl.pallas_call(
        kernel,
        out_shape=[jax.ShapeDtypeStruct(s, F32) for s in out],
        in_specs=[smem if a.dtype == jnp.int32 else vmem for a in args],
        out_specs=[vmem] * len(out),
        scratch_shapes=[pltpu.VMEM(s, F32) for s in scratch],
        compiler_params=pltpu.CompilerParams(vmem_limit_bytes=48 * 1024 * 1024),
    )(*args)


def four(x, one, one_bit, two, two_bit):
    def swap(axes, bits):
        sizes = [lax.axis_size(a) for a in axes]
        flat = [np.ravel_multi_index([i ^ b for i, b in zip(at, bits)], sizes) for at in np.ndindex(*sizes)]
        return lax.ppermute(x, axes, [(i, int(j)) for i, j in enumerate(flat)])

    if one == two:
        parts = [swap((one,), (bits,)) for bits in (one_bit, two_bit, one_bit ^ two_bit)]
    else:
        parts = [swap((one, two), bits) for bits in ((one_bit, 0), (0, two_bit), (one_bit, two_bit))]
    return (x + parts[0]) + (parts[1] + parts[2])


def local(orbitals, potential, coefficients):
    chunks = ("z", "x")
    dom = ("z", "x", "u", "c")
    count = lax.axis_size(chunks)

    shift = [(d, d + 4 if d % 4 >= 2 else d - 4) for d in range(4 * count)]
    beyond = lax.ppermute(potential, dom, [(i, j) for i, j in shift if 0 <= j < 4 * count])
    slabs = lax.all_to_all(orbitals.reshape(4, OWN, 8, NY, NZ), ("u", "c"), 0, 0, tiled=True)
    slabs, beyond = lax.optimization_barrier((slabs, beyond))
    far = 3 * WIDTH
    part = far - 16
    chunk = lax.axis_index(chunks)
    first = jnp.concatenate([slabs[0], slabs[1], slabs[2, :, :part]], axis=1)
    last = jnp.concatenate([slabs[1, :, 8 - part :], slabs[2], slabs[3]], axis=1)
    swaps = [[(i, j) for k in range(s, count - 1, 2) for i, j in ((k, k + 1), (k + 1, k))] for s in (1, 0)]
    ahead = lax.ppermute(jnp.where(chunk % 2 == 1, last, first), chunks, swaps[0])
    behind = lax.ppermute(jnp.where(chunk % 2 == 1, first, last), chunks, swaps[1])
    own = lax.all_gather(potential, ("u", "c"))
    beyond = lax.all_gather(beyond, ("u", "c"))

    scratch = [
        (CHUNK + 2 * far, 8 + 2 * EXT, 8, NZ),
        (CHUNK + 2 * (2 * WIDTH + 2), 8 + 2 * EXT, 8, NZ),
        (64, 8, 8, NZ),
        (8, 8, 8, 8, NZ),
        (CHUNK, 8, 8, NZ),
        (2 * 8 * NZ, NZ),
    ]
    bands = jnp.asarray(banded(1.0 / HALF))
    (weights,) = call(weights_kernel, [(256, 256)])(coefficients)
    (message,) = call(filter_kernel, [(4, 2, 32, 8, 128)], scratch)(
        chunk.reshape(1), slabs, ahead, behind, own, beyond, bands
    )
    ring = lax.all_to_all(message.reshape(8, 256, 128), ("u", "c", "b"), 0, 0, tiled=True)
    (rotated,) = call(rotate_kernel, [(32, 2, 9, 4, 128)])(ring, weights)
    received = lax.all_to_all(rotated.reshape(64, 9, 4, 128), ("z", "x", "b"), 0, 0, tiled=True)
    gram = four(received[:, 8].sum(axis=0), "u", 1, "c", 1) / (NX * NY * NZ)
    intersection = jnp.concatenate([gram[:, q * NORB : (q + 1) * NORB] for q in range(4)], axis=0)
    (lines,) = call(lines_kernel, [(8, NY, NX)])(received.reshape(32, 2, 9, 4, 128))
    return intersection, lines


def solution(mesh):
    grid = Mesh(mesh.devices.reshape(8, 4, 2, 2, 2), ("z", "x", "u", "c", "b"))
    dom = ("z", "x", "u", "c")
    return jax.shard_map(
        local,
        mesh=grid,
        in_specs=(P("b", dom, None, None), P(dom, None, None), P()),
        out_specs=(P(), P("b", dom, None)),
        check_vma=False,
    )
```

```python
import functools

import jax
import jax.numpy as jnp
import ml_dtypes
import numpy as np
from jax import lax
from jax.experimental import pallas as pl
from jax.experimental.pallas import tpu as pltpu
from jax.sharding import Mesh
from jax.sharding import PartitionSpec as P

STENCIL = (
    -5369.0 / 1800.0,
    12.0 / 7.0,
    -15.0 / 56.0,
    10.0 / 189.0,
    -1.0 / 112.0,
    2.0 / 1925.0,
    -1.0 / 16632.0,
)
CENTER = 8.5
HALF = 6.5
WIDTH = 6
EXT = 6
NORB, NX, NY, NZ = 16, 1024, 32, 128
CHUNK = 32
OWN = 2
F32 = jnp.float32
BF16 = jnp.bfloat16


def banded(scale):
    band = np.zeros((NZ, NZ), np.float64)
    for k in range(1, 7):
        band += np.eye(NZ, k=k) * STENCIL[k] + np.eye(NZ, k=-k) * STENCIL[k]
    band = (-0.5 * scale * band).astype(np.float32)
    high = band.astype(ml_dtypes.bfloat16)
    low = (band - high.astype(np.float32)).astype(ml_dtypes.bfloat16)
    zero = np.zeros_like(high)
    return np.block([[high, low], [high, zero]]).astype(ml_dtypes.bfloat16)


def split(x):
    high = x.astype(BF16)
    low = (x - high.astype(F32)).astype(BF16)
    return high, low


def filter_kernel(
    chunk, slabs, ahead, behind, own, beyond, bands, out, field, other, local, z, result, turned
):
    far, near = 3 * WIDTH, 2 * WIDTH + 2
    row = lax.broadcasted_iota(jnp.int32, (8, 8, NZ), 1) % 4

    def store(target, plane, r, value):
        planes = pl.ds(plane, 8)
        target[planes, EXT + r] = value
        if r >= 8 - EXT:
            target[planes, r - (8 - EXT)] = jnp.where(row == 0, 0.0, pltpu.roll(value, 1, 1))
        if r < EXT:
            target[planes, EXT + 8 + r] = jnp.where(row == 3, 0.0, pltpu.roll(value, 7, 1))

    def tiles(sources):
        rows = [jnp.concatenate([source[(*at, pl.ds(r, 4, stride=8), slice(None))] for source, at in sources], axis=0) for r in range(8)]
        return jnp.stack(rows)

    def enter(plane, sources):
        value = tiles(sources)
        field[plane, EXT : EXT + 8] = value
        field[plane, 0:EXT] = jnp.where(row[:EXT] == 0, 0.0, pltpu.roll(value[8 - EXT :], 1, 1))
        field[plane, EXT + 8 :] = jnp.where(row[:EXT] == 3, 0.0, pltpu.roll(value[:EXT], 7, 1))

    odd = chunk[0] % 2

    def enter_ends(p, _):
        enter(odd * (far + CHUNK) + p, [(ahead, (o, p)) for o in range(OWN)])
        enter((1 - odd) * (far + CHUNK) + p, [(behind, (o, p)) for o in range(OWN)])
        return 0

    lax.fori_loop(0, far, enter_ends, 0)

    def enter_slabs(p, _):
        for s in range(4):
            enter(far + 8 * s + p, [(slabs, (s, o, p)) for o in range(OWN)])
        return 0

    lax.fori_loop(0, 8, enter_slabs, 0)

    def enter_local(p, _):
        for j, (source, s) in enumerate(
            [(beyond, 2), (beyond, 3), (own, 0), (own, 1), (own, 2), (own, 3), (beyond, 0), (beyond, 1)]
        ):
            value = tiles([(source, (s, p)), (source, (s, p))])
            local[8 * j + p] = (value + (-1.5 * STENCIL[0] - CENTER)) * (1.0 / HALF)
        return 0

    lax.fori_loop(0, 8, enter_local, 0)

    def along_z(source, index):
        high, low = split(source[pl.ds(index, 4), EXT : EXT + 8].reshape(4 * 64, NZ))
        both = jnp.dot(jnp.concatenate([high, low], axis=1), bands[...], preferred_element_type=F32)
        return (both[:, :NZ] + both[:, NZ:]).reshape(4, 8, 8, NZ)

    def step(source, shift, first, blocks, put):
        def body(i, _):
            start = first + 8 * i
            later = first + 8 * jnp.minimum(i + 1, blocks - 1) + shift
            for half in range(2):
                ahead = along_z(source, later + 4 * half)
                for r in range(4 * half, 4 * half + 4):
                    window = source[pl.ds(start + shift - WIDTH, 8 + 2 * WIDTH), EXT + r]
                    total = local[pl.ds(start + 16, 8), r] * window[WIDTH : WIDTH + 8] + z[i, :, r]
                    for k in range(1, 7):
                        beside = window[WIDTH + k : WIDTH + 8 + k] + window[WIDTH - k : WIDTH + 8 - k]
                        planes = pl.ds(start + shift, 8)
                        beside = beside + (source[planes, EXT + r + k] + source[planes, EXT + r - k])
                        total = total + (-0.5 / HALF * STENCIL[k]) * beside
                    put(start, r, total)
                z[i + 1, 4 * half : 4 * half + 4] = ahead
            return 0

        for half in range(2):
            z[0, 4 * half : 4 * half + 4] = along_z(source, first + shift + 4 * half)
        lax.fori_loop(0, blocks, body, 0)

    def put_first(start, r, total):
        store(other, start + near, r, total)

    def put_second(start, r, total):
        store(field, start + far, r, (total + total) - field[pl.ds(start + far, 8), EXT + r])

    def put_third(start, r, total):
        result[pl.ds(start, 8), r] = (total + total) - other[pl.ds(start + near, 8), EXT + r]

    def outside(target, shift, count):
        blank = jnp.zeros((count, 8 + 2 * EXT, 8, NZ), F32)

        @pl.when(chunk[0] == 0)
        def _():
            target[shift - count : shift] = blank

        @pl.when(chunk[0] == NX // CHUNK - 1)
        def _():
            target[shift + CHUNK : shift + CHUNK + count] = blank

    step(field, far, -12, 7, put_first)
    outside(other, near, 12)
    step(other, near, -8, 6, put_second)
    outside(field, far, 8)
    step(field, far, 0, 4, put_third)

    def turn(x, _):
        for b in range(2):
            pieces = [result[t * 8 + x, b * 4 + r] for t in range(4) for r in range(4)]
            turned[pl.ds((b * 8 + x) * NZ, NZ), :] = jnp.concatenate(pieces, axis=0).T
        return 0

    lax.fori_loop(0, 8, turn, 0)

    def pick(q, _):
        for c in range(4):
            for b in range(2):
                out[c, b, q] = turned[pl.ds(b * 8 * NZ + 4 * q + c, 8, stride=NZ), :]
        return 0

    lax.fori_loop(0, NZ // 4, pick, 0)


exact = functools.partial(lax.dot_general, precision=lax.Precision.HIGHEST, preferred_element_type=F32)


def weights_kernel(coefficients, out):
    row = lax.broadcasted_iota(jnp.int32, (256, 256), 0)
    column = lax.broadcasted_iota(jnp.int32, (256, 256), 1)
    number = lax.broadcasted_iota(jnp.int32, (256, 16), 0)
    entry = lax.broadcasted_iota(jnp.int32, (256, 16), 1)
    before = (number // 32 * 2 + number // 4 % 2 == entry).astype(F32)
    after = (number // 16 == entry).astype(F32)
    spread = exact(before, exact(coefficients[...], after, (((1,), (1,)), ((), ()))), (((1,), (0,)), ((), ())))
    same = (row // 8 % 4 == column % 4) & (row % 4 == column // 4 % 4)
    out[...] = jnp.where(same, spread, 0.0)


def rotate_kernel(ring, weights, out):
    lane = lax.broadcasted_iota(jnp.int32, (256, 128), 1) // 32
    weights_high, weights_low = split(weights[...])
    dot = functools.partial(lax.dot_general, preferred_element_type=F32)
    right = (((1,), (0,)), ((), ()))
    rows_out = (((0,), (0,)), ((), ()))
    straight, cross = jnp.zeros((256, 256), F32), jnp.zeros((256, 256), F32)
    for t in range(4):
        halves = []
        for b in range(2):
            value = None
            for c in range(4):
                piece = ring[c * 2 + b]
                if c != t:
                    piece = pltpu.roll(piece, ((c - t) % 4) * 32, 1)
                value = piece if value is None else jnp.where(lane == c, piece, value)
            halves.append(value)
        all_orbitals = jnp.concatenate(halves, axis=1)
        high, low = split(all_orbitals)
        turned = dot(high, weights_high, right) + (dot(high, weights_low, right) + dot(low, weights_high, right))
        for b in range(2):
            rows = turned[:, b * 128 : (b + 1) * 128].reshape(8, 4, 8, 128)
            for x in range(4):
                out[x, b, :, 2 * t] = rows[:, x, 0:4]
                out[x, b, :, 2 * t + 1] = rows[:, x, 4:8]
        straight = straight + dot(high, high, rows_out)
        cross = cross + dot(high, low, rows_out)
    row = lax.broadcasted_iota(jnp.int32, (256, 256), 0)
    column = lax.broadcasted_iota(jnp.int32, (256, 256), 1)
    same = (row // 8 % 4 == column // 8 % 4) & (row % 4 == column % 4)
    diagonal = jnp.where(same, straight + (cross + cross.T), 0.0).reshape(8, 4, 8, 256).sum(axis=1).reshape(64, 256)
    number = lax.broadcasted_iota(jnp.int32, (256, 16), 0)
    entry = lax.broadcasted_iota(jnp.int32, (256, 16), 1)
    columns = (number // 32 * 2 + number // 4 % 2 == entry).astype(F32)
    number, entry = number[:64], entry[:64]
    rows = (number // 8 * 2 + number // 4 % 2 == entry).astype(F32)
    both = exact(rows, exact(diagonal, columns, (((1,), (0,)), ((), ()))), (((0,), (0,)), ((), ())))
    tile = jnp.concatenate([both[4 * q : 4 * q + 4] for q in range(4)] + [jnp.zeros((4, 64), F32)], axis=1)
    out[:, :, :, 8] = jnp.broadcast_to(tile, (4, 2, 8, 4, 128))


def lines_kernel(received, out):
    low = lax.broadcasted_iota(jnp.int32, (16, 8, 128), 1) < 4

    def lines(s, b):
        pieces = [
            jnp.concatenate([received[c, b, s, 2 * j], received[c, b, s, 2 * j + 1]], axis=0)
            for c in range(4)
            for j in range(4)
        ]
        return jnp.concatenate(pieces, axis=0).T.reshape(16, 8, 128)

    for s in range(8):
        first, second = lines(s, 0), lines(s, 1)
        even = jnp.where(low, first, pltpu.roll(second, 4, 1)).reshape(8, 2, 8, 128)
        odd = jnp.where(low, pltpu.roll(first, 4, 1), second).reshape(8, 2, 8, 128)
        for q in range(2):
            out[:, q * 16 : q * 16 + 8, s * 128 : (s + 1) * 128] = even[:, q]
            out[:, q * 16 + 8 : q * 16 + 16, s * 128 : (s + 1) * 128] = odd[:, q]


def call(kernel, out, scratch=()):
    vmem = pl.BlockSpec(memory_space=pltpu.VMEM)
    smem = pl.BlockSpec(memory_space=pltpu.SMEM)
    return lambda *args: pl.pallas_call(
        kernel,
        out_shape=[jax.ShapeDtypeStruct(s, F32) for s in out],
        in_specs=[smem if a.dtype == jnp.int32 else vmem for a in args],
        out_specs=[vmem] * len(out),
        scratch_shapes=[pltpu.VMEM(s, F32) for s in scratch],
        compiler_params=pltpu.CompilerParams(vmem_limit_bytes=48 * 1024 * 1024),
    )(*args)


def four(x, one, one_bit, two, two_bit):
    def swap(axes, bits):
        sizes = [lax.axis_size(a) for a in axes]
        flat = [np.ravel_multi_index([i ^ b for i, b in zip(at, bits)], sizes) for at in np.ndindex(*sizes)]
        return lax.ppermute(x, axes, [(i, int(j)) for i, j in enumerate(flat)])

    if one == two:
        parts = [swap((one,), (bits,)) for bits in (one_bit, two_bit, one_bit ^ two_bit)]
    else:
        parts = [swap((one, two), bits) for bits in ((one_bit, 0), (0, two_bit), (one_bit, two_bit))]
    return (x + parts[0]) + (parts[1] + parts[2])


def local(orbitals, potential, coefficients):
    chunks = ("z", "x")
    dom = ("z", "x", "u", "c")
    count = lax.axis_size(chunks)

    shift = [(d, d + 4 if d % 4 >= 2 else d - 4) for d in range(4 * count)]
    beyond = lax.ppermute(potential, dom, [(i, j) for i, j in shift if 0 <= j < 4 * count])
    slabs = lax.all_to_all(orbitals.reshape(4, OWN, 8, NY, NZ), ("u", "c"), 0, 0, tiled=True)
    (weights,) = call(weights_kernel, [(256, 256)])(coefficients)
    slabs, beyond, weights = lax.optimization_barrier((slabs, beyond, weights))
    far = 3 * WIDTH
    part = far - 16
    chunk = lax.axis_index(chunks)
    first = jnp.concatenate([slabs[0], slabs[1], slabs[2, :, :part]], axis=1)
    last = jnp.concatenate([slabs[1, :, 8 - part :], slabs[2], slabs[3]], axis=1)
    swaps = [[(i, j) for k in range(s, count - 1, 2) for i, j in ((k, k + 1), (k + 1, k))] for s in (1, 0)]
    ahead = lax.ppermute(jnp.where(chunk % 2 == 1, last, first), chunks, swaps[0])
    behind = lax.ppermute(jnp.where(chunk % 2 == 1, first, last), chunks, swaps[1])
    own = lax.all_gather(potential, ("u", "c"))
    beyond = lax.all_gather(beyond, ("u", "c"))

    scratch = [
        (CHUNK + 2 * far, 8 + 2 * EXT, 8, NZ),
        (CHUNK + 2 * (2 * WIDTH + 2), 8 + 2 * EXT, 8, NZ),
        (64, 8, 8, NZ),
        (8, 8, 8, 8, NZ),
        (CHUNK, 8, 8, NZ),
        (2 * 8 * NZ, NZ),
    ]
    bands = jnp.asarray(banded(1.0 / HALF))
    (message,) = call(filter_kernel, [(4, 2, 32, 8, 128)], scratch)(
        chunk.reshape(1), slabs, ahead, behind, own, beyond, bands
    )
    ring = lax.all_to_all(message.reshape(8, 256, 128), ("u", "c", "b"), 0, 0, tiled=True)
    (rotated,) = call(rotate_kernel, [(4, 2, 8, 9, 4, 128)])(ring, weights)
    everyone = np.arange(256).reshape(8, 4, 4, 2)
    groups = everyone.transpose(2, 1, 3, 0).reshape(4, 64).tolist()
    received = lax.all_to_all(
        rotated.reshape(64, 9, 4, 128), ("z", "x", "u", "c", "b"), 0, 0, axis_index_groups=groups, tiled=True
    )
    gram = four(received[:, 8].sum(axis=0), "u", 1, "c", 1) / (NX * NY * NZ)
    intersection = jnp.concatenate([gram[:, q * NORB : (q + 1) * NORB] for q in range(4)], axis=0)
    (lines,) = call(lines_kernel, [(8, NY, NX)])(received.reshape(4, 2, 8, 9, 4, 128))
    return intersection, lines


def solution(mesh):
    grid = Mesh(mesh.devices.reshape(8, 4, 2, 2, 2), ("z", "x", "u", "c", "b"))
    dom = ("z", "x", "u", "c")
    return jax.shard_map(
        local,
        mesh=grid,
        in_specs=(P("b", dom, None, None), P(dom, None, None), P()),
        out_specs=(P(), P("b", dom, None)),
        check_vma=False,
    )
```

```python
import functools

import jax
import jax.numpy as jnp
import ml_dtypes
import numpy as np
from jax import lax
from jax.experimental import pallas as pl
from jax.experimental.pallas import tpu as pltpu
from jax.sharding import Mesh
from jax.sharding import PartitionSpec as P

STENCIL = (
    -5369.0 / 1800.0,
    12.0 / 7.0,
    -15.0 / 56.0,
    10.0 / 189.0,
    -1.0 / 112.0,
    2.0 / 1925.0,
    -1.0 / 16632.0,
)
CENTER = 8.5
HALF = 6.5
WIDTH = 6
EXT = 6
NORB, NX, NY, NZ = 16, 1024, 32, 128
CHUNK = 32
OWN = 2
F32 = jnp.float32
BF16 = jnp.bfloat16


def banded(scale):
    band = np.zeros((NZ, NZ), np.float64)
    for k in range(1, 7):
        band += np.eye(NZ, k=k) * STENCIL[k] + np.eye(NZ, k=-k) * STENCIL[k]
    band = (-0.5 * scale * band).astype(np.float32)
    high = band.astype(ml_dtypes.bfloat16)
    low = (band - high.astype(np.float32)).astype(ml_dtypes.bfloat16)
    zero = np.zeros_like(high)
    return np.block([[high, low], [high, zero]]).astype(ml_dtypes.bfloat16)


def split(x):
    high = x.astype(BF16)
    low = (x - high.astype(F32)).astype(BF16)
    return high, low


def edges_kernel(place, piece_0, piece_1, piece_2, piece_3, ahead, behind):
    def copy(first, last):
        for m, piece in enumerate((piece_0, piece_1, piece_2, piece_3)):
            slab = place[1] ^ m

            @pl.when(slab == 0)
            def _():
                first[:, 0:8] = piece[...]

            @pl.when(slab == 1)
            def _():
                first[:, 8:16] = piece[...]
                last[:, 0:2] = piece[:, 6:8]

            @pl.when(slab == 2)
            def _():
                first[:, 16:18] = piece[:, 0:2]
                last[:, 2:10] = piece[...]

            @pl.when(slab == 3)
            def _():
                last[:, 10:18] = piece[...]

    @pl.when(place[0] % 2 == 1)
    def _():
        copy(behind, ahead)

    @pl.when(place[0] % 2 == 0)
    def _():
        copy(ahead, behind)


def filter_kernel(
    place, piece_0, piece_1, piece_2, piece_3, ahead, behind, own, beyond, bands,
    out, field, other, local, z, result, turned,
):
    far, near = 3 * WIDTH, 2 * WIDTH + 2
    row = lax.broadcasted_iota(jnp.int32, (8, 8, NZ), 1) % 4

    def store(target, plane, r, value):
        planes = pl.ds(plane, 8)
        target[planes, EXT + r] = value
        if r >= 8 - EXT:
            target[planes, r - (8 - EXT)] = jnp.where(row == 0, 0.0, pltpu.roll(value, 1, 1))
        if r < EXT:
            target[planes, EXT + 8 + r] = jnp.where(row == 3, 0.0, pltpu.roll(value, 7, 1))

    def tiles(sources):
        rows = [jnp.concatenate([source[(*at, pl.ds(r, 4, stride=8), slice(None))] for source, at in sources], axis=0) for r in range(8)]
        return jnp.stack(rows)

    def enter(plane, sources):
        value = tiles(sources)
        field[plane, EXT : EXT + 8] = value
        field[plane, 0:EXT] = jnp.where(row[:EXT] == 0, 0.0, pltpu.roll(value[8 - EXT :], 1, 1))
        field[plane, EXT + 8 :] = jnp.where(row[:EXT] == 3, 0.0, pltpu.roll(value[:EXT], 7, 1))

    odd = place[0] % 2

    def enter_ends(p, _):
        enter(odd * (far + CHUNK) + p, [(ahead, (o, p)) for o in range(OWN)])
        enter((1 - odd) * (far + CHUNK) + p, [(behind, (o, p)) for o in range(OWN)])
        return 0

    lax.fori_loop(0, far, enter_ends, 0)

    def enter_slabs(p, _):
        for m, piece in enumerate((piece_0, piece_1, piece_2, piece_3)):
            enter(far + 8 * (place[1] ^ m) + p, [(piece, (o, p)) for o in range(OWN)])
        return 0

    lax.fori_loop(0, 8, enter_slabs, 0)

    def enter_local(p, _):
        for j, (source, s) in enumerate(
            [(beyond, 2), (beyond, 3), (own, 0), (own, 1), (own, 2), (own, 3), (beyond, 0), (beyond, 1)]
        ):
            value = tiles([(source, (s, p)), (source, (s, p))])
            local[8 * j + p] = (value + (-1.5 * STENCIL[0] - CENTER)) * (1.0 / HALF)
        return 0

    lax.fori_loop(0, 8, enter_local, 0)

    def along_z(source, index):
        high, low = split(source[pl.ds(index, 4), EXT : EXT + 8].reshape(4 * 64, NZ))
        both = jnp.dot(jnp.concatenate([high, low], axis=1), bands[...], preferred_element_type=F32)
        return (both[:, :NZ] + both[:, NZ:]).reshape(4, 8, 8, NZ)

    def step(source, shift, first, blocks, put):
        def body(i, _):
            start = first + 8 * i
            later = first + 8 * jnp.minimum(i + 1, blocks - 1) + shift
            for half in range(2):
                ahead = along_z(source, later + 4 * half)
                for r in range(4 * half, 4 * half + 4):
                    window = source[pl.ds(start + shift - WIDTH, 8 + 2 * WIDTH), EXT + r]
                    total = local[pl.ds(start + 16, 8), r] * window[WIDTH : WIDTH + 8] + z[i, :, r]
                    for k in range(1, 7):
                        beside = window[WIDTH + k : WIDTH + 8 + k] + window[WIDTH - k : WIDTH + 8 - k]
                        planes = pl.ds(start + shift, 8)
                        beside = beside + (source[planes, EXT + r + k] + source[planes, EXT + r - k])
                        total = total + (-0.5 / HALF * STENCIL[k]) * beside
                    put(start, r, total)
                z[i + 1, 4 * half : 4 * half + 4] = ahead
            return 0

        for half in range(2):
            z[0, 4 * half : 4 * half + 4] = along_z(source, first + shift + 4 * half)
        lax.fori_loop(0, blocks, body, 0)

    def put_first(start, r, total):
        store(other, start + near, r, total)

    def put_second(start, r, total):
        store(field, start + far, r, (total + total) - field[pl.ds(start + far, 8), EXT + r])

    def put_third(start, r, total):
        result[pl.ds(start, 8), r] = (total + total) - other[pl.ds(start + near, 8), EXT + r]

    def outside(target, shift, count):
        blank = jnp.zeros((count, 8 + 2 * EXT, 8, NZ), F32)

        @pl.when(place[0] == 0)
        def _():
            target[shift - count : shift] = blank

        @pl.when(place[0] == NX // CHUNK - 1)
        def _():
            target[shift + CHUNK : shift + CHUNK + count] = blank

    step(field, far, -12, 7, put_first)
    outside(other, near, 12)
    step(other, near, -8, 6, put_second)
    outside(field, far, 8)
    step(field, far, 0, 4, put_third)

    def turn(x, _):
        for b in range(2):
            pieces = [result[t * 8 + x, b * 4 + r] for t in range(4) for r in range(4)]
            turned[pl.ds((b * 8 + x) * NZ, NZ), :] = jnp.concatenate(pieces, axis=0).T
        return 0

    lax.fori_loop(0, 8, turn, 0)

    def pick(q, _):
        for c in range(4):
            for b in range(2):
                out[c, b, q] = turned[pl.ds(b * 8 * NZ + 4 * q + c, 8, stride=NZ), :]
        return 0

    lax.fori_loop(0, NZ // 4, pick, 0)


exact = functools.partial(lax.dot_general, precision=lax.Precision.HIGHEST, preferred_element_type=F32)


def weights_kernel(coefficients, out):
    row = lax.broadcasted_iota(jnp.int32, (256, 256), 0)
    column = lax.broadcasted_iota(jnp.int32, (256, 256), 1)
    number = lax.broadcasted_iota(jnp.int32, (256, 16), 0)
    entry = lax.broadcasted_iota(jnp.int32, (256, 16), 1)
    before = (number // 32 * 2 + number // 4 % 2 == entry).astype(F32)
    after = (number // 16 == entry).astype(F32)
    spread = exact(before, exact(coefficients[...], after, (((1,), (1,)), ((), ()))), (((1,), (0,)), ((), ())))
    same = (row // 8 % 4 == column % 4) & (row % 4 == column // 4 % 4)
    out[...] = jnp.where(same, spread, 0.0)


def rotate_kernel(ring, weights, out):
    lane = lax.broadcasted_iota(jnp.int32, (256, 128), 1) // 32
    weights_high, weights_low = split(weights[...])
    dot = functools.partial(lax.dot_general, preferred_element_type=F32)
    right = (((1,), (0,)), ((), ()))
    rows_out = (((0,), (0,)), ((), ()))
    straight, cross = jnp.zeros((256, 256), F32), jnp.zeros((256, 256), F32)
    for t in range(4):
        halves = []
        for b in range(2):
            value = None
            for c in range(4):
                piece = ring[c * 2 + b]
                if c != t:
                    piece = pltpu.roll(piece, ((c - t) % 4) * 32, 1)
                value = piece if value is None else jnp.where(lane == c, piece, value)
            halves.append(value)
        all_orbitals = jnp.concatenate(halves, axis=1)
        high, low = split(all_orbitals)
        turned = dot(high, weights_high, right) + (dot(high, weights_low, right) + dot(low, weights_high, right))
        for b in range(2):
            rows = turned[:, b * 128 : (b + 1) * 128].reshape(8, 4, 8, 128)
            for x in range(4):
                out[x, b, :, 2 * t] = rows[:, x, 0:4]
                out[x, b, :, 2 * t + 1] = rows[:, x, 4:8]
        straight = straight + dot(high, high, rows_out)
        cross = cross + dot(high, low, rows_out)
    row = lax.broadcasted_iota(jnp.int32, (256, 256), 0)
    column = lax.broadcasted_iota(jnp.int32, (256, 256), 1)
    same = (row // 8 % 4 == column // 8 % 4) & (row % 4 == column % 4)
    diagonal = jnp.where(same, straight + (cross + cross.T), 0.0).reshape(8, 4, 8, 256).sum(axis=1).reshape(64, 256)
    number = lax.broadcasted_iota(jnp.int32, (256, 16), 0)
    entry = lax.broadcasted_iota(jnp.int32, (256, 16), 1)
    columns = (number // 32 * 2 + number // 4 % 2 == entry).astype(F32)
    number, entry = number[:64], entry[:64]
    rows = (number // 8 * 2 + number // 4 % 2 == entry).astype(F32)
    both = exact(rows, exact(diagonal, columns, (((1,), (0,)), ((), ()))), (((0,), (0,)), ((), ())))
    tile = jnp.concatenate([both[4 * q : 4 * q + 4] for q in range(4)] + [jnp.zeros((4, 64), F32)], axis=1)
    out[:, :, :, 8] = jnp.broadcast_to(tile, (4, 2, 8, 4, 128))


def lines_kernel(received, out):
    low = lax.broadcasted_iota(jnp.int32, (16, 8, 128), 1) < 4

    def lines(s, b):
        pieces = [
            jnp.concatenate([received[c, b, s, 2 * j], received[c, b, s, 2 * j + 1]], axis=0)
            for c in range(4)
            for j in range(4)
        ]
        return jnp.concatenate(pieces, axis=0).T.reshape(16, 8, 128)

    for s in range(8):
        first, second = lines(s, 0), lines(s, 1)
        even = jnp.where(low, first, pltpu.roll(second, 4, 1)).reshape(8, 2, 8, 128)
        odd = jnp.where(low, pltpu.roll(first, 4, 1), second).reshape(8, 2, 8, 128)
        for q in range(2):
            out[:, q * 16 : q * 16 + 8, s * 128 : (s + 1) * 128] = even[:, q]
            out[:, q * 16 + 8 : q * 16 + 16, s * 128 : (s + 1) * 128] = odd[:, q]


def call(kernel, out, scratch=()):
    vmem = pl.BlockSpec(memory_space=pltpu.VMEM)
    smem = pl.BlockSpec(memory_space=pltpu.SMEM)
    return lambda *args: pl.pallas_call(
        kernel,
        out_shape=[jax.ShapeDtypeStruct(s, F32) for s in out],
        in_specs=[smem if a.dtype == jnp.int32 else vmem for a in args],
        out_specs=[vmem] * len(out),
        scratch_shapes=[pltpu.VMEM(s, F32) for s in scratch],
        compiler_params=pltpu.CompilerParams(vmem_limit_bytes=48 * 1024 * 1024),
    )(*args)


def four(x, one, one_bit, two, two_bit):
    def swap(axes, bits):
        sizes = [lax.axis_size(a) for a in axes]
        flat = [np.ravel_multi_index([i ^ b for i, b in zip(at, bits)], sizes) for at in np.ndindex(*sizes)]
        return lax.ppermute(x, axes, [(i, int(j)) for i, j in enumerate(flat)])

    if one == two:
        parts = [swap((one,), (bits,)) for bits in (one_bit, two_bit, one_bit ^ two_bit)]
    else:
        parts = [swap((one, two), bits) for bits in ((one_bit, 0), (0, two_bit), (one_bit, two_bit))]
    return (x + parts[0]) + (parts[1] + parts[2])


def local(orbitals, potential, coefficients):
    chunks = ("z", "x")
    dom = ("z", "x", "u", "c")
    count = lax.axis_size(chunks)

    shift = [(d, d + 4 if d % 4 >= 2 else d - 4) for d in range(4 * count)]
    beyond = lax.ppermute(potential, dom, [(i, j) for i, j in shift if 0 <= j < 4 * count])
    group = lax.axis_index(("u", "c"))
    pieces = {0: lax.dynamic_slice_in_dim(orbitals, OWN * group, OWN, 0)}
    for m in (2, 3, 1):
        piece = lax.dynamic_slice_in_dim(orbitals, OWN * (group ^ m), OWN, 0)
        pieces[m] = lax.ppermute(piece, ("u", "c"), [(i, i ^ m) for i in range(4)])
    (weights,) = call(weights_kernel, [(256, 256)])(coefficients)
    pieces, beyond, weights = lax.optimization_barrier(([pieces[m] for m in range(4)], beyond, weights))
    far = 3 * WIDTH
    chunk = lax.axis_index(chunks)
    place = jnp.stack([chunk, group])
    ahead, behind = call(edges_kernel, [(OWN, far, NY, NZ)] * 2)(place, *pieces)
    swaps = [[(i, j) for k in range(s, count - 1, 2) for i, j in ((k, k + 1), (k + 1, k))] for s in (1, 0)]
    ahead = lax.ppermute(ahead, chunks, swaps[0])
    behind = lax.ppermute(behind, chunks, swaps[1])
    own = lax.all_gather(potential, ("u", "c"))
    beyond = lax.all_gather(beyond, ("u", "c"))

    scratch = [
        (CHUNK + 2 * far, 8 + 2 * EXT, 8, NZ),
        (CHUNK + 2 * (2 * WIDTH + 2), 8 + 2 * EXT, 8, NZ),
        (64, 8, 8, NZ),
        (8, 8, 8, 8, NZ),
        (CHUNK, 8, 8, NZ),
        (2 * 8 * NZ, NZ),
    ]
    bands = jnp.asarray(banded(1.0 / HALF))
    (message,) = call(filter_kernel, [(4, 2, 32, 8, 128)], scratch)(
        place, *pieces, ahead, behind, own, beyond, bands
    )
    ring = lax.all_to_all(message.reshape(8, 256, 128), ("u", "c", "b"), 0, 0, tiled=True)
    (rotated,) = call(rotate_kernel, [(4, 2, 8, 9, 4, 128)])(ring, weights)
    everyone = np.arange(256).reshape(8, 4, 4, 2)
    groups = everyone.transpose(2, 1, 3, 0).reshape(4, 64).tolist()
    received = lax.all_to_all(
        rotated.reshape(64, 9, 4, 128), ("z", "x", "u", "c", "b"), 0, 0, axis_index_groups=groups, tiled=True
    )
    gram = four(received[:, 8].sum(axis=0), "u", 1, "c", 1) / (NX * NY * NZ)
    intersection = jnp.concatenate([gram[:, q * NORB : (q + 1) * NORB] for q in range(4)], axis=0)
    (lines,) = call(lines_kernel, [(8, NY, NX)])(received.reshape(4, 2, 8, 9, 4, 128))
    return intersection, lines


def solution(mesh):
    grid = Mesh(mesh.devices.reshape(8, 4, 2, 2, 2), ("z", "x", "u", "c", "b"))
    dom = ("z", "x", "u", "c")
    return jax.shard_map(
        local,
        mesh=grid,
        in_specs=(P("b", dom, None, None), P(dom, None, None), P()),
        out_specs=(P(), P("b", dom, None)),
        check_vma=False,
    )
```

```python
import functools

import jax
import jax.numpy as jnp
import ml_dtypes
import numpy as np
from jax import lax
from jax.experimental import pallas as pl
from jax.experimental.pallas import tpu as pltpu
from jax.sharding import Mesh
from jax.sharding import PartitionSpec as P

STENCIL = (
    -5369.0 / 1800.0,
    12.0 / 7.0,
    -15.0 / 56.0,
    10.0 / 189.0,
    -1.0 / 112.0,
    2.0 / 1925.0,
    -1.0 / 16632.0,
)
CENTER = 8.5
HALF = 6.5
WIDTH = 6
EXT = 6
NORB, NX, NY, NZ = 16, 1024, 32, 128
CHUNK = 32
OWN = 2
F32 = jnp.float32
BF16 = jnp.bfloat16


def banded(scale):
    band = np.zeros((NZ, NZ), np.float64)
    for k in range(1, 7):
        band += np.eye(NZ, k=k) * STENCIL[k] + np.eye(NZ, k=-k) * STENCIL[k]
    band = (-0.5 * scale * band).astype(np.float32)
    high = band.astype(ml_dtypes.bfloat16)
    low = (band - high.astype(np.float32)).astype(ml_dtypes.bfloat16)
    zero = np.zeros_like(high)
    return np.block([[high, low], [high, zero]]).astype(ml_dtypes.bfloat16)


def split(x):
    high = x.astype(BF16)
    low = (x - high.astype(F32)).astype(BF16)
    return high, low


def edges_kernel(place, piece_0, piece_1, piece_2, piece_3, ahead, behind):
    def copy(first, last):
        for m, piece in enumerate((piece_0, piece_1, piece_2, piece_3)):
            slab = place[1] ^ m

            @pl.when(slab == 0)
            def _():
                first[:, 0:8] = piece[...]

            @pl.when(slab == 1)
            def _():
                first[:, 8:16] = piece[...]
                last[:, 0:2] = piece[:, 6:8]

            @pl.when(slab == 2)
            def _():
                first[:, 16:18] = piece[:, 0:2]
                last[:, 2:10] = piece[...]

            @pl.when(slab == 3)
            def _():
                last[:, 10:18] = piece[...]

    @pl.when(place[0] % 2 == 1)
    def _():
        copy(behind, ahead)

    @pl.when(place[0] % 2 == 0)
    def _():
        copy(ahead, behind)


def filter_kernel(
    place, piece_0, piece_1, piece_2, piece_3, ahead, behind, own, beyond, bands,
    out, field, other, local, z, result, turned,
):
    far, near = 3 * WIDTH, 2 * WIDTH + 2
    row = lax.broadcasted_iota(jnp.int32, (8, 8, NZ), 1) % 4

    def store(target, plane, r, value):
        planes = pl.ds(plane, 8)
        target[planes, EXT + r] = value
        if r >= 8 - EXT:
            target[planes, r - (8 - EXT)] = jnp.where(row == 0, 0.0, pltpu.roll(value, 1, 1))
        if r < EXT:
            target[planes, EXT + 8 + r] = jnp.where(row == 3, 0.0, pltpu.roll(value, 7, 1))

    def tiles(sources):
        rows = [jnp.concatenate([source[(*at, pl.ds(r, 4, stride=8), slice(None))] for source, at in sources], axis=0) for r in range(8)]
        return jnp.stack(rows)

    def enter(*entries):
        values = [tiles(sources) for _, sources in entries]
        for (plane, _), value in zip(entries, values):
            field[plane, EXT : EXT + 8] = value
            field[plane, 0:EXT] = jnp.where(row[:EXT] == 0, 0.0, pltpu.roll(value[8 - EXT :], 1, 1))
            field[plane, EXT + 8 :] = jnp.where(row[:EXT] == 3, 0.0, pltpu.roll(value[:EXT], 7, 1))

    odd = place[0] % 2

    def enter_ends(p, _):
        enter(
            (odd * (far + CHUNK) + p, [(ahead, (o, p)) for o in range(OWN)]),
            ((1 - odd) * (far + CHUNK) + p, [(behind, (o, p)) for o in range(OWN)]),
        )
        return 0

    lax.fori_loop(0, far, enter_ends, 0)

    def enter_slabs(p, _):
        for pair in (((0, piece_0), (1, piece_1)), ((2, piece_2), (3, piece_3))):
            enter(*[(far + 8 * (place[1] ^ m) + p, [(piece, (o, p)) for o in range(OWN)]) for m, piece in pair])
        return 0

    lax.fori_loop(0, 8, enter_slabs, 0)

    def enter_local(p, _):
        order = [(beyond, 2), (beyond, 3), (own, 0), (own, 1), (own, 2), (own, 3), (beyond, 0), (beyond, 1)]
        for j in (0, 4):
            values = [tiles([(source, (s, p)), (source, (s, p))]) for source, s in order[j : j + 4]]
            for i, value in enumerate(values):
                local[8 * (j + i) + p] = (value + (-1.5 * STENCIL[0] - CENTER)) * (1.0 / HALF)
        return 0

    lax.fori_loop(0, 8, enter_local, 0)

    def along_z(source, index):
        high, low = split(source[pl.ds(index, 4), EXT : EXT + 8].reshape(4 * 64, NZ))
        both = jnp.dot(jnp.concatenate([high, low], axis=1), bands[...], preferred_element_type=F32)
        return (both[:, :NZ] + both[:, NZ:]).reshape(4, 8, 8, NZ)

    def step(source, shift, first, blocks, finish, put):
        def row_of(i, start, r):
            window = source[pl.ds(start + shift - WIDTH, 8 + 2 * WIDTH), EXT + r]
            total = local[pl.ds(start + 16, 8), r] * window[WIDTH : WIDTH + 8] + z[i, :, r]
            for k in range(1, 7):
                beside = window[WIDTH + k : WIDTH + 8 + k] + window[WIDTH - k : WIDTH + 8 - k]
                planes = pl.ds(start + shift, 8)
                beside = beside + (source[planes, EXT + r + k] + source[planes, EXT + r - k])
                total = total + (-0.5 / HALF * STENCIL[k]) * beside
            return finish(start, r, total)

        def body(i, _):
            start = first + 8 * i
            later = first + 8 * jnp.minimum(i + 1, blocks - 1) + shift
            last = None
            for half in range(2):
                next_z = along_z(source, later + 4 * half)
                for r in range(4 * half, 4 * half + 4):
                    value = row_of(i, start, r)
                    if last is not None:
                        put(start, r - 1, last)
                    last = value
                z[i + 1, 4 * half : 4 * half + 4] = next_z
            put(start, 7, last)
            return 0

        for half in range(2):
            z[0, 4 * half : 4 * half + 4] = along_z(source, first + shift + 4 * half)
        lax.fori_loop(0, blocks, body, 0)

    def put_first(start, r, value):
        store(other, start + near, r, value)

    def finish_second(start, r, total):
        return (total + total) - field[pl.ds(start + far, 8), EXT + r]

    def put_second(start, r, value):
        store(field, start + far, r, value)

    def finish_third(start, r, total):
        return (total + total) - other[pl.ds(start + near, 8), EXT + r]

    def put_third(start, r, value):
        result[pl.ds(start, 8), r] = value

    def outside(target, shift, count):
        blank = jnp.zeros((count, 8 + 2 * EXT, 8, NZ), F32)

        @pl.when(place[0] == 0)
        def _():
            target[shift - count : shift] = blank

        @pl.when(place[0] == NX // CHUNK - 1)
        def _():
            target[shift + CHUNK : shift + CHUNK + count] = blank

    step(field, far, -12, 7, lambda start, r, total: total, put_first)
    outside(other, near, 12)
    step(other, near, -8, 6, finish_second, put_second)
    outside(field, far, 8)
    step(field, far, 0, 4, finish_third, put_third)

    def turn(x, _):
        blocks = [
            jnp.concatenate([result[t * 8 + x, b * 4 + r] for t in range(4) for r in range(4)], axis=0) for b in range(2)
        ]
        for b in range(2):
            turned[pl.ds((b * 8 + x) * NZ, NZ), :] = blocks[b].T
        return 0

    lax.fori_loop(0, 8, turn, 0)

    def pick(i, _):
        places = [(c, b, 4 * i + q) for q in range(4) for c in range(4) for b in range(2)]
        values = [turned[pl.ds(b * 8 * NZ + 4 * q + c, 8, stride=NZ), :] for c, b, q in places]
        for (c, b, q), value in zip(places, values):
            out[c, b, q] = value
        return 0

    lax.fori_loop(0, NZ // 16, pick, 0)


exact = functools.partial(lax.dot_general, precision=lax.Precision.HIGHEST, preferred_element_type=F32)


def weights_kernel(coefficients, out):
    row = lax.broadcasted_iota(jnp.int32, (256, 256), 0)
    column = lax.broadcasted_iota(jnp.int32, (256, 256), 1)
    number = lax.broadcasted_iota(jnp.int32, (256, 16), 0)
    entry = lax.broadcasted_iota(jnp.int32, (256, 16), 1)
    before = (number // 32 * 2 + number // 4 % 2 == entry).astype(F32)
    after = (number // 16 == entry).astype(F32)
    spread = exact(before, exact(coefficients[...], after, (((1,), (1,)), ((), ()))), (((1,), (0,)), ((), ())))
    same = (row // 8 % 4 == column % 4) & (row % 4 == column // 4 % 4)
    out[...] = jnp.where(same, spread, 0.0)


def rotate_kernel(ring, weights, out):
    lane = lax.broadcasted_iota(jnp.int32, (256, 128), 1) // 32
    weights_high, weights_low = split(weights[...])
    dot = functools.partial(lax.dot_general, preferred_element_type=F32)
    right = (((1,), (0,)), ((), ()))
    rows_out = (((0,), (0,)), ((), ()))
    straight, cross = jnp.zeros((256, 256), F32), jnp.zeros((256, 256), F32)
    for t in range(4):
        halves = []
        for b in range(2):
            value = None
            for c in range(4):
                piece = ring[c * 2 + b]
                if c != t:
                    piece = pltpu.roll(piece, ((c - t) % 4) * 32, 1)
                value = piece if value is None else jnp.where(lane == c, piece, value)
            halves.append(value)
        all_orbitals = jnp.concatenate(halves, axis=1)
        high, low = split(all_orbitals)
        turned = dot(high, weights_high, right) + (dot(high, weights_low, right) + dot(low, weights_high, right))
        for b in range(2):
            rows = turned[:, b * 128 : (b + 1) * 128].reshape(8, 4, 8, 128)
            for x in range(4):
                out[x, b, :, 2 * t] = rows[:, x, 0:4]
                out[x, b, :, 2 * t + 1] = rows[:, x, 4:8]
        straight = straight + dot(high, high, rows_out)
        cross = cross + dot(high, low, rows_out)
    row = lax.broadcasted_iota(jnp.int32, (256, 256), 0)
    column = lax.broadcasted_iota(jnp.int32, (256, 256), 1)
    same = (row // 8 % 4 == column // 8 % 4) & (row % 4 == column % 4)
    diagonal = jnp.where(same, straight + (cross + cross.T), 0.0).reshape(8, 4, 8, 256).sum(axis=1).reshape(64, 256)
    number = lax.broadcasted_iota(jnp.int32, (256, 16), 0)
    entry = lax.broadcasted_iota(jnp.int32, (256, 16), 1)
    columns = (number // 32 * 2 + number // 4 % 2 == entry).astype(F32)
    number, entry = number[:64], entry[:64]
    rows = (number // 8 * 2 + number // 4 % 2 == entry).astype(F32)
    both = exact(rows, exact(diagonal, columns, (((1,), (0,)), ((), ()))), (((0,), (0,)), ((), ())))
    tile = jnp.concatenate([both[4 * q : 4 * q + 4] for q in range(4)] + [jnp.zeros((4, 64), F32)], axis=1)
    out[:, :, :, 8] = jnp.broadcast_to(tile, (4, 2, 8, 4, 128))


def lines_kernel(received, out):
    low = lax.broadcasted_iota(jnp.int32, (16, 8, 128), 1) < 4

    def lines(s, b):
        pieces = [
            jnp.concatenate([received[c, b, s, 2 * j], received[c, b, s, 2 * j + 1]], axis=0)
            for c in range(4)
            for j in range(4)
        ]
        return jnp.concatenate(pieces, axis=0).T.reshape(16, 8, 128)

    for s in range(8):
        first, second = lines(s, 0), lines(s, 1)
        even = jnp.where(low, first, pltpu.roll(second, 4, 1)).reshape(8, 2, 8, 128)
        odd = jnp.where(low, pltpu.roll(first, 4, 1), second).reshape(8, 2, 8, 128)
        for q in range(2):
            out[:, q * 16 : q * 16 + 8, s * 128 : (s + 1) * 128] = even[:, q]
            out[:, q * 16 + 8 : q * 16 + 16, s * 128 : (s + 1) * 128] = odd[:, q]


def call(kernel, out, scratch=()):
    vmem = pl.BlockSpec(memory_space=pltpu.VMEM)
    smem = pl.BlockSpec(memory_space=pltpu.SMEM)
    return lambda *args: pl.pallas_call(
        kernel,
        out_shape=[jax.ShapeDtypeStruct(s, F32) for s in out],
        in_specs=[smem if a.dtype == jnp.int32 else vmem for a in args],
        out_specs=[vmem] * len(out),
        scratch_shapes=[pltpu.VMEM(s, F32) for s in scratch],
        compiler_params=pltpu.CompilerParams(vmem_limit_bytes=48 * 1024 * 1024),
    )(*args)


def four(x, one, one_bit, two, two_bit):
    def swap(axes, bits):
        sizes = [lax.axis_size(a) for a in axes]
        flat = [np.ravel_multi_index([i ^ b for i, b in zip(at, bits)], sizes) for at in np.ndindex(*sizes)]
        return lax.ppermute(x, axes, [(i, int(j)) for i, j in enumerate(flat)])

    if one == two:
        parts = [swap((one,), (bits,)) for bits in (one_bit, two_bit, one_bit ^ two_bit)]
    else:
        parts = [swap((one, two), bits) for bits in ((one_bit, 0), (0, two_bit), (one_bit, two_bit))]
    return (x + parts[0]) + (parts[1] + parts[2])


def local(orbitals, potential, coefficients):
    chunks = ("z", "x")
    dom = ("z", "x", "u", "c")
    count = lax.axis_size(chunks)

    shift = [(d, d + 4 if d % 4 >= 2 else d - 4) for d in range(4 * count)]
    beyond = lax.ppermute(potential, dom, [(i, j) for i, j in shift if 0 <= j < 4 * count])
    group = lax.axis_index(("u", "c"))
    pieces = {}
    for m in (2, 3, 1):
        if m == 3:
            orbitals, piece = lax.optimization_barrier((orbitals, piece))
            pieces[2] = lax.ppermute(piece, ("u", "c"), [(i, i ^ 2) for i in range(4)])
        piece = lax.dynamic_slice_in_dim(orbitals, OWN * (group ^ m), OWN, 0)
        if m != 2:
            pieces[m] = lax.ppermute(piece, ("u", "c"), [(i, i ^ m) for i in range(4)])
    pieces[0] = lax.dynamic_slice_in_dim(orbitals, OWN * group, OWN, 0)
    (weights,) = call(weights_kernel, [(256, 256)])(coefficients)
    pieces, beyond, weights = lax.optimization_barrier(([pieces[m] for m in range(4)], beyond, weights))
    far = 3 * WIDTH
    chunk = lax.axis_index(chunks)
    place = jnp.stack([chunk, group])
    ahead, behind = call(edges_kernel, [(OWN, far, NY, NZ)] * 2)(place, *pieces)
    swaps = [[(i, j) for k in range(s, count - 1, 2) for i, j in ((k, k + 1), (k + 1, k))] for s in (1, 0)]
    ahead = lax.ppermute(ahead, chunks, swaps[0])
    behind = lax.ppermute(behind, chunks, swaps[1])
    own = lax.all_gather(potential, ("u", "c"))
    beyond = lax.all_gather(beyond, ("u", "c"))

    scratch = [
        (CHUNK + 2 * far, 8 + 2 * EXT, 8, NZ),
        (CHUNK + 2 * (2 * WIDTH + 2), 8 + 2 * EXT, 8, NZ),
        (64, 8, 8, NZ),
        (8, 8, 8, 8, NZ),
        (CHUNK, 8, 8, NZ),
        (2 * 8 * NZ, NZ),
    ]
    bands = jnp.asarray(banded(1.0 / HALF))
    (message,) = call(filter_kernel, [(4, 2, 32, 8, 128)], scratch)(
        place, *pieces, ahead, behind, own, beyond, bands
    )
    ring = lax.all_to_all(message.reshape(8, 256, 128), ("u", "c", "b"), 0, 0, tiled=True)
    (rotated,) = call(rotate_kernel, [(4, 2, 8, 9, 4, 128)])(ring, weights)
    everyone = np.arange(256).reshape(8, 4, 4, 2)
    groups = everyone.transpose(2, 1, 3, 0).reshape(4, 64).tolist()
    received = lax.all_to_all(
        rotated.reshape(64, 9, 4, 128), ("z", "x", "u", "c", "b"), 0, 0, axis_index_groups=groups, tiled=True
    )
    gram = four(received[:, 8].sum(axis=0), "u", 1, "c", 1) / (NX * NY * NZ)
    intersection = jnp.concatenate([gram[:, q * NORB : (q + 1) * NORB] for q in range(4)], axis=0)
    (lines,) = call(lines_kernel, [(8, NY, NX)])(received.reshape(4, 2, 8, 9, 4, 128))
    return intersection, lines


def solution(mesh):
    grid = Mesh(mesh.devices.reshape(8, 4, 2, 2, 2), ("z", "x", "u", "c", "b"))
    dom = ("z", "x", "u", "c")
    return jax.shard_map(
        local,
        mesh=grid,
        in_specs=(P("b", dom, None, None), P(dom, None, None), P()),
        out_specs=(P(), P("b", dom, None)),
        check_vma=False,
    )
```

```python
import functools

import jax
import jax.numpy as jnp
import ml_dtypes
import numpy as np
from jax import lax
from jax.experimental import pallas as pl
from jax.experimental.pallas import tpu as pltpu
from jax.sharding import Mesh
from jax.sharding import PartitionSpec as P

STENCIL = (
    -5369.0 / 1800.0,
    12.0 / 7.0,
    -15.0 / 56.0,
    10.0 / 189.0,
    -1.0 / 112.0,
    2.0 / 1925.0,
    -1.0 / 16632.0,
)
CENTER = 8.5
HALF = 6.5
WIDTH = 6
EXT = 6
NORB, NX, NY, NZ = 16, 1024, 32, 128
CHUNK = 32
OWN = 2
F32 = jnp.float32
BF16 = jnp.bfloat16


def banded(scale):
    band = np.zeros((NZ, NZ), np.float64)
    for k in range(1, 7):
        band += np.eye(NZ, k=k) * STENCIL[k] + np.eye(NZ, k=-k) * STENCIL[k]
    band = (-0.5 * scale * band).astype(np.float32)
    high = band.astype(ml_dtypes.bfloat16)
    low = (band - high.astype(np.float32)).astype(ml_dtypes.bfloat16)
    zero = np.zeros_like(high)
    return np.block([[high, low], [high, zero]]).astype(ml_dtypes.bfloat16)


def split(x):
    high = x.astype(BF16)
    low = (x - high.astype(F32)).astype(BF16)
    return high, low


def edges_kernel(place, piece_0, piece_1, piece_2, piece_3, ahead, behind):
    def copy(first, last):
        for m, piece in enumerate((piece_0, piece_1, piece_2, piece_3)):
            slab = place[1] ^ m

            @pl.when(slab == 0)
            def _():
                first[:, 0:8] = piece[...]

            @pl.when(slab == 1)
            def _():
                first[:, 8:16] = piece[...]
                last[:, 0:2] = piece[:, 6:8]

            @pl.when(slab == 2)
            def _():
                first[:, 16:18] = piece[:, 0:2]
                last[:, 2:10] = piece[...]

            @pl.when(slab == 3)
            def _():
                last[:, 10:18] = piece[...]

    @pl.when(place[0] % 2 == 1)
    def _():
        copy(behind, ahead)

    @pl.when(place[0] % 2 == 0)
    def _():
        copy(ahead, behind)


def filter_kernel(
    place, piece_0, piece_1, piece_2, piece_3, ahead, behind,
    own_0, own_1, own_2, own_3, beyond_0, beyond_1, beyond_2, beyond_3, bands,
    out, field, other, local, z, result, turned,
):
    far, near = 3 * WIDTH, 2 * WIDTH + 2
    row = lax.broadcasted_iota(jnp.int32, (8, 8, NZ), 1) % 4

    def store(target, plane, r, value):
        planes = pl.ds(plane, 8)
        target[planes, EXT + r] = value
        if r >= 8 - EXT:
            target[planes, r - (8 - EXT)] = jnp.where(row == 0, 0.0, pltpu.roll(value, 1, 1))
        if r < EXT:
            target[planes, EXT + 8 + r] = jnp.where(row == 3, 0.0, pltpu.roll(value, 7, 1))

    def tiles(sources):
        rows = [jnp.concatenate([source[(*at, pl.ds(r, 4, stride=8), slice(None))] for source, at in sources], axis=0) for r in range(8)]
        return jnp.stack(rows)

    def enter(*entries):
        values = [tiles(sources) for _, sources in entries]
        for (plane, _), value in zip(entries, values):
            field[plane, EXT : EXT + 8] = value
            field[plane, 0:EXT] = jnp.where(row[:EXT] == 0, 0.0, pltpu.roll(value[8 - EXT :], 1, 1))
            field[plane, EXT + 8 :] = jnp.where(row[:EXT] == 3, 0.0, pltpu.roll(value[:EXT], 7, 1))

    odd = place[0] % 2

    def enter_ends(p, _):
        enter(
            (odd * (far + CHUNK) + p, [(ahead, (o, p)) for o in range(OWN)]),
            ((1 - odd) * (far + CHUNK) + p, [(behind, (o, p)) for o in range(OWN)]),
        )
        return 0

    lax.fori_loop(0, far, enter_ends, 0)

    def enter_slabs(p, _):
        for pair in (((0, piece_0), (1, piece_1)), ((2, piece_2), (3, piece_3))):
            enter(*[(far + 8 * (place[1] ^ m) + p, [(piece, (o, p)) for o in range(OWN)]) for m, piece in pair])
        return 0

    lax.fori_loop(0, 8, enter_slabs, 0)

    def enter_local(p, _):
        for first, sources in ((2, (own_0, own_1, own_2, own_3)), (6, (beyond_0, beyond_1, beyond_2, beyond_3))):
            values = [tiles([(source, (p,)), (source, (p,))]) for source in sources]
            for m, value in enumerate(values):
                start = 8 * ((first + (place[1] ^ m)) % 8)
                local[start + p] = (value + (-1.5 * STENCIL[0] - CENTER)) * (1.0 / HALF)
        return 0

    lax.fori_loop(0, 8, enter_local, 0)

    def along_z(source, index):
        high, low = split(source[pl.ds(index, 4), EXT : EXT + 8].reshape(4 * 64, NZ))
        both = jnp.dot(jnp.concatenate([high, low], axis=1), bands[...], preferred_element_type=F32)
        return (both[:, :NZ] + both[:, NZ:]).reshape(4, 8, 8, NZ)

    def step(source, shift, first, blocks, finish, put):
        def row_of(i, start, r):
            window = source[pl.ds(start + shift - WIDTH, 8 + 2 * WIDTH), EXT + r]
            total = local[pl.ds(start + 16, 8), r] * window[WIDTH : WIDTH + 8] + z[i, :, r]
            for k in range(1, 7):
                beside = window[WIDTH + k : WIDTH + 8 + k] + window[WIDTH - k : WIDTH + 8 - k]
                planes = pl.ds(start + shift, 8)
                beside = beside + (source[planes, EXT + r + k] + source[planes, EXT + r - k])
                total = total + (-0.5 / HALF * STENCIL[k]) * beside
            return finish(start, r, total)

        def body(i, _):
            start = first + 8 * i
            later = first + 8 * jnp.minimum(i + 1, blocks - 1) + shift
            last = None
            for half in range(2):
                next_z = along_z(source, later + 4 * half)
                for r in range(4 * half, 4 * half + 4):
                    value = row_of(i, start, r)
                    if last is not None:
                        put(start, r - 1, last)
                    last = value
                z[i + 1, 4 * half : 4 * half + 4] = next_z
            put(start, 7, last)
            return 0

        for half in range(2):
            z[0, 4 * half : 4 * half + 4] = along_z(source, first + shift + 4 * half)
        lax.fori_loop(0, blocks, body, 0)

    def put_first(start, r, value):
        store(other, start + near, r, value)

    def finish_second(start, r, total):
        return (total + total) - field[pl.ds(start + far, 8), EXT + r]

    def put_second(start, r, value):
        store(field, start + far, r, value)

    def finish_third(start, r, total):
        return (total + total) - other[pl.ds(start + near, 8), EXT + r]

    def put_third(start, r, value):
        result[pl.ds(start, 8), r] = value

    def outside(target, shift, count):
        blank = jnp.zeros((count, 8 + 2 * EXT, 8, NZ), F32)

        @pl.when(place[0] == 0)
        def _():
            target[shift - count : shift] = blank

        @pl.when(place[0] == NX // CHUNK - 1)
        def _():
            target[shift + CHUNK : shift + CHUNK + count] = blank

    step(field, far, -12, 7, lambda start, r, total: total, put_first)
    outside(other, near, 12)
    step(other, near, -8, 6, finish_second, put_second)
    outside(field, far, 8)
    step(field, far, 0, 4, finish_third, put_third)

    def turn(x, _):
        blocks = [
            jnp.concatenate([result[t * 8 + x, b * 4 + r] for t in range(4) for r in range(4)], axis=0) for b in range(2)
        ]
        for b in range(2):
            turned[pl.ds((b * 8 + x) * NZ, NZ), :] = blocks[b].T
        return 0

    lax.fori_loop(0, 8, turn, 0)

    def pick(i, _):
        places = [(c, b, 4 * i + q) for q in range(4) for c in range(4) for b in range(2)]
        values = [turned[pl.ds(b * 8 * NZ + 4 * q + c, 8, stride=NZ), :] for c, b, q in places]
        for (c, b, q), value in zip(places, values):
            out[c, b, q] = value
        return 0

    lax.fori_loop(0, NZ // 16, pick, 0)


exact = functools.partial(lax.dot_general, precision=lax.Precision.HIGHEST, preferred_element_type=F32)


def weights_kernel(coefficients, out):
    row = lax.broadcasted_iota(jnp.int32, (256, 256), 0)
    column = lax.broadcasted_iota(jnp.int32, (256, 256), 1)
    number = lax.broadcasted_iota(jnp.int32, (256, 16), 0)
    entry = lax.broadcasted_iota(jnp.int32, (256, 16), 1)
    before = (number // 32 * 2 + number // 4 % 2 == entry).astype(F32)
    after = (number // 16 == entry).astype(F32)
    spread = exact(before, exact(coefficients[...], after, (((1,), (1,)), ((), ()))), (((1,), (0,)), ((), ())))
    same = (row // 8 % 4 == column % 4) & (row % 4 == column // 4 % 4)
    out[...] = jnp.where(same, spread, 0.0)


def rotate_kernel(ring, weights, out):
    lane = lax.broadcasted_iota(jnp.int32, (256, 128), 1) // 32
    weights_high, weights_low = split(weights[...])
    dot = functools.partial(lax.dot_general, preferred_element_type=F32)
    right = (((1,), (0,)), ((), ()))
    rows_out = (((0,), (0,)), ((), ()))
    straight, cross = jnp.zeros((256, 256), F32), jnp.zeros((256, 256), F32)
    for t in range(4):
        halves = []
        for b in range(2):
            value = None
            for c in range(4):
                piece = ring[c * 2 + b]
                if c != t:
                    piece = pltpu.roll(piece, ((c - t) % 4) * 32, 1)
                value = piece if value is None else jnp.where(lane == c, piece, value)
            halves.append(value)
        all_orbitals = jnp.concatenate(halves, axis=1)
        high, low = split(all_orbitals)
        turned = dot(high, weights_high, right) + (dot(high, weights_low, right) + dot(low, weights_high, right))
        for b in range(2):
            rows = turned[:, b * 128 : (b + 1) * 128].reshape(8, 4, 8, 128)
            for x in range(4):
                out[x, b, :, 2 * t] = rows[:, x, 0:4]
                out[x, b, :, 2 * t + 1] = rows[:, x, 4:8]
        straight = straight + dot(high, high, rows_out)
        cross = cross + dot(high, low, rows_out)
    row = lax.broadcasted_iota(jnp.int32, (256, 256), 0)
    column = lax.broadcasted_iota(jnp.int32, (256, 256), 1)
    same = (row // 8 % 4 == column // 8 % 4) & (row % 4 == column % 4)
    diagonal = jnp.where(same, straight + (cross + cross.T), 0.0).reshape(8, 4, 8, 256).sum(axis=1).reshape(64, 256)
    number = lax.broadcasted_iota(jnp.int32, (256, 16), 0)
    entry = lax.broadcasted_iota(jnp.int32, (256, 16), 1)
    columns = (number // 32 * 2 + number // 4 % 2 == entry).astype(F32)
    number, entry = number[:64], entry[:64]
    rows = (number // 8 * 2 + number // 4 % 2 == entry).astype(F32)
    both = exact(rows, exact(diagonal, columns, (((1,), (0,)), ((), ()))), (((0,), (0,)), ((), ())))
    tile = jnp.concatenate([both[4 * q : 4 * q + 4] for q in range(4)] + [jnp.zeros((4, 64), F32)], axis=1)
    out[:, :, :, 8] = jnp.broadcast_to(tile, (4, 2, 8, 4, 128))


def lines_kernel(received, out):
    low = lax.broadcasted_iota(jnp.int32, (16, 8, 128), 1) < 4

    def lines(s, b):
        pieces = [
            jnp.concatenate([received[c, b, s, 2 * j], received[c, b, s, 2 * j + 1]], axis=0)
            for c in range(4)
            for j in range(4)
        ]
        return jnp.concatenate(pieces, axis=0).T.reshape(16, 8, 128)

    for s in range(8):
        first, second = lines(s, 0), lines(s, 1)
        even = jnp.where(low, first, pltpu.roll(second, 4, 1)).reshape(8, 2, 8, 128)
        odd = jnp.where(low, pltpu.roll(first, 4, 1), second).reshape(8, 2, 8, 128)
        for q in range(2):
            out[:, q * 16 : q * 16 + 8, s * 128 : (s + 1) * 128] = even[:, q]
            out[:, q * 16 + 8 : q * 16 + 16, s * 128 : (s + 1) * 128] = odd[:, q]


def call(kernel, out, scratch=()):
    vmem = pl.BlockSpec(memory_space=pltpu.VMEM)
    smem = pl.BlockSpec(memory_space=pltpu.SMEM)
    return lambda *args: pl.pallas_call(
        kernel,
        out_shape=[jax.ShapeDtypeStruct(s, F32) for s in out],
        in_specs=[smem if a.dtype == jnp.int32 else vmem for a in args],
        out_specs=[vmem] * len(out),
        scratch_shapes=[pltpu.VMEM(s, F32) for s in scratch],
        compiler_params=pltpu.CompilerParams(vmem_limit_bytes=48 * 1024 * 1024),
    )(*args)


def four(x, one, one_bit, two, two_bit):
    def swap(axes, bits):
        sizes = [lax.axis_size(a) for a in axes]
        flat = [np.ravel_multi_index([i ^ b for i, b in zip(at, bits)], sizes) for at in np.ndindex(*sizes)]
        return lax.ppermute(x, axes, [(i, int(j)) for i, j in enumerate(flat)])

    if one == two:
        parts = [swap((one,), (bits,)) for bits in (one_bit, two_bit, one_bit ^ two_bit)]
    else:
        parts = [swap((one, two), bits) for bits in ((one_bit, 0), (0, two_bit), (one_bit, two_bit))]
    return (x + parts[0]) + (parts[1] + parts[2])


def local(orbitals, potential, coefficients):
    chunks = ("z", "x")
    dom = ("z", "x", "u", "c")
    count = lax.axis_size(chunks)

    shift = [(d, d + 4 if d % 4 >= 2 else d - 4) for d in range(4 * count)]
    beyond = lax.ppermute(potential, dom, [(i, j) for i, j in shift if 0 <= j < 4 * count])
    group = lax.axis_index(("u", "c"))
    pieces = {}
    for m in (2, 3, 1):
        if m == 3:
            orbitals, piece = lax.optimization_barrier((orbitals, piece))
            pieces[2] = lax.ppermute(piece, ("u", "c"), [(i, i ^ 2) for i in range(4)])
        piece = lax.dynamic_slice_in_dim(orbitals, OWN * (group ^ m), OWN, 0)
        if m != 2:
            pieces[m] = lax.ppermute(piece, ("u", "c"), [(i, i ^ m) for i in range(4)])
    pieces[0] = lax.dynamic_slice_in_dim(orbitals, OWN * group, OWN, 0)
    (weights,) = call(weights_kernel, [(256, 256)])(coefficients)
    pieces, beyond, potential, weights = lax.optimization_barrier(
        ([pieces[m] for m in range(4)], beyond, potential, weights)
    )
    far = 3 * WIDTH
    chunk = lax.axis_index(chunks)
    place = jnp.stack([chunk, group])
    ahead, behind = call(edges_kernel, [(OWN, far, NY, NZ)] * 2)(place, *pieces)
    ahead, behind, beyond, potential = lax.optimization_barrier((ahead, behind, beyond, potential))
    swaps = [[(i, j) for k in range(s, count - 1, 2) for i, j in ((k, k + 1), (k + 1, k))] for s in (1, 0)]
    ahead = lax.ppermute(ahead, chunks, swaps[0])
    behind = lax.ppermute(behind, chunks, swaps[1])

    def of_group(x):
        return [x] + [lax.ppermute(x, ("u", "c"), [(i, i ^ m) for i in range(4)]) for m in (1, 2, 3)]

    own, beyond = of_group(potential), of_group(beyond)
    scratch = [
        (CHUNK + 2 * far, 8 + 2 * EXT, 8, NZ),
        (CHUNK + 2 * (2 * WIDTH + 2), 8 + 2 * EXT, 8, NZ),
        (64, 8, 8, NZ),
        (8, 8, 8, 8, NZ),
        (CHUNK, 8, 8, NZ),
        (2 * 8 * NZ, NZ),
    ]
    bands = jnp.asarray(banded(1.0 / HALF))
    (message,) = call(filter_kernel, [(4, 2, 32, 8, 128)], scratch)(
        place, *pieces, ahead, behind, *own, *beyond, bands
    )
    ring = lax.all_to_all(message.reshape(8, 256, 128), ("u", "c", "b"), 0, 0, tiled=True)
    (rotated,) = call(rotate_kernel, [(4, 2, 8, 9, 4, 128)])(ring, weights)
    everyone = np.arange(256).reshape(8, 4, 4, 2)
    groups = everyone.transpose(2, 1, 3, 0).reshape(4, 64).tolist()
    received = lax.all_to_all(
        rotated.reshape(64, 9, 4, 128), ("z", "x", "u", "c", "b"), 0, 0, axis_index_groups=groups, tiled=True
    )
    gram = four(received[:, 8].sum(axis=0), "u", 1, "c", 1) / (NX * NY * NZ)
    intersection = jnp.concatenate([gram[:, q * NORB : (q + 1) * NORB] for q in range(4)], axis=0)
    (lines,) = call(lines_kernel, [(8, NY, NX)])(received.reshape(4, 2, 8, 9, 4, 128))
    return intersection, lines


def solution(mesh):
    grid = Mesh(mesh.devices.reshape(8, 4, 2, 2, 2), ("z", "x", "u", "c", "b"))
    dom = ("z", "x", "u", "c")
    return jax.shard_map(
        local,
        mesh=grid,
        in_specs=(P("b", dom, None, None), P(dom, None, None), P()),
        out_specs=(P(), P("b", dom, None)),
        check_vma=False,
    )
```

```python
import functools

import jax
import jax.numpy as jnp
import ml_dtypes
import numpy as np
from jax import lax
from jax.experimental import pallas as pl
from jax.experimental.pallas import tpu as pltpu
from jax.sharding import Mesh
from jax.sharding import PartitionSpec as P

STENCIL = (
    -5369.0 / 1800.0,
    12.0 / 7.0,
    -15.0 / 56.0,
    10.0 / 189.0,
    -1.0 / 112.0,
    2.0 / 1925.0,
    -1.0 / 16632.0,
)
CENTER = 8.5
HALF = 6.5
WIDTH = 6
EXT = 6
NORB, NX, NY, NZ = 16, 1024, 32, 128
CHUNK = 32
OWN = 2
F32 = jnp.float32
BF16 = jnp.bfloat16


def banded(scale):
    band = np.zeros((NZ, NZ), np.float64)
    for k in range(1, 7):
        band += np.eye(NZ, k=k) * STENCIL[k] + np.eye(NZ, k=-k) * STENCIL[k]
    band = (-0.5 * scale * band).astype(np.float32)
    high = band.astype(ml_dtypes.bfloat16)
    low = (band - high.astype(np.float32)).astype(ml_dtypes.bfloat16)
    zero = np.zeros_like(high)
    return np.block([[high, low], [high, zero]]).astype(ml_dtypes.bfloat16)


def split(x):
    high = x.astype(BF16)
    low = (x - high.astype(F32)).astype(BF16)
    return high, low


def edges_kernel(place, piece_0, piece_1, piece_2, piece_3, ahead, behind):
    def copy(first, last):
        for m, piece in enumerate((piece_0, piece_1, piece_2, piece_3)):
            slab = place[1] ^ m

            @pl.when(slab == 0)
            def _():
                first[:, 0:8] = piece[...]

            @pl.when(slab == 1)
            def _():
                first[:, 8:16] = piece[...]
                last[:, 0:2] = piece[:, 6:8]

            @pl.when(slab == 2)
            def _():
                first[:, 16:18] = piece[:, 0:2]
                last[:, 2:10] = piece[...]

            @pl.when(slab == 3)
            def _():
                last[:, 10:18] = piece[...]

    @pl.when(place[0] % 2 == 1)
    def _():
        copy(behind, ahead)

    @pl.when(place[0] % 2 == 0)
    def _():
        copy(ahead, behind)


def filter_kernel(
    place, piece_0, piece_1, piece_2, piece_3, ahead, behind,
    own_0, own_1, own_2, own_3, beyond_0, beyond_1, beyond_2, beyond_3, bands,
    out, field, other, local, z, result, turned,
):
    far, near = 3 * WIDTH, 2 * WIDTH + 2
    row = lax.broadcasted_iota(jnp.int32, (8, 8, NZ), 1) % 4

    def store(target, plane, r, value):
        planes = pl.ds(plane, 8)
        target[planes, EXT + r] = value
        if r >= 8 - EXT:
            target[planes, r - (8 - EXT)] = jnp.where(row == 0, 0.0, pltpu.roll(value, 1, 1))
        if r < EXT:
            target[planes, EXT + 8 + r] = jnp.where(row == 3, 0.0, pltpu.roll(value, 7, 1))

    def tiles(sources):
        rows = [jnp.concatenate([source[(*at, pl.ds(r, 4, stride=8), slice(None))] for source, at in sources], axis=0) for r in range(8)]
        return jnp.stack(rows)

    def enter(*entries):
        values = [tiles(sources) for _, sources in entries]
        for (plane, _), value in zip(entries, values):
            field[plane, EXT : EXT + 8] = value
            field[plane, 0:EXT] = jnp.where(row[:EXT] == 0, 0.0, pltpu.roll(value[8 - EXT :], 1, 1))
            field[plane, EXT + 8 :] = jnp.where(row[:EXT] == 3, 0.0, pltpu.roll(value[:EXT], 7, 1))

    odd = place[0] % 2

    def enter_ends(p, _):
        enter(
            (odd * (far + CHUNK) + p, [(ahead, (o, p)) for o in range(OWN)]),
            ((1 - odd) * (far + CHUNK) + p, [(behind, (o, p)) for o in range(OWN)]),
        )
        return 0

    lax.fori_loop(0, far, enter_ends, 0, unroll=3)

    def enter_slabs(p, _):
        for pair in (((0, piece_0), (1, piece_1)), ((2, piece_2), (3, piece_3))):
            enter(*[(far + 8 * (place[1] ^ m) + p, [(piece, (o, p)) for o in range(OWN)]) for m, piece in pair])
        return 0

    lax.fori_loop(0, 8, enter_slabs, 0, unroll=2)

    def enter_local(p, _):
        for first, sources in ((2, (own_0, own_1, own_2, own_3)), (6, (beyond_0, beyond_1, beyond_2, beyond_3))):
            values = [tiles([(source, (p,)), (source, (p,))]) for source in sources]
            for m, value in enumerate(values):
                start = 8 * ((first + (place[1] ^ m)) % 8)
                local[start + p] = (value + (-1.5 * STENCIL[0] - CENTER)) * (1.0 / HALF)
        return 0

    lax.fori_loop(0, 8, enter_local, 0, unroll=2)

    def along_z(source, index):
        high, low = split(source[pl.ds(index, 4), EXT : EXT + 8].reshape(4 * 64, NZ))
        both = jnp.dot(jnp.concatenate([high, low], axis=1), bands[...], preferred_element_type=F32)
        return (both[:, :NZ] + both[:, NZ:]).reshape(4, 8, 8, NZ)

    def step(source, shift, first, blocks, finish, put):
        def row_of(i, start, r):
            window = source[pl.ds(start + shift - WIDTH, 8 + 2 * WIDTH), EXT + r]
            total = local[pl.ds(start + 16, 8), r] * window[WIDTH : WIDTH + 8] + z[i, :, r]
            for k in range(1, 7):
                beside = window[WIDTH + k : WIDTH + 8 + k] + window[WIDTH - k : WIDTH + 8 - k]
                planes = pl.ds(start + shift, 8)
                beside = beside + (source[planes, EXT + r + k] + source[planes, EXT + r - k])
                total = total + (-0.5 / HALF * STENCIL[k]) * beside
            return finish(start, r, total)

        def body(i, _):
            start = first + 8 * i
            later = first + 8 * jnp.minimum(i + 1, blocks - 1) + shift
            last = None
            for half in range(2):
                next_z = along_z(source, later + 4 * half)
                for r in range(4 * half, 4 * half + 4):
                    value = row_of(i, start, r)
                    if last is not None:
                        put(start, r - 1, last)
                    last = value
                z[i + 1, 4 * half : 4 * half + 4] = next_z
            put(start, 7, last)
            return 0

        for half in range(2):
            z[0, 4 * half : 4 * half + 4] = along_z(source, first + shift + 4 * half)
        lax.fori_loop(0, blocks, body, 0)

    def put_first(start, r, value):
        store(other, start + near, r, value)

    def finish_second(start, r, total):
        return (total + total) - field[pl.ds(start + far, 8), EXT + r]

    def put_second(start, r, value):
        store(field, start + far, r, value)

    def finish_third(start, r, total):
        return (total + total) - other[pl.ds(start + near, 8), EXT + r]

    def put_third(start, r, value):
        result[pl.ds(start, 8), r] = value

    def outside(target, shift, count):
        blank = jnp.zeros((count, 8 + 2 * EXT, 8, NZ), F32)

        @pl.when(place[0] == 0)
        def _():
            target[shift - count : shift] = blank

        @pl.when(place[0] == NX // CHUNK - 1)
        def _():
            target[shift + CHUNK : shift + CHUNK + count] = blank

    step(field, far, -12, 7, lambda start, r, total: total, put_first)
    outside(other, near, 12)
    step(other, near, -8, 6, finish_second, put_second)
    outside(field, far, 8)
    step(field, far, 0, 4, finish_third, put_third)

    def turn(x, _):
        blocks = [
            jnp.concatenate([result[t * 8 + x, b * 4 + r] for t in range(4) for r in range(4)], axis=0) for b in range(2)
        ]
        for b in range(2):
            turned[pl.ds((b * 8 + x) * NZ, NZ), :] = blocks[b].T
        return 0

    lax.fori_loop(0, 8, turn, 0, unroll=2)

    def pick(i, _):
        places = [(c, b, 4 * i + q) for q in range(4) for c in range(4) for b in range(2)]
        values = [turned[pl.ds(b * 8 * NZ + 4 * q + c, 8, stride=NZ), :] for c, b, q in places]
        for (c, b, q), value in zip(places, values):
            out[c, b, q] = value
        return 0

    lax.fori_loop(0, NZ // 16, pick, 0, unroll=2)


exact = functools.partial(lax.dot_general, precision=lax.Precision.HIGHEST, preferred_element_type=F32)


def weights_kernel(coefficients, out):
    row = lax.broadcasted_iota(jnp.int32, (256, 256), 0)
    column = lax.broadcasted_iota(jnp.int32, (256, 256), 1)
    number = lax.broadcasted_iota(jnp.int32, (256, 16), 0)
    entry = lax.broadcasted_iota(jnp.int32, (256, 16), 1)
    before = (number // 32 * 2 + number // 4 % 2 == entry).astype(F32)
    after = (number // 16 == entry).astype(F32)
    spread = exact(before, exact(coefficients[...], after, (((1,), (1,)), ((), ()))), (((1,), (0,)), ((), ())))
    same = (row // 8 % 4 == column % 4) & (row % 4 == column // 4 % 4)
    out[...] = jnp.where(same, spread, 0.0)


def rotate_kernel(ring, weights, out):
    lane = lax.broadcasted_iota(jnp.int32, (256, 128), 1) // 32
    weights_high, weights_low = split(weights[...])
    dot = functools.partial(lax.dot_general, preferred_element_type=F32)
    right = (((1,), (0,)), ((), ()))
    rows_out = (((0,), (0,)), ((), ()))
    straight, cross = jnp.zeros((256, 256), F32), jnp.zeros((256, 256), F32)
    for t in range(4):
        halves = []
        for b in range(2):
            value = None
            for c in range(4):
                piece = ring[c * 2 + b]
                if c != t:
                    piece = pltpu.roll(piece, ((c - t) % 4) * 32, 1)
                value = piece if value is None else jnp.where(lane == c, piece, value)
            halves.append(value)
        all_orbitals = jnp.concatenate(halves, axis=1)
        high, low = split(all_orbitals)
        turned = dot(high, weights_high, right) + (dot(high, weights_low, right) + dot(low, weights_high, right))
        for b in range(2):
            rows = turned[:, b * 128 : (b + 1) * 128].reshape(8, 4, 8, 128)
            for x in range(4):
                out[x, b, :, 2 * t] = rows[:, x, 0:4]
                out[x, b, :, 2 * t + 1] = rows[:, x, 4:8]
        straight = straight + dot(high, high, rows_out)
        cross = cross + dot(high, low, rows_out)
    row = lax.broadcasted_iota(jnp.int32, (256, 256), 0)
    column = lax.broadcasted_iota(jnp.int32, (256, 256), 1)
    same = (row // 8 % 4 == column // 8 % 4) & (row % 4 == column % 4)
    diagonal = jnp.where(same, straight + (cross + cross.T), 0.0).reshape(8, 4, 8, 256).sum(axis=1).reshape(64, 256)
    number = lax.broadcasted_iota(jnp.int32, (256, 16), 0)
    entry = lax.broadcasted_iota(jnp.int32, (256, 16), 1)
    columns = (number // 32 * 2 + number // 4 % 2 == entry).astype(F32)
    number, entry = number[:64], entry[:64]
    rows = (number // 8 * 2 + number // 4 % 2 == entry).astype(F32)
    both = exact(rows, exact(diagonal, columns, (((1,), (0,)), ((), ()))), (((0,), (0,)), ((), ())))
    tile = jnp.concatenate([both[4 * q : 4 * q + 4] for q in range(4)] + [jnp.zeros((4, 64), F32)], axis=1)
    out[:, :, :, 8] = jnp.broadcast_to(tile, (4, 2, 8, 4, 128))


def lines_kernel(received, out):
    low = lax.broadcasted_iota(jnp.int32, (16, 8, 128), 1) < 4

    def lines(s, b):
        pieces = [
            jnp.concatenate([received[c, b, s, 2 * j], received[c, b, s, 2 * j + 1]], axis=0)
            for c in range(4)
            for j in range(4)
        ]
        return jnp.concatenate(pieces, axis=0).T.reshape(16, 8, 128)

    for s in range(8):
        first, second = lines(s, 0), lines(s, 1)
        even = jnp.where(low, first, pltpu.roll(second, 4, 1)).reshape(8, 2, 8, 128)
        odd = jnp.where(low, pltpu.roll(first, 4, 1), second).reshape(8, 2, 8, 128)
        for q in range(2):
            out[:, q * 16 : q * 16 + 8, s * 128 : (s + 1) * 128] = even[:, q]
            out[:, q * 16 + 8 : q * 16 + 16, s * 128 : (s + 1) * 128] = odd[:, q]


def call(kernel, out, scratch=()):
    vmem = pl.BlockSpec(memory_space=pltpu.VMEM)
    smem = pl.BlockSpec(memory_space=pltpu.SMEM)
    return lambda *args: pl.pallas_call(
        kernel,
        out_shape=[jax.ShapeDtypeStruct(s, F32) for s in out],
        in_specs=[smem if a.dtype == jnp.int32 else vmem for a in args],
        out_specs=[vmem] * len(out),
        scratch_shapes=[pltpu.VMEM(s, F32) for s in scratch],
        compiler_params=pltpu.CompilerParams(vmem_limit_bytes=48 * 1024 * 1024),
    )(*args)


def four(x, one, one_bit, two, two_bit):
    def swap(axes, bits):
        sizes = [lax.axis_size(a) for a in axes]
        flat = [np.ravel_multi_index([i ^ b for i, b in zip(at, bits)], sizes) for at in np.ndindex(*sizes)]
        return lax.ppermute(x, axes, [(i, int(j)) for i, j in enumerate(flat)])

    if one == two:
        parts = [swap((one,), (bits,)) for bits in (one_bit, two_bit, one_bit ^ two_bit)]
    else:
        parts = [swap((one, two), bits) for bits in ((one_bit, 0), (0, two_bit), (one_bit, two_bit))]
    return (x + parts[0]) + (parts[1] + parts[2])


def local(orbitals, potential, coefficients):
    chunks = ("z", "x")
    dom = ("z", "x", "u", "c")
    count = lax.axis_size(chunks)

    shift = [(d, d + 4 if d % 4 >= 2 else d - 4) for d in range(4 * count)]
    beyond = lax.ppermute(potential, dom, [(i, j) for i, j in shift if 0 <= j < 4 * count])
    group = lax.axis_index(("u", "c"))
    pieces = {}
    for m in (2, 3, 1):
        if m == 3:
            orbitals, piece = lax.optimization_barrier((orbitals, piece))
            pieces[2] = lax.ppermute(piece, ("u", "c"), [(i, i ^ 2) for i in range(4)])
        piece = lax.dynamic_slice_in_dim(orbitals, OWN * (group ^ m), OWN, 0)
        if m != 2:
            pieces[m] = lax.ppermute(piece, ("u", "c"), [(i, i ^ m) for i in range(4)])
    pieces[0] = lax.dynamic_slice_in_dim(orbitals, OWN * group, OWN, 0)
    (weights,) = call(weights_kernel, [(256, 256)])(coefficients)
    pieces, beyond, potential, weights = lax.optimization_barrier(
        ([pieces[m] for m in range(4)], beyond, potential, weights)
    )
    far = 3 * WIDTH
    chunk = lax.axis_index(chunks)
    place = jnp.stack([chunk, group])
    ahead, behind = call(edges_kernel, [(OWN, far, NY, NZ)] * 2)(place, *pieces)
    ahead, behind, beyond, potential = lax.optimization_barrier((ahead, behind, beyond, potential))
    swaps = [[(i, j) for k in range(s, count - 1, 2) for i, j in ((k, k + 1), (k + 1, k))] for s in (1, 0)]
    ahead = lax.ppermute(ahead, chunks, swaps[0])
    behind = lax.ppermute(behind, chunks, swaps[1])

    def of_group(x):
        return [x] + [lax.ppermute(x, ("u", "c"), [(i, i ^ m) for i in range(4)]) for m in (1, 2, 3)]

    own, beyond = of_group(potential), of_group(beyond)
    scratch = [
        (CHUNK + 2 * far, 8 + 2 * EXT, 8, NZ),
        (CHUNK + 2 * (2 * WIDTH + 2), 8 + 2 * EXT, 8, NZ),
        (64, 8, 8, NZ),
        (8, 8, 8, 8, NZ),
        (CHUNK, 8, 8, NZ),
        (2 * 8 * NZ, NZ),
    ]
    bands = jnp.asarray(banded(1.0 / HALF))
    (message,) = call(filter_kernel, [(4, 2, 32, 8, 128)], scratch)(
        place, *pieces, ahead, behind, *own, *beyond, bands
    )
    ring = lax.all_to_all(message.reshape(8, 256, 128), ("u", "c", "b"), 0, 0, tiled=True)
    (rotated,) = call(rotate_kernel, [(4, 2, 8, 9, 4, 128)])(ring, weights)
    everyone = np.arange(256).reshape(8, 4, 4, 2)
    groups = everyone.transpose(2, 1, 3, 0).reshape(4, 64).tolist()
    received = lax.all_to_all(
        rotated.reshape(64, 9, 4, 128), ("z", "x", "u", "c", "b"), 0, 0, axis_index_groups=groups, tiled=True
    )
    gram = four(received[:, 8].sum(axis=0), "u", 1, "c", 1) / (NX * NY * NZ)
    intersection = jnp.concatenate([gram[:, q * NORB : (q + 1) * NORB] for q in range(4)], axis=0)
    (lines,) = call(lines_kernel, [(8, NY, NX)])(received.reshape(4, 2, 8, 9, 4, 128))
    return intersection, lines


def solution(mesh):
    grid = Mesh(mesh.devices.reshape(8, 4, 2, 2, 2), ("z", "x", "u", "c", "b"))
    dom = ("z", "x", "u", "c")
    return jax.shard_map(
        local,
        mesh=grid,
        in_specs=(P("b", dom, None, None), P(dom, None, None), P()),
        out_specs=(P(), P("b", dom, None)),
        check_vma=False,
    )
```

```python
import functools

import jax
import jax.numpy as jnp
import ml_dtypes
import numpy as np
from jax import lax
from jax.experimental import pallas as pl
from jax.experimental.pallas import tpu as pltpu
from jax.sharding import Mesh
from jax.sharding import PartitionSpec as P

STENCIL = (
    -5369.0 / 1800.0,
    12.0 / 7.0,
    -15.0 / 56.0,
    10.0 / 189.0,
    -1.0 / 112.0,
    2.0 / 1925.0,
    -1.0 / 16632.0,
)
CENTER = 8.5
HALF = 6.5
WIDTH = 6
EXT = 6
NORB, NX, NY, NZ = 16, 1024, 32, 128
CHUNK = 32
OWN = 2
F32 = jnp.float32
BF16 = jnp.bfloat16


def banded(scale):
    band = np.zeros((NZ, NZ), np.float64)
    for k in range(1, 7):
        band += np.eye(NZ, k=k) * STENCIL[k] + np.eye(NZ, k=-k) * STENCIL[k]
    band = (-0.5 * scale * band).astype(np.float32)
    high = band.astype(ml_dtypes.bfloat16)
    low = (band - high.astype(np.float32)).astype(ml_dtypes.bfloat16)
    zero = np.zeros_like(high)
    return np.block([[high, low], [high, zero]]).astype(ml_dtypes.bfloat16)


def split(x):
    high = x.astype(BF16)
    low = (x - high.astype(F32)).astype(BF16)
    return high, low


def edges_kernel(place, piece_0, piece_1, piece_2, piece_3, ahead, behind):
    def copy(first, last):
        for m, piece in enumerate((piece_0, piece_1, piece_2, piece_3)):
            slab = place[1] ^ m

            @pl.when(slab == 0)
            def _():
                first[:, 0:8] = piece[...]

            @pl.when(slab == 1)
            def _():
                first[:, 8:16] = piece[...]
                last[:, 0:2] = piece[:, 6:8]

            @pl.when(slab == 2)
            def _():
                first[:, 16:18] = piece[:, 0:2]
                last[:, 2:10] = piece[...]

            @pl.when(slab == 3)
            def _():
                last[:, 10:18] = piece[...]

    @pl.when(place[0] % 2 == 1)
    def _():
        copy(behind, ahead)

    @pl.when(place[0] % 2 == 0)
    def _():
        copy(ahead, behind)


def filter_kernel(
    place, piece_0, piece_1, piece_2, piece_3, ahead, behind,
    own_0, own_1, own_2, own_3, beyond_0, beyond_1, beyond_2, beyond_3, bands,
    out, field, other, local, z, result, turned,
):
    far, near = 3 * WIDTH, 2 * WIDTH + 2
    row = lax.broadcasted_iota(jnp.int32, (8, 8, NZ), 1) % 4

    def store(target, plane, r, value):
        planes = pl.ds(plane, 8)
        target[planes, EXT + r] = value
        if r >= 8 - EXT:
            target[planes, r - (8 - EXT)] = jnp.where(row == 0, 0.0, pltpu.roll(value, 1, 1))
        if r < EXT:
            target[planes, EXT + 8 + r] = jnp.where(row == 3, 0.0, pltpu.roll(value, 7, 1))

    def tiles(sources):
        rows = [jnp.concatenate([source[(*at, pl.ds(r, 4, stride=8), slice(None))] for source, at in sources], axis=0) for r in range(8)]
        return jnp.stack(rows)

    def enter(*entries):
        values = [tiles(sources) for _, sources in entries]
        for (plane, _), value in zip(entries, values):
            field[plane, EXT : EXT + 8] = value
            field[plane, 0:EXT] = jnp.where(row[:EXT] == 0, 0.0, pltpu.roll(value[8 - EXT :], 1, 1))
            field[plane, EXT + 8 :] = jnp.where(row[:EXT] == 3, 0.0, pltpu.roll(value[:EXT], 7, 1))

    odd = place[0] % 2

    def enter_ends(p, _):
        enter(
            (odd * (far + CHUNK) + p, [(ahead, (o, p)) for o in range(OWN)]),
            ((1 - odd) * (far + CHUNK) + p, [(behind, (o, p)) for o in range(OWN)]),
        )
        return 0

    lax.fori_loop(0, far, enter_ends, 0, unroll=3)

    def enter_slabs(p, _):
        for pair in (((0, piece_0), (1, piece_1)), ((2, piece_2), (3, piece_3))):
            enter(*[(far + 8 * (place[1] ^ m) + p, [(piece, (o, p)) for o in range(OWN)]) for m, piece in pair])
        return 0

    lax.fori_loop(0, 8, enter_slabs, 0, unroll=2)

    def enter_local(p, _):
        for first, sources in ((2, (own_0, own_1, own_2, own_3)), (6, (beyond_0, beyond_1, beyond_2, beyond_3))):
            values = [tiles([(source, (p,)), (source, (p,))]) for source in sources]
            for m, value in enumerate(values):
                start = 8 * ((first + (place[1] ^ m)) % 8)
                local[start + p] = (value + (-1.5 * STENCIL[0] - CENTER)) * (1.0 / HALF)
        return 0

    lax.fori_loop(0, 8, enter_local, 0, unroll=2)

    def along_z(source, index):
        high, low = split(source[pl.ds(index, 4), EXT : EXT + 8].reshape(4 * 64, NZ))
        both = jnp.dot(jnp.concatenate([high, low], axis=1), bands[...], preferred_element_type=F32)
        return (both[:, :NZ] + both[:, NZ:]).reshape(4, 8, 8, NZ)

    def step(source, shift, first, blocks, finish, put):
        def row_of(i, start, r):
            window = source[pl.ds(start + shift - WIDTH, 8 + 2 * WIDTH), EXT + r]
            total = local[pl.ds(start + 16, 8), r] * window[WIDTH : WIDTH + 8] + z[i, :, r]
            for k in range(1, 7):
                beside = window[WIDTH + k : WIDTH + 8 + k] + window[WIDTH - k : WIDTH + 8 - k]
                planes = pl.ds(start + shift, 8)
                beside = beside + (source[planes, EXT + r + k] + source[planes, EXT + r - k])
                total = total + (-0.5 / HALF * STENCIL[k]) * beside
            return finish(start, r, total)

        def body(i, _):
            start = first + 8 * i
            later = first + 8 * jnp.minimum(i + 1, blocks - 1) + shift
            last = None
            for half in range(2):
                next_z = along_z(source, later + 4 * half)
                for r in range(4 * half, 4 * half + 4):
                    value = row_of(i, start, r)
                    if last is not None:
                        put(start, r - 1, last)
                    last = value
                z[i + 1, 4 * half : 4 * half + 4] = next_z
            put(start, 7, last)
            return 0

        for half in range(2):
            z[0, 4 * half : 4 * half + 4] = along_z(source, first + shift + 4 * half)
        lax.fori_loop(0, blocks, body, 0)

    def put_first(start, r, value):
        store(other, start + near, r, value)

    def finish_second(start, r, total):
        return (total + total) - field[pl.ds(start + far, 8), EXT + r]

    def put_second(start, r, value):
        store(field, start + far, r, value)

    def finish_third(start, r, total):
        return (total + total) - other[pl.ds(start + near, 8), EXT + r]

    def put_third(start, r, value):
        result[pl.ds(start, 8), r] = value

    def outside(target, shift, count):
        blank = jnp.zeros((count, 8 + 2 * EXT, 8, NZ), F32)

        @pl.when(place[0] == 0)
        def _():
            target[shift - count : shift] = blank

        @pl.when(place[0] == NX // CHUNK - 1)
        def _():
            target[shift + CHUNK : shift + CHUNK + count] = blank

    step(field, far, -12, 7, lambda start, r, total: total, put_first)
    outside(other, near, 12)
    step(other, near, -8, 6, finish_second, put_second)
    outside(field, far, 8)
    step(field, far, 0, 4, finish_third, put_third)

    def turn(x, _):
        blocks = [
            jnp.concatenate([result[t * 8 + x, b * 4 + r] for t in range(4) for r in range(4)], axis=0) for b in range(2)
        ]
        for b in range(2):
            turned[pl.ds((b * 8 + x) * NZ, NZ), :] = blocks[b].T
        return 0

    lax.fori_loop(0, 8, turn, 0, unroll=2)

    def pick(i, _):
        places = [(c, b, 4 * i + q) for q in range(4) for c in range(4) for b in range(2)]
        values = [turned[pl.ds(b * 8 * NZ + 4 * q + c, 8, stride=NZ), :] for c, b, q in places]
        for (c, b, q), value in zip(places, values):
            out[c, b, q] = value
        return 0

    lax.fori_loop(0, NZ // 16, pick, 0, unroll=2)


exact = functools.partial(lax.dot_general, precision=lax.Precision.HIGHEST, preferred_element_type=F32)


def weights_kernel(coefficients, out):
    row = lax.broadcasted_iota(jnp.int32, (256, 256), 0)
    column = lax.broadcasted_iota(jnp.int32, (256, 256), 1)
    number = lax.broadcasted_iota(jnp.int32, (256, 16), 0)
    entry = lax.broadcasted_iota(jnp.int32, (256, 16), 1)
    before = (number // 32 * 2 + number // 4 % 2 == entry).astype(F32)
    after = (number // 16 == entry).astype(F32)
    spread = exact(before, exact(coefficients[...], after, (((1,), (1,)), ((), ()))), (((1,), (0,)), ((), ())))
    same = (row // 8 % 4 == column % 4) & (row % 4 == column // 4 % 4)
    out[...] = jnp.where(same, spread, 0.0)


def rotate_kernel(ring, weights, out):
    lane = lax.broadcasted_iota(jnp.int32, (256, 128), 1) // 32
    weights_high, weights_low = split(weights[...])
    dot = functools.partial(lax.dot_general, preferred_element_type=F32)
    right = (((1,), (0,)), ((), ()))
    rows_out = (((0,), (0,)), ((), ()))
    straight, cross = jnp.zeros((256, 256), F32), jnp.zeros((256, 256), F32)
    for t in range(4):
        halves = []
        for b in range(2):
            value = None
            for c in range(4):
                piece = ring[c * 2 + b]
                if c != t:
                    piece = pltpu.roll(piece, ((c - t) % 4) * 32, 1)
                value = piece if value is None else jnp.where(lane == c, piece, value)
            halves.append(value)
        all_orbitals = jnp.concatenate(halves, axis=1)
        high, low = split(all_orbitals)
        turned = dot(high, weights_high, right) + (dot(high, weights_low, right) + dot(low, weights_high, right))
        for b in range(2):
            rows = turned[:, b * 128 : (b + 1) * 128].reshape(8, 4, 8, 128)
            for x in range(4):
                for q in range(4):
                    out[x, b, :, 4 * t + q] = rows[:, x, 2 * q : 2 * q + 2]
        straight = straight + dot(high, high, rows_out)
        cross = cross + dot(high, low, rows_out)
    row = lax.broadcasted_iota(jnp.int32, (256, 256), 0)
    column = lax.broadcasted_iota(jnp.int32, (256, 256), 1)
    same = (row // 8 % 4 == column // 8 % 4) & (row % 4 == column % 4)
    diagonal = jnp.where(same, straight + (cross + cross.T), 0.0).reshape(8, 4, 8, 256).sum(axis=1).reshape(64, 256)
    number = lax.broadcasted_iota(jnp.int32, (256, 16), 0)
    entry = lax.broadcasted_iota(jnp.int32, (256, 16), 1)
    columns = (number // 32 * 2 + number // 4 % 2 == entry).astype(F32)
    number, entry = number[:64], entry[:64]
    rows = (number // 8 * 2 + number // 4 % 2 == entry).astype(F32)
    both = exact(rows, exact(diagonal, columns, (((1,), (0,)), ((), ()))), (((0,), (0,)), ((), ())))
    tile = jnp.concatenate([both[2 * q : 2 * q + 2] for q in range(8)], axis=1)
    out[:, :, :, 16] = jnp.broadcast_to(tile, (4, 2, 8, 2, 128))


def lines_kernel(received, out):
    low = lax.broadcasted_iota(jnp.int32, (16, 8, 128), 1) < 4

    def lines(s, b):
        pieces = [
            jnp.concatenate([received[c, b, s, 4 * j + q] for q in range(4)], axis=0)
            for c in range(4)
            for j in range(4)
        ]
        return jnp.concatenate(pieces, axis=0).T.reshape(16, 8, 128)

    for s in range(8):
        first, second = lines(s, 0), lines(s, 1)
        even = jnp.where(low, first, pltpu.roll(second, 4, 1)).reshape(8, 2, 8, 128)
        odd = jnp.where(low, pltpu.roll(first, 4, 1), second).reshape(8, 2, 8, 128)
        for q in range(2):
            out[:, q * 16 : q * 16 + 8, s * 128 : (s + 1) * 128] = even[:, q]
            out[:, q * 16 + 8 : q * 16 + 16, s * 128 : (s + 1) * 128] = odd[:, q]


def call(kernel, out, scratch=()):
    vmem = pl.BlockSpec(memory_space=pltpu.VMEM)
    smem = pl.BlockSpec(memory_space=pltpu.SMEM)
    return lambda *args: pl.pallas_call(
        kernel,
        out_shape=[jax.ShapeDtypeStruct(s, F32) for s in out],
        in_specs=[smem if a.dtype == jnp.int32 else vmem for a in args],
        out_specs=[vmem] * len(out),
        scratch_shapes=[pltpu.VMEM(s, F32) for s in scratch],
        compiler_params=pltpu.CompilerParams(vmem_limit_bytes=48 * 1024 * 1024),
    )(*args)


def four(x, one, one_bit, two, two_bit):
    def swap(axes, bits):
        sizes = [lax.axis_size(a) for a in axes]
        flat = [np.ravel_multi_index([i ^ b for i, b in zip(at, bits)], sizes) for at in np.ndindex(*sizes)]
        return lax.ppermute(x, axes, [(i, int(j)) for i, j in enumerate(flat)])

    if one == two:
        parts = [swap((one,), (bits,)) for bits in (one_bit, two_bit, one_bit ^ two_bit)]
    else:
        parts = [swap((one, two), bits) for bits in ((one_bit, 0), (0, two_bit), (one_bit, two_bit))]
    return (x + parts[0]) + (parts[1] + parts[2])


def local(orbitals, potential, coefficients):
    chunks = ("z", "x")
    dom = ("z", "x", "u", "c")
    count = lax.axis_size(chunks)

    shift = [(d, d + 4 if d % 4 >= 2 else d - 4) for d in range(4 * count)]
    beyond = lax.ppermute(potential, dom, [(i, j) for i, j in shift if 0 <= j < 4 * count])
    group = lax.axis_index(("u", "c"))
    pieces = {}
    for m in (2, 3, 1):
        if m == 3:
            orbitals, piece = lax.optimization_barrier((orbitals, piece))
            pieces[2] = lax.ppermute(piece, ("u", "c"), [(i, i ^ 2) for i in range(4)])
        piece = lax.dynamic_slice_in_dim(orbitals, OWN * (group ^ m), OWN, 0)
        if m != 2:
            pieces[m] = lax.ppermute(piece, ("u", "c"), [(i, i ^ m) for i in range(4)])
    pieces[0] = lax.dynamic_slice_in_dim(orbitals, OWN * group, OWN, 0)
    (weights,) = call(weights_kernel, [(256, 256)])(coefficients)
    pieces, beyond, potential, weights = lax.optimization_barrier(
        ([pieces[m] for m in range(4)], beyond, potential, weights)
    )
    far = 3 * WIDTH
    chunk = lax.axis_index(chunks)
    place = jnp.stack([chunk, group])
    ahead, behind = call(edges_kernel, [(OWN, far, NY, NZ)] * 2)(place, *pieces)
    ahead, behind, beyond, potential = lax.optimization_barrier((ahead, behind, beyond, potential))
    swaps = [[(i, j) for k in range(s, count - 1, 2) for i, j in ((k, k + 1), (k + 1, k))] for s in (1, 0)]
    ahead = lax.ppermute(ahead, chunks, swaps[0])
    behind = lax.ppermute(behind, chunks, swaps[1])

    def of_group(x):
        return [x] + [lax.ppermute(x, ("u", "c"), [(i, i ^ m) for i in range(4)]) for m in (1, 2, 3)]

    own, beyond = of_group(potential), of_group(beyond)
    scratch = [
        (CHUNK + 2 * far, 8 + 2 * EXT, 8, NZ),
        (CHUNK + 2 * (2 * WIDTH + 2), 8 + 2 * EXT, 8, NZ),
        (64, 8, 8, NZ),
        (8, 8, 8, 8, NZ),
        (CHUNK, 8, 8, NZ),
        (2 * 8 * NZ, NZ),
    ]
    bands = jnp.asarray(banded(1.0 / HALF))
    (message,) = call(filter_kernel, [(4, 2, 32, 8, 128)], scratch)(
        place, *pieces, ahead, behind, *own, *beyond, bands
    )
    ring = lax.all_to_all(message.reshape(8, 256, 128), ("u", "c", "b"), 0, 0, tiled=True)
    (rotated,) = call(rotate_kernel, [(4, 2, 8, 17, 2, 128)])(ring, weights)
    everyone = np.arange(256).reshape(8, 4, 4, 2)
    groups = everyone.transpose(2, 1, 3, 0).reshape(4, 64).tolist()
    received = lax.all_to_all(
        rotated.reshape(64, 17, 2, 128), ("z", "x", "u", "c", "b"), 0, 0, axis_index_groups=groups, tiled=True
    )
    gram = four(received[:, 16].sum(axis=0), "u", 1, "c", 1) / (NX * NY * NZ)
    intersection = jnp.concatenate([gram[:, q * NORB : (q + 1) * NORB] for q in range(8)], axis=0)
    (lines,) = call(lines_kernel, [(8, NY, NX)])(received.reshape(4, 2, 8, 17, 2, 128))
    return intersection, lines


def solution(mesh):
    grid = Mesh(mesh.devices.reshape(8, 4, 2, 2, 2), ("z", "x", "u", "c", "b"))
    dom = ("z", "x", "u", "c")
    return jax.shard_map(
        local,
        mesh=grid,
        in_specs=(P("b", dom, None, None), P(dom, None, None), P()),
        out_specs=(P(), P("b", dom, None)),
        check_vma=False,
    )
```
